32 devices in a mesh: row: 8 (over y, x, core), col: 4 (over z).
Axes of the slice: x: 2, y: 2, z: 4, core: 2. Of those that a mesh axis runs over, the one named last changes fastest.
Arguments:
- tokens: bfloat16 [8192, 1536], P('row', 'col'), may hold values from -6 to 6
- cotangent: bfloat16 [8192, 1536], P('row', 'col'), may hold values from -6 to 6
- adapter_ids: int32 [4], replicated, may hold values from 0 to 7
- doc_lengths: int32 [4], replicated, may hold values from 1 to 7679, as said below
- norm_gain: float32 [2, 2, 1536], P(None, None, 'col'), may hold values from 0.5 to 1.5
- inlet_weight: bfloat16 [2, 1536, 2, 2048], P(None, 'row', None, 'col'), may hold values from -0.15625 to 0.15625
- inlet_lower: bfloat16 [2, 1536, 2, 8, 16], replicated, may hold values from -0.15625 to 0.15625
- inlet_upper: bfloat16 [2, 2, 8, 16, 2048], P(None, None, None, None, 'col'), may hold values from -0.8984375 to 0.8984375
- conv_weight: float32 [2, 4, 2048], P(None, None, 'col'), may hold values from -3 to 3
- conv_bias: float32 [2, 2048], P(None, 'col'), may hold values from -1.8 to 1.8
- gate_weight: bfloat16 [2, 2, 8, 256, 256], P(None, None, 'col'), may hold values from -0.375 to 0.375
- gate_bias: float32 [2, 2, 2048], P(None, None, 'col'), may hold values from -3 to 3
- decay_param: float32 [2, 2048], P(None, 'col'), may hold values from -30 to -4
- outlet_weight: bfloat16 [2, 1536, 2048], P(None, 'row', 'col'), may hold values from -0.125 to 0.125
- outlet_lower: bfloat16 [2, 2048, 8, 16], P(None, 'col'), may hold values from -0.125 to 0.125
- outlet_upper: bfloat16 [2, 8, 16, 1536], replicated, may hold values from -0.8984375 to 0.8984375
- expand_weight: bfloat16 [2, 1536, 2, 4608], P(None, 'row', None, 'col'), may hold values from -0.15625 to 0.15625
- expand_lower: bfloat16 [2, 1536, 2, 8, 16], replicated, may hold values from -0.15625 to 0.15625
- expand_upper: bfloat16 [2, 2, 8, 16, 4608], P(None, None, None, None, 'col'), may hold values from -0.8984375 to 0.8984375
- shrink_weight: bfloat16 [2, 1536, 4608], P(None, 'row', 'col'), may hold values from -0.09375 to 0.09375
- shrink_lower: bfloat16 [2, 4608, 8, 16], P(None, 'col'), may hold values from -0.09375 to 0.09375
- shrink_upper: bfloat16 [2, 8, 16, 1536], replicated, may hold values from -0.8984375 to 0.8984375
Outputs:
- states: bfloat16 [2, 8192, 1536], P(None, 'row', 'col')
- tokens_grad: float32 [8192, 1536], P('row', 'col')
- inlet_lower_grad: float32 [2, 1536, 2, 8, 16], replicated
- inlet_upper_grad: float32 [2, 2, 8, 16, 2048], P(None, None, None, None, 'col')
- outlet_lower_grad: float32 [2, 2048, 8, 16], P(None, 'col')
- outlet_upper_grad: float32 [2, 8, 16, 1536], replicated
- expand_lower_grad: float32 [2, 1536, 2, 8, 16], replicated
- expand_upper_grad: float32 [2, 2, 8, 16, 4608], P(None, None, None, None, 'col')
- shrink_lower_grad: float32 [2, 4608, 8, 16], P(None, 'col')
- shrink_upper_grad: float32 [2, 8, 16, 1536], replicated
The draws below stay inside these ranges and needn't reach their ends.
Inputs may be any that keep to these rules, and one draw needn't show every extreme that they name: `doc_lengths`: each document has at least one token and the lengths sum to 8192; one of them, at a place drawn from the seed, is the longest, with more than 7168 tokens.
All inputs are finite; a program needn't handle non-finite values.
Results may differ from the reference program's by a relative error of at most 0.03.
Values may be sent and summed in bfloat16 or wider, within the bound.
A program may use at most 384 MiB of HBM per device.

```python
import jax
import jax.numpy as jnp
from jax import lax

D = 1536
R = 2048
FF = 4608
HS = 256
HEADS = 8
CONV = 4
ADAPTERS = 8
RANK = 16
LAYERS = 2
SEQS = 4
TOK_DEV = 1024
TOKENS = 8192


def draw_doc_lengths(key, part):
    key = jax.random.fold_in(key, 11)
    pair_key, order_key, place_key = jax.random.split(key, 3)
    most_short = (TOK_DEV - 1) // (SEQS - 1)
    pairs = (SEQS - 1) // 2
    values = jnp.zeros((0,), jnp.int32)
    if pairs > 0:
        lower = jax.random.randint(pair_key, (pairs,), 1, most_short + 1).astype(jnp.int32)
        lower = lower.at[0].set(1)
        values = jnp.concatenate([lower, (most_short + 1 - lower).astype(jnp.int32)], axis=0)
    if (SEQS - 1) % 2 == 1:
        middle = jnp.full((1,), (most_short + 1) // 2, jnp.int32)
        values = jnp.concatenate([values, middle], axis=0)
    shorter = jax.random.permutation(order_key, values).astype(jnp.int32)
    place = jax.random.randint(place_key, (), 0, SEQS)
    longest = TOKENS - jnp.sum(shorter)
    order = jnp.arange(SEQS)
    source = jnp.clip(order - (order > place).astype(jnp.int32), 0, SEQS - 2)
    return jnp.where(order == place, longest, shorter[source]).astype(jnp.int32)


def draw_decay_param(key, part):
    key = jax.random.fold_in(key, 23)
    kind_key, slow_key, fast_key = jax.random.split(key, 3)
    share = 0.5
    slower = jax.random.uniform(kind_key, (LAYERS, R)) < share
    retained = jax.random.uniform(slow_key, (LAYERS, R), minval=0.1, maxval=0.5)
    slow_rate = -jnp.log(retained) / TOKENS
    fast_rate = jax.random.uniform(fast_key, (LAYERS, R), minval=1.0 / 50.0, maxval=1.0 / 30.0)
    rate = jnp.where(slower, slow_rate, fast_rate)
    return jnp.log(jnp.expm1(rate / 4.0)).astype(jnp.float32)


def touch_ends(values, key, low, largest):
    longest = values.shape.index(max(values.shape))
    spots = []
    for shift in (0, 1):
        where = [jax.random.randint(jax.random.fold_in(key, axis), (), 0, length) for axis, length in enumerate(values.shape)]
        where[longest] = (where[longest] + shift) % values.shape[longest]
        spots.append(tuple(where))
    return values.at[spots[0]].set(low).at[spots[1]].set(largest)


def block_levels(key, shape, pieces, least, high):
    loudness, own = 1.0, jax.random.fold_in(key, 6)
    for dim, parts in pieces:
        draws = jnp.exp(jax.random.uniform(jax.random.fold_in(own, dim), (parts,), jnp.float32, least / len(pieces), high / len(pieces)))
        loudness = loudness * jnp.repeat(draws, shape[dim] // parts).reshape([-1 if axis == dim else 1 for axis in range(len(shape))])
    return loudness


def normal_values(rng, extent, width, bound, cuts=(), held_as=jnp.bfloat16):
    loudness = block_levels(rng, extent, cuts, -0.22, 0.18) if cuts else 1.0
    entries = jax.random.normal(rng, extent, jnp.float32) * width * loudness
    return jnp.minimum(jnp.maximum(entries, -bound), bound).astype(held_as)


def setup_inputs(seed: int = 0) -> dict:
    splits = jax.random.split(jax.random.key(seed), 23)
    return {
        "tokens": normal_values(splits[0], (TOKENS, D), 1.0, 6.0, ((0, 8), (1, 4))),
        "cotangent": normal_values(splits[1], (TOKENS, D), 1.0, 6.0, ((0, 8), (1, 4))),
        "adapter_ids": touch_ends(jax.random.randint(splits[2], (SEQS,), 0, ADAPTERS), jax.random.fold_in(splits[2], 1), 0, ADAPTERS - 1).astype(jnp.int32),
        "doc_lengths": draw_doc_lengths(jax.random.fold_in(splits[22], 71), 0),
        "norm_gain": jnp.clip(1.0 + 0.1 * jax.random.normal(splits[4], (LAYERS, 2, D), jnp.float32), 0.5, 1.5),
        "inlet_weight": normal_values(splits[5], (LAYERS, D, 2, R), D ** -0.5, 0.15625, ((1, 8), (3, 4))),
        "inlet_lower": normal_values(splits[6], (LAYERS, D, 2, ADAPTERS, RANK), D ** -0.5, 0.15625),
        "inlet_upper": normal_values(splits[7], (LAYERS, 2, ADAPTERS, RANK, R), 0.15, 0.8984375, ((4, 4),)),
        "conv_weight": normal_values(splits[8], (LAYERS, CONV, R), 0.5, 3.0, ((2, 4),), jnp.float32),
        "conv_bias": normal_values(splits[9], (LAYERS, R), 0.3, 1.8, ((1, 4),), jnp.float32),
        "gate_weight": normal_values(splits[10], (LAYERS, 2, HEADS, HS, HS), HS ** -0.5, 0.375, ((2, 4),)),
        "gate_bias": normal_values(splits[11], (LAYERS, 2, R), 0.5, 3.0, ((2, 4),), jnp.float32),
        "decay_param": draw_decay_param(jax.random.fold_in(splits[22], 71), 0),
        "outlet_weight": normal_values(splits[13], (LAYERS, D, R), R ** -0.5, 0.125, ((1, 8), (2, 4))),
        "outlet_lower": normal_values(splits[14], (LAYERS, R, ADAPTERS, RANK), R ** -0.5, 0.125, ((1, 4),)),
        "outlet_upper": normal_values(splits[15], (LAYERS, ADAPTERS, RANK, D), 0.15, 0.8984375),
        "expand_weight": normal_values(splits[16], (LAYERS, D, 2, FF), D ** -0.5, 0.15625, ((1, 8), (3, 4))),
        "expand_lower": normal_values(splits[17], (LAYERS, D, 2, ADAPTERS, RANK), D ** -0.5, 0.15625),
        "expand_upper": normal_values(splits[18], (LAYERS, 2, ADAPTERS, RANK, FF), 0.15, 0.8984375, ((4, 4),)),
        "shrink_weight": normal_values(splits[19], (LAYERS, D, FF), FF ** -0.5, 0.09375, ((1, 8), (2, 4))),
        "shrink_lower": normal_values(splits[20], (LAYERS, FF, ADAPTERS, RANK), FF ** -0.5, 0.09375, ((1, 4),)),
        "shrink_upper": normal_values(splits[21], (LAYERS, ADAPTERS, RANK, D), 0.15, 0.8984375),
    }


HIGH = lax.Precision.HIGHEST
EPSILON = 1e-06

@jax.custom_vjp
def low(v):
    return lax.optimization_barrier(v.astype(jnp.bfloat16)).astype(jnp.float32)

@jax.custom_vjp
def low_back(v):
    return v

def low_keep(v):
    return (low(v), None)

def low_pass(kept, grad):
    return (grad,)

def back_keep(v):
    return (v, None)

def back_low(kept, grad):
    return (low(grad),)
low.defvjp(low_keep, low_pass)
low_back.defvjp(back_keep, back_low)

def widen(value):
    return value.astype(jnp.float32)

def gelu_tanh(value):
    return jax.nn.gelu(value, approximate=True)

def gated_mix(hidden, gate):
    return hidden * gelu_tanh(gate)

def geglu(gate, upper):
    return gelu_tanh(gate) * upper

def recurrence_terms(conv_value, logit_rate, logit_input, softness, first):
    rate = jax.nn.sigmoid(logit_rate)
    inward = jax.nn.sigmoid(logit_input)
    log_decay = -8.0 * softness * rate
    keep = 1.0 - first
    decay = jnp.exp(log_decay) * keep
    scale = keep * jnp.sqrt(-jnp.expm1(2.0 * log_decay)) + first
    return (decay, scale * inward * conv_value)

def locate(places, doc_lengths, adapter_ids):
    ends = jnp.cumsum(doc_lengths).astype(jnp.int32)
    starts = (ends - doc_lengths).astype(jnp.int32)
    inside = (places[:, None] >= starts[None, :]) & (places[:, None] < ends[None, :])
    begin = lax.optimization_barrier(jnp.sum(jnp.where(inside, starts[None, :], 0), axis=1)).astype(jnp.int32)
    chosen = lax.optimization_barrier(jnp.sum(jnp.where(inside, adapter_ids[None, :], 0), axis=1)).astype(jnp.int32)
    pick = (chosen[:, None] == jnp.arange(ADAPTERS, dtype=jnp.int32)[None, :]).astype(jnp.float32)
    offset = (places - begin).astype(jnp.int32)
    first = (offset == 0).astype(jnp.float32)[:, None]
    return (offset, pick, first)

def mask_rows(inner, pick):
    shaped = inner.reshape(inner.shape[:-1] + (ADAPTERS, RANK))
    spread = pick.reshape((pick.shape[0],) + (1,) * (inner.ndim - 2) + (ADAPTERS, 1))
    return (shaped * spread).reshape(inner.shape)

def both_low(value):
    return low(low_back(value))

def rms_norm(stream, gain):
    return stream * lax.rsqrt(lax.optimization_barrier(jnp.mean(stream * stream, axis=-1, keepdims=True)) + EPSILON) * gain

def advance(state, pair):
    state = pair[0] * state + pair[1]
    return (state, state)

def block(stream, frozen, adapters, pick, offset, first):
    gains, inlet, conv_weight, conv_bias, gate_weight, gate_bias, decay_param, outlet, expand, shrink = frozen
    inlet_lower, inlet_upper, outlet_lower, outlet_upper, expand_lower, expand_upper, shrink_lower, shrink_upper = adapters
    rows = stream.shape[0]
    ranks = ADAPTERS * RANK
    normed = low(rms_norm(stream, gains[0]))
    inner = both_low(mask_rows(jnp.dot(normed, inlet_lower.reshape(D, 2 * ranks), precision=HIGH).reshape(rows, 2, ranks), pick))
    branch = jnp.einsum('td,dbc->tbc', normed, inlet, precision=HIGH)
    branch = low_back(branch + jnp.einsum('tbk,bkc->tbc', inner, inlet_upper.reshape(2, ranks, R), precision=HIGH))
    lead = branch[:, 0]
    gate = branch[:, 1]
    conv = conv_bias[None, :] + conv_weight[0][None, :] * lead
    for shift_by in range(1, CONV):
        moved = jnp.concatenate([jnp.zeros((shift_by, R), jnp.float32), lead[:rows - shift_by]], axis=0)
        valid = (offset >= shift_by).astype(jnp.float32)[:, None]
        conv = conv + conv_weight[shift_by][None, :] * moved * valid
    conv = low(conv)
    logits = jnp.einsum('thi,jhio->jtho', conv.reshape(rows, HEADS, HS), gate_weight, precision=HIGH)
    logits = low_back(logits.reshape(2, rows, R) + gate_bias[:, None, :])
    decay, drive = recurrence_terms(conv, logits[0], logits[1], jax.nn.softplus(decay_param), first)
    _, hidden = lax.scan(advance, jnp.zeros((R,), jnp.float32), (decay, drive))
    mixed = low(gated_mix(hidden, gate))
    lowrank = both_low(mask_rows(jnp.dot(mixed, outlet_lower.reshape(R, ranks), precision=HIGH), pick))
    out = jnp.einsum('tc,dc->td', mixed, outlet, precision=HIGH)
    out = low_back(out + jnp.dot(lowrank, outlet_upper.reshape(ranks, D), precision=HIGH))
    middle = stream + out
    normed_two = low(rms_norm(middle, gains[1]))
    inner_two = both_low(mask_rows(jnp.dot(normed_two, expand_lower.reshape(D, 2 * ranks), precision=HIGH).reshape(rows, 2, ranks), pick))
    branch_two = jnp.einsum('td,dbf->tbf', normed_two, expand, precision=HIGH)
    branch_two = low_back(branch_two + jnp.einsum('tbk,bkf->tbf', inner_two, expand_upper.reshape(2, ranks, FF), precision=HIGH))
    product = low(geglu(branch_two[:, 0], branch_two[:, 1]))
    lowrank_two = both_low(mask_rows(jnp.dot(product, shrink_lower.reshape(FF, ranks), precision=HIGH), pick))
    out_two = jnp.einsum('tf,df->td', product, shrink, precision=HIGH)
    out_two = low_back(out_two + jnp.dot(lowrank_two, shrink_upper.reshape(ranks, D), precision=HIGH))
    return middle + out_two

def reference(tokens, cotangent, adapter_ids, doc_lengths, norm_gain, inlet_weight, inlet_lower, inlet_upper, conv_weight, conv_bias, gate_weight, gate_bias, decay_param, outlet_weight, outlet_lower, outlet_upper, expand_weight, expand_lower, expand_upper, shrink_weight, shrink_lower, shrink_upper):
    places = jnp.arange(TOKENS, dtype=jnp.int32)
    offset, pick, first = locate(places, doc_lengths, adapter_ids)
    frozen_all = (widen(norm_gain), widen(inlet_weight), widen(conv_weight), widen(conv_bias), widen(gate_weight), widen(gate_bias), widen(decay_param), widen(outlet_weight), widen(expand_weight), widen(shrink_weight))
    checked = jax.checkpoint(block)

    def forward(stream, in_lower, in_upper, out_lower, out_upper, ex_lower, ex_upper, sh_lower, sh_upper):
        outputs = []
        for layer in range(LAYERS):
            frozen = tuple((array[layer] for array in frozen_all))
            adapters = (in_lower[layer], in_upper[layer], out_lower[layer], out_upper[layer], ex_lower[layer], ex_upper[layer], sh_lower[layer], sh_upper[layer])
            stream = checked(stream, frozen, adapters, pick, offset, first)
            outputs.append(stream)
        return jnp.stack(outputs)
    outputs, pull = jax.vjp(forward, widen(tokens), widen(inlet_lower), widen(inlet_upper), widen(outlet_lower), widen(outlet_upper), widen(expand_lower), widen(expand_upper), widen(shrink_lower), widen(shrink_upper))
    seeded = jnp.zeros_like(outputs).at[LAYERS - 1].set(widen(cotangent))
    grads = pull(seeded)
    return (outputs.astype(jnp.bfloat16), grads[0], grads[1], grads[2], grads[3], grads[4], grads[5], grads[6], grads[7], grads[8])
```

```python
from functools import partial

import jax
import jax.numpy as jnp
from jax import lax
from jax.experimental import pallas as pl
from jax.experimental.pallas import tpu as pltpu
from jax.sharding import PartitionSpec as P

HS = 256
CONV = 4
LAYERS = 2
SEGS = 8

EPSILON = 1e-06
FLOAT = jnp.float32
BRAIN = jnp.bfloat16
VMEM_BYTES = 48 * 1024 * 1024
CURVE = 0.7978845608028654
CUBIC = 0.044715
LANES = 128
SLABS = HS // LANES


def nn(left, right):
    return lax.dot_general(left, right, (((1,), (0,)), ((), ())), preferred_element_type=FLOAT)


def nt(left, right):
    return lax.dot_general(left, right, (((1,), (1,)), ((), ())), preferred_element_type=FLOAT)


def tn(left, right):
    return lax.dot_general(left, right, (((0,), (0,)), ((), ())), preferred_element_type=FLOAT)


def gelu_tanh(value):
    return 0.5 * value * (1.0 + jnp.tanh(CURVE * (value + CUBIC * value * value * value)))


def gelu_pair(value):
    square = value * value
    bend = jnp.tanh(CURVE * value * (1.0 + CUBIC * square))
    half = 0.5 * (1.0 + bend)
    slope = half + 0.5 * value * (1.0 - bend * bend) * CURVE * (1.0 + 3.0 * CUBIC * square)
    return value * half, slope


def put(slabs, value, rows=slice(None)):
    for slab in range(SLABS):
        slabs[slab, rows] = value[:, slab * LANES : (slab + 1) * LANES]


def take(slabs, rows=slice(None)):
    return jnp.concatenate([slabs[slab, rows] for slab in range(SLABS)], axis=1)


def flat(parts):
    return jnp.concatenate(parts, axis=1)


def one_less_square(twice, square):
    series = -twice * (
        1.0 + twice * (0.5 + twice * (1.0 / 6.0 + twice * (1.0 / 24.0 + twice * (1.0 / 120.0))))
    )
    return jnp.where(twice > -0.1, series, 1.0 - square)


def gate_values(conv, gate_w, gate_b, soft):
    rate = jax.nn.sigmoid(nn(conv, gate_w[0]) + gate_b[0:1])
    inward = jax.nn.sigmoid(nn(conv, gate_w[1]) + gate_b[1:2])
    log_decay = (-8.0 * soft) * rate
    raw = jnp.exp(log_decay)
    gap = one_less_square(2.0 * log_decay, raw * raw)
    return rate, inward, raw, gap


def forward_kernel(
    par, lead, halo, offset, conv_w, conv_b, gate_w, gate_b, soft,
    conv_out, decay_out, state_out, cum_out, seg_out, ext, drive,
):
    rows = lead.shape[0]
    half = rows // 2
    span = rows // SEGS
    start = pl.multiple_of(par[0] * half, half)
    other = pl.multiple_of(half - par[0] * half, half)
    ext[0:8] = halo[...]
    ext[8 : 8 + half] = lead[pl.ds(start, half), :]
    ext[8 + half : 8 + rows] = lead[pl.ds(other, half), :]
    place = offset[...]
    total = conv_b[...] + conv_w[0:1] * ext[8 : 8 + rows]
    for step in range(1, CONV):
        valid = (place >= step).astype(FLOAT)
        total = total + conv_w[step : step + 1] * ext[8 - step : 8 - step + rows] * valid
    conv = total.astype(BRAIN)
    conv_out[...] = conv
    rate, inward, raw, gap = gate_values(conv, gate_w, gate_b, soft[...])
    first = (place == 0).astype(FLOAT)
    keep = 1.0 - first
    put(decay_out, raw * keep)
    put(drive, (keep * jnp.sqrt(gap) + first) * inward * conv.astype(FLOAT))

    def advance(step, carried):
        where = pl.ds(step, SEGS, stride=span)
        after = []
        for slab, (state, cum) in enumerate(carried):
            rates = decay_out[slab, where, :]
            state = rates * state + drive[slab, where, :]
            cum = rates * cum
            state_out[slab, where, :] = state
            cum_out[slab, where, :] = cum
            after.append((state, cum))
        return tuple(after)

    shape = (SEGS, lead.shape[1])
    fresh = (jnp.zeros((SEGS, LANES), FLOAT), jnp.ones((SEGS, LANES), FLOAT))
    ends = lax.fori_loop(0, span, advance, (fresh,) * SLABS, unroll=8)
    state, cum = (flat(parts) for parts in zip(*ends))
    run_state = jnp.zeros((1, shape[1]), FLOAT)
    run_cum = jnp.ones((1, shape[1]), FLOAT)
    for seg in range(SEGS):
        seg_out[seg : seg + 1] = run_state
        seg_out[SEGS + seg : SEGS + seg + 1] = run_cum
        run_state = cum[seg : seg + 1] * run_state + state[seg : seg + 1]
        run_cum = cum[seg : seg + 1] * run_cum
    seg_out[2 * SEGS : 2 * SEGS + 1] = run_cum
    seg_out[2 * SEGS + 1 : 2 * SEGS + 2] = run_state
    seg_out[2 * SEGS + 2 : 3 * SEGS] = jnp.zeros((SEGS - 2, shape[1]), FLOAT)


def mix_kernel(par, state, cum, seg, carry, gate, hidden_out, mixed_out, hidden):
    rows = gate.shape[0]
    half = rows // 2
    span = rows // SEGS
    start = pl.multiple_of(par[0] * half, half)
    other = pl.multiple_of(half - par[0] * half, half)
    entering = seg[0:SEGS] + seg[SEGS : 2 * SEGS] * carry[0:1]
    for at in range(SEGS):
        part = slice(at * span, (at + 1) * span)
        hidden[part] = take(state, part) + take(cum, part) * entering[at : at + 1]
    put(hidden_out, hidden[...])
    for place, part in ((start, slice(0, half)), (other, slice(half, rows))):
        mixed_out[pl.ds(place, half), :] = (
            hidden[part] * gelu_tanh(gate[pl.ds(place, half), :])
        ).astype(BRAIN)


def backward_kernel(
    par, grad, gate, hidden, decay, gate_grad, local_out, reach_out, seg_out, ext, grads
):
    rows = grad.shape[0]
    half = rows // 2
    span = rows // SEGS
    start = pl.multiple_of(par[0] * half, half)
    other = pl.multiple_of(half - par[0] * half, half)
    for place, part in ((start, slice(0, half)), (other, slice(half, rows))):
        value, slope = gelu_pair(gate[pl.ds(place, half), :])
        coming = grad[pl.ds(place, half), :]
        put(grads, coming * value, part)
        gate_grad[pl.ds(place, half), :] = (coming * take(hidden, part) * slope).astype(BRAIN)
    ext[:, 0:rows] = decay[...]
    ext[:, rows : rows + 8] = jnp.ones((SLABS, 8, LANES), FLOAT)

    def retreat(turn, carried):
        step = span - 1 - turn
        follows = pl.ds(step + 1, SEGS, stride=span)
        where = pl.ds(step, SEGS, stride=span)
        after = []
        for slab, (state, cum) in enumerate(carried):
            rates = ext[slab, follows, :]
            state = rates * state + grads[slab, where, :]
            cum = rates * cum
            local_out[slab, where, :] = state
            reach_out[slab, where, :] = cum
            after.append((state, cum))
        return tuple(after)

    shape = (SEGS, grad.shape[1])
    fresh = (jnp.zeros((SEGS, LANES), FLOAT), jnp.ones((SEGS, LANES), FLOAT))
    ends = lax.fori_loop(0, span, retreat, (fresh,) * SLABS, unroll=8)
    state, cum = (flat(parts) for parts in zip(*ends))
    run_state = jnp.zeros((1, shape[1]), FLOAT)
    run_cum = jnp.ones((1, shape[1]), FLOAT)
    for seg in reversed(range(SEGS)):
        seg_out[seg : seg + 1] = run_state
        seg_out[SEGS + seg : SEGS + seg + 1] = run_cum
        run_state = cum[seg : seg + 1] * run_state + state[seg : seg + 1]
        run_cum = cum[seg : seg + 1] * run_cum
    opening = take(decay, slice(0, 1))
    seg_out[2 * SEGS : 2 * SEGS + 1] = run_cum * opening
    seg_out[2 * SEGS + 1 : 2 * SEGS + 2] = run_state * opening
    seg_out[2 * SEGS + 2 : 3 * SEGS] = jnp.zeros((SEGS - 2, shape[1]), FLOAT)


def terms_kernel(
    par, local, reach, seg, carry, hidden, state_in, conv, offset,
    conv_w, gate_w, gate_b, soft,
    lead_grad, tail_out, head_out, ext, prior,
):
    rows = conv.shape[0]
    half = rows // 2
    span = rows // SEGS
    start = pl.multiple_of(par[0] * half, half)
    other = pl.multiple_of(half - par[0] * half, half)
    entering = seg[0:SEGS] + seg[SEGS : 2 * SEGS] * carry[0:1]
    for at in range(SEGS):
        part = slice(at * span, (at + 1) * span)
        ext[part] = take(local, part) + take(reach, part) * entering[at : at + 1]
    carried = ext[0:rows]
    prior[7:8] = state_in[0:1]
    prior[8 : 8 + rows] = take(hidden)
    before = prior[7 : 7 + rows]
    low = conv[...]
    value = low.astype(FLOAT)
    place = offset[...]
    first = (place == 0).astype(FLOAT)
    keep = 1.0 - first
    rate, inward, raw, gap = gate_values(low, gate_w, gate_b, soft[...])
    root = jnp.sqrt(gap)
    scale = keep * root + first
    pushed = carried * inward
    log_grad = keep * raw * (carried * before - pushed * value * (raw / root))
    rate_grad = ((-8.0 * soft[...]) * log_grad * rate * (1.0 - rate)).astype(BRAIN)
    scaled = carried * scale
    input_grad = (scaled * value * inward * (1.0 - inward)).astype(BRAIN)
    conv_grad = scaled * inward + nt(rate_grad, gate_w[0]) + nt(input_grad, gate_w[1])
    ext[0:rows] = conv_grad
    ext[rows : rows + 8] = jnp.zeros((8, conv.shape[1]), FLOAT)
    prior[0:rows] = conv_w[0:1] * conv_grad
    head = jnp.zeros((8, conv.shape[1]), FLOAT)
    for step in range(1, CONV):
        valid = (place >= step).astype(FLOAT)
        prior_term = conv_w[step : step + 1] * conv_grad * valid
        ext[0:rows] = prior_term
        prior[0:rows] = prior[0:rows] + ext[step : step + rows]
        lines = lax.broadcasted_iota(jnp.int32, (8, 1), 0)
        moved = pltpu.roll(prior_term[0:8], 8 - step, 0)
        head = head + jnp.where(lines >= 8 - step, moved, 0.0)
    head_out[...] = head
    tail_out[...] = prior[rows - 8 : rows]
    lead_grad[pl.ds(start, half), :] = prior[0:half].astype(BRAIN)
    lead_grad[pl.ds(other, half), :] = prior[half:rows].astype(BRAIN)


def column_call(kernel, parity, operands, kinds, outs, out_kinds, scratch, width):
    def spec(kind, shape):
        if kind == "all":
            return pl.BlockSpec(shape, lambda at, par: (0,) * len(shape))
        if kind == "heads":
            return pl.BlockSpec((shape[0], None) + shape[2:], lambda at, par: (0, at, 0, 0))
        if kind == "slabs":
            return pl.BlockSpec((SLABS,) + shape[1:], lambda at, par: (at, 0, 0))
        return pl.BlockSpec((shape[0], HS), lambda at, par: (0, at))

    return pl.pallas_call(
        kernel,
        out_shape=[jax.ShapeDtypeStruct(*out) for out in outs],
        grid_spec=pltpu.PrefetchScalarGridSpec(
            num_scalar_prefetch=1,
            grid=(width // HS,),
            in_specs=[spec(kind, value.shape) for kind, value in zip(kinds, operands)],
            out_specs=[spec(kind, out[0]) for kind, out in zip(out_kinds, outs)],
            scratch_shapes=scratch,
        ),
        compiler_params=pltpu.CompilerParams(vmem_limit_bytes=VMEM_BYTES),
    )(parity, *operands)


def partner(value):
    peers = lax.axis_size("col")
    return lax.ppermute(value, "col", [(at, at ^ 1) for at in range(peers)])


def from_shard(value, turn):
    peers = lax.axis_size("col")
    return lax.ppermute(value, "col", [((at + 2 * turn) % peers, at) for at in range(peers)])


def to_shard(value, turn):
    peers = lax.axis_size("col")
    return lax.ppermute(value, "col", [(at, (at + 2 * turn) % peers) for at in range(peers)])


def all_shards(value):
    return [value] + [from_shard(value, turn) for turn in range(1, lax.axis_size("col") // 2)]


def along_tokens(value, by):
    shards = lax.axis_size("col") // 2
    size = lax.axis_size("row") * lax.axis_size("col")
    pairs = [(at, at + 2 * by) for at in range(size) if 0 <= at + 2 * by < size]
    moved = lax.ppermute(value, ("row", "col"), pairs)
    return jnp.roll(moved, -by * (value.shape[-1] // shards), axis=-1)


def carry_in(total, direction):
    blocks = lax.axis_size("row") * lax.axis_size("col") // 2
    reach = 1
    while reach < blocks:
        earlier = along_tokens(total, direction * reach)
        total = jnp.stack([total[0] * earlier[0], total[0] * earlier[1] + total[1]])
        reach *= 2
    return along_tokens(total[1:2], direction)


def to_sequence(value):
    return lax.all_to_all(value, "col", split_axis=0, concat_axis=1, tiled=True)


def from_sequence(value):
    return lax.all_to_all(value, "col", split_axis=1, concat_axis=0, tiled=True)


def both_halves(value):
    return jnp.concatenate([value, partner(value)], axis=0)


def half_share(own, other):
    return own + partner(other.astype(BRAIN)).astype(FLOAT)


def norm_forward(stream, gain):
    scale = lax.rsqrt(jnp.mean(stream * stream, axis=1, keepdims=True) + EPSILON)
    return scale, (stream * scale * gain[None, :]).astype(BRAIN)


def norm_backward(stream, scale, gain, d_normed):
    gained = d_normed * gain[None, :]
    total = jnp.mean(gained * stream, axis=1, keepdims=True)
    return scale * gained - stream * (scale * scale * scale * total)


def masked(value, pick):
    return (value * pick).astype(BRAIN)


def layer_forward(stream, wide, small, gains, ctx):
    inlet, outlet, expand, shrink = wide
    pick, offset, parity = ctx["pick"], ctx["offset"], ctx["parity"]
    ranks = pick.shape[1]
    own = stream.shape[0]
    rows = 2 * own
    width = outlet.shape[1]
    spread = shrink.shape[1]

    scale_one, normed = norm_forward(stream, gains[0])
    normed_full = both_halves(normed)
    low = nt(normed_full, small["inlet_lower"])
    inner = [masked(low[:, b * ranks : (b + 1) * ranks], pick) for b in range(2)]
    branch = nn(normed_full, inlet)
    lead = branch[:, :width] + nn(inner[0], small["inlet_upper"][0])
    gate = branch[:, width:] + nn(inner[1], small["inlet_upper"][1])
    last = lax.dynamic_slice_in_dim(lead, (1 - parity[0]) * own + own - 8, 8, axis=0)
    halo = along_tokens(last, 1)
    full, slabs = (rows, width), (width // LANES, rows, LANES)
    conv, decay, state, cum, seg = column_call(
        forward_kernel,
        parity,
        [lead, halo, offset, small["conv_weight"], small["conv_bias"], small["gate_weight"],
         small["gate_bias"], small["soft"]],
        ["cols", "cols", "all", "cols", "cols", "heads", "cols", "cols"],
        [(full, BRAIN), (slabs, FLOAT), (slabs, FLOAT), (slabs, FLOAT), ((3 * SEGS, width), FLOAT)],
        ["cols", "slabs", "slabs", "slabs", "cols"],
        [pltpu.VMEM((rows + 8, HS), FLOAT), pltpu.VMEM((SLABS, rows, LANES), FLOAT)],
        width,
    )
    state_in = carry_in(seg[2 * SEGS : 2 * SEGS + 2], 1)
    hidden, mixed = column_call(
        mix_kernel,
        parity,
        [state, cum, seg, state_in, gate],
        ["slabs", "slabs", "cols", "cols", "cols"],
        [(slabs, FLOAT), (full, BRAIN)],
        ["slabs", "cols"],
        [pltpu.VMEM((rows, HS), FLOAT)],
        width,
    )
    lowrank = masked(nt(mixed, small["outlet_lower"]), pick)

    def outward(part):
        return nt(mixed[part], outlet) + nn(lowrank[part], small["outlet_upper"])

    middle = stream + half_share(outward(slice(0, own)), outward(slice(own, rows)))
    scale_two, normed_two = norm_forward(middle, gains[1])
    normed_two_full = both_halves(normed_two)
    low_two = nt(normed_two_full, small["expand_lower"])
    inner_two = [masked(low_two[:, b * ranks : (b + 1) * ranks], pick) for b in range(2)]
    branch_two = nn(normed_two_full, expand)
    up_gate = branch_two[:, :spread] + nn(inner_two[0], small["expand_upper"][0])
    up_value = branch_two[:, spread:] + nn(inner_two[1], small["expand_upper"][1])
    product = (gelu_tanh(up_gate) * up_value).astype(BRAIN)
    lowrank_two = masked(nt(product, small["shrink_lower"]), pick)

    def downward(part):
        return nt(product[part], shrink) + nn(lowrank_two[part], small["shrink_upper"])

    result = middle + half_share(downward(slice(0, own)), downward(slice(own, rows)))
    kept = dict(
        stream=stream, scale_one=scale_one, normed_full=normed_full, inner=inner, gate=gate,
        conv=conv, decay=decay, hidden=hidden, state_in=state_in, mixed=mixed, lowrank=lowrank,
        middle=middle, scale_two=scale_two, normed_two_full=normed_two_full, inner_two=inner_two,
        up_gate=up_gate, up_value=up_value, product=product, lowrank_two=lowrank_two,
    )
    return result, kept


def layer_backward(d_stream, wide, small, gains, kept, ctx):
    inlet, outlet, expand, shrink = wide
    pick, offset, parity = ctx["pick"], ctx["offset"], ctx["parity"]
    own = d_stream.shape[0]
    rows = 2 * own
    width = outlet.shape[1]
    spread = shrink.shape[1]

    d_out = both_halves(d_stream.astype(BRAIN))
    d_low_two = masked(nt(d_out, small["shrink_upper"]), pick)
    d_product = nn(d_out, shrink) + nn(d_low_two, small["shrink_lower"])
    shrink_upper_grad = tn(kept["lowrank_two"], d_out)
    shrink_lower_grad = tn(d_low_two, kept["product"])
    value, slope = gelu_pair(kept["up_gate"])
    d_branch_two = jnp.concatenate(
        [(slope * kept["up_value"] * d_product).astype(BRAIN), (value * d_product).astype(BRAIN)],
        axis=1,
    )
    d_inner_two = jnp.concatenate(
        [
            masked(nt(d_branch_two[:, b * spread : (b + 1) * spread], small["expand_upper"][b]), pick)
            for b in range(2)
        ],
        axis=1,
    )

    def inward_two(part):
        return nt(d_branch_two[part], expand) + nn(d_inner_two[part], small["expand_lower"])

    d_normed_two = half_share(inward_two(slice(0, own)), inward_two(slice(own, rows)))
    expand_lower_grad = tn(d_inner_two, kept["normed_two_full"])
    expand_upper_grad = jnp.concatenate(
        [
            tn(kept["inner_two"][b], d_branch_two[:, b * spread : (b + 1) * spread])
            for b in range(2)
        ],
        axis=0,
    )
    d_middle = d_stream + norm_backward(kept["middle"], kept["scale_two"], gains[1], d_normed_two)

    d_mid = both_halves(d_middle.astype(BRAIN))
    d_low = masked(nt(d_mid, small["outlet_upper"]), pick)
    d_mixed = nn(d_mid, outlet) + nn(d_low, small["outlet_lower"])
    outlet_upper_grad = tn(kept["lowrank"], d_mid)
    outlet_lower_grad = tn(d_low, kept["mixed"])
    full, slabs = (rows, width), (width // LANES, rows, LANES)
    d_gate, local_grad, reach, seg = column_call(
        backward_kernel,
        parity,
        [d_mixed, kept["gate"], kept["hidden"], kept["decay"]],
        ["cols", "cols", "slabs", "slabs"],
        [(full, BRAIN), (slabs, FLOAT), (slabs, FLOAT), ((3 * SEGS, width), FLOAT)],
        ["cols", "slabs", "slabs", "cols"],
        [
            pltpu.VMEM((SLABS, rows + 8, LANES), FLOAT),
            pltpu.VMEM((SLABS, rows, LANES), FLOAT),
        ],
        width,
    )
    arriving = carry_in(seg[2 * SEGS : 2 * SEGS + 2], -1)
    d_lead, tail, head = column_call(
        terms_kernel,
        parity,
        [local_grad, reach, seg, arriving, kept["hidden"], kept["state_in"], kept["conv"], offset,
         small["conv_weight"], small["gate_weight"], small["gate_bias"], small["soft"]],
        ["slabs", "slabs", "cols", "cols", "slabs", "cols", "cols", "all", "cols", "heads", "cols",
         "cols"],
        [(full, BRAIN), ((8, width), FLOAT), ((8, width), FLOAT)],
        ["cols"] * 3,
        [pltpu.VMEM((rows + 8, HS), FLOAT), pltpu.VMEM((rows + 8, HS), FLOAT)],
        width,
    )
    tail = (tail + along_tokens(head, -1)).astype(BRAIN)
    d_lead = lax.dynamic_update_slice_in_dim(
        d_lead, tail, (1 - parity[0]) * own + own - 8, axis=0
    )
    d_branch = jnp.concatenate([d_lead, d_gate], axis=1)
    d_inner = jnp.concatenate(
        [
            masked(nt(d_branch[:, b * width : (b + 1) * width], small["inlet_upper"][b]), pick)
            for b in range(2)
        ],
        axis=1,
    )

    def inward(part):
        return nt(d_branch[part], inlet) + nn(d_inner[part], small["inlet_lower"])

    d_normed = half_share(inward(slice(0, own)), inward(slice(own, rows)))
    inlet_lower_grad = tn(d_inner, kept["normed_full"])
    inlet_upper_grad = jnp.concatenate(
        [tn(kept["inner"][b], d_branch[:, b * width : (b + 1) * width]) for b in range(2)], axis=0
    )
    d_input = d_middle + norm_backward(kept["stream"], kept["scale_one"], gains[0], d_normed)
    shared = jnp.concatenate(
        [inlet_lower_grad, outlet_upper_grad, expand_lower_grad, shrink_upper_grad], axis=0
    )
    split = (
        jnp.concatenate([inlet_upper_grad, outlet_lower_grad], axis=0),
        jnp.concatenate([expand_upper_grad, shrink_lower_grad], axis=0),
    )
    return d_input, shared, split


def owned(grad, shards):
    piece = grad.shape[1] // shards
    parts = [grad[:, turn * piece : (turn + 1) * piece].astype(BRAIN) for turn in range(shards)]
    total = parts[0].astype(FLOAT)
    for turn in range(1, shards):
        total = total + to_shard(parts[turn], turn).astype(FLOAT)
    return total.astype(BRAIN)


def local(
    tokens, cotangent, adapter_ids, doc_lengths, norm_gain, inlet_weight, inlet_lower, inlet_upper,
    conv_weight, conv_bias, gate_weight, gate_bias, decay_param, outlet_weight, outlet_lower,
    outlet_upper, expand_weight, expand_lower, expand_upper, shrink_weight, shrink_lower,
    shrink_upper,
):
    row_at, col_at = lax.axis_index("row"), lax.axis_index("col")
    cols = lax.axis_size("col")
    shards = cols // 2
    rows = tokens.shape[0]
    own = rows // cols
    block = 2 * own
    docs = adapter_ids.shape[0]
    adapters, rank = inlet_lower.shape[3:]
    depth, part_width = inlet_weight.shape[1], inlet_weight.shape[3]
    part_spread = expand_weight.shape[3]
    d_model = inlet_lower.shape[1]

    parity = (col_at % 2).astype(jnp.int32)
    ends = jnp.cumsum(doc_lengths)
    starts = ends - doc_lengths
    ordered = row_at * rows + (col_at // 2) * block + jnp.arange(block, dtype=jnp.int32)
    inside = (ordered[:, None] >= starts[None, :]) & (ordered[:, None] < ends[None, :])
    offset = (ordered - jnp.sum(jnp.where(inside, starts[None, :], 0), axis=1))[:, None]
    halves = (parity * own, own - parity * own)
    at_home = jnp.concatenate(
        [ordered[0] + begin + jnp.arange(own, dtype=jnp.int32) for begin in halves]
    )
    within = (at_home[:, None] >= starts[None, :]) & (at_home[:, None] < ends[None, :])
    pick = jnp.repeat(within.astype(FLOAT), rank, axis=1)
    ctx = dict(pick=pick, offset=offset, parity=parity[None])

    stream = to_sequence(tokens).astype(FLOAT)
    d_stream = to_sequence(cotangent).astype(FLOAT)
    gains = lax.all_gather(norm_gain, "col", axis=2, tiled=True)

    def by_doc(factor, axis):
        return jnp.concatenate(
            [lax.dynamic_slice_in_dim(factor, adapter_ids[at], 1, axis) for at in range(docs)], axis
        )

    def gather_rows(value):
        return lax.all_gather(value, "row", axis=0, tiled=True)

    def joined(value, lead_shape, piece):
        parts = [part.reshape(lead_shape + (1, piece)) for part in all_shards(value)]
        return jnp.concatenate(parts, axis=-2).reshape(depth, -1)

    wides, smalls = [], []
    for layer in range(LAYERS):
        wide_inlet = gather_rows(joined(inlet_weight[layer], (depth, 2), part_width))
        wide_outlet = gather_rows(joined(outlet_weight[layer], (depth,), part_width))
        wide_expand = gather_rows(joined(expand_weight[layer], (depth, 2), part_spread))
        wide_shrink = gather_rows(joined(shrink_weight[layer], (depth,), part_spread))
        wides.append((wide_inlet, wide_outlet, wide_expand, wide_shrink))

        def lower_t(factor):
            return by_doc(jnp.moveaxis(factor[layer], 0, -1), factor.ndim - 4)

        def upper_t(factor):
            return by_doc(factor[layer], factor.ndim - 4)

        narrow = jnp.concatenate(
            [
                upper_t(inlet_upper).reshape(-1, part_width),
                lower_t(outlet_lower).reshape(-1, part_width),
            ]
        )
        broad = jnp.concatenate(
            [
                upper_t(expand_upper).reshape(-1, part_spread),
                lower_t(shrink_lower).reshape(-1, part_spread),
            ]
        )
        vectors = jnp.concatenate(
            [conv_weight[layer], gate_bias[layer], conv_bias[layer][None], decay_param[layer][None]]
        )
        narrow, broad, vectors = (
            jnp.concatenate(all_shards(value), axis=1) for value in (narrow, broad, vectors)
        )
        ranks = docs * rank
        smalls.append(
            dict(
                inlet_lower=lower_t(inlet_lower).reshape(2 * ranks, d_model),
                inlet_upper=narrow[: 2 * ranks].reshape(2, ranks, -1),
                outlet_lower=narrow[2 * ranks :],
                outlet_upper=upper_t(outlet_upper).reshape(ranks, d_model),
                expand_lower=lower_t(expand_lower).reshape(2 * ranks, d_model),
                expand_upper=broad[: 2 * ranks].reshape(2, ranks, -1),
                shrink_lower=broad[2 * ranks :],
                shrink_upper=upper_t(shrink_upper).reshape(ranks, d_model),
                conv_weight=vectors[:CONV],
                gate_bias=vectors[CONV : CONV + 2],
                conv_bias=vectors[CONV + 2 : CONV + 3],
                soft=jax.nn.softplus(vectors[CONV + 3 : CONV + 4]),
                gate_weight=jnp.concatenate(all_shards(gate_weight[layer]), axis=1),
            )
        )

    outputs, saved = [], []
    for layer in range(LAYERS):
        stream, kept = layer_forward(stream, wides[layer], smalls[layer], gains[layer], ctx)
        outputs.append(from_sequence(stream.astype(BRAIN)))
        saved.append(kept)
    shared, narrow, broad = [None] * LAYERS, [None] * LAYERS, [None] * LAYERS
    for layer in reversed(range(LAYERS)):
        d_stream, everywhere, split = layer_backward(
            d_stream, wides[layer], smalls[layer], gains[layer], saved[layer], ctx
        )
        shared[layer] = lax.psum(everywhere.astype(BRAIN), ("row", "col")).astype(FLOAT)
        narrow[layer] = lax.psum(owned(split[0], shards), "row").astype(FLOAT)
        broad[layer] = lax.psum(owned(split[1], shards), "row").astype(FLOAT)
    shared, narrow, broad = jnp.stack(shared), jnp.stack(narrow), jnp.stack(broad)
    ranks = docs * rank
    spread_out = (adapter_ids[None, :] == jnp.arange(adapters, dtype=jnp.int32)[:, None])

    def by_adapter(grad, count):
        grad = grad.reshape(LAYERS, count, docs, rank, -1)
        total = 0.0
        for doc in range(docs):
            total = total + jnp.where(
                spread_out[None, None, :, doc, None, None], grad[:, :, doc][:, :, None], 0.0
            )
        return total

    def lower_out(grad, count):
        grad = by_adapter(grad, count)
        if count == 1:
            grad = grad[:, 0]
        return jnp.moveaxis(grad, -1, 1)

    return (
        jnp.stack(outputs, axis=0),
        from_sequence(d_stream),
        lower_out(shared[:, : 2 * ranks], 2),
        by_adapter(narrow[:, : 2 * ranks], 2),
        lower_out(narrow[:, 2 * ranks :], 1),
        by_adapter(shared[:, 2 * ranks : 3 * ranks], 1)[:, 0],
        lower_out(shared[:, 3 * ranks : 5 * ranks], 2),
        by_adapter(broad[:, : 2 * ranks], 2),
        lower_out(broad[:, 2 * ranks :], 1),
        by_adapter(shared[:, 5 * ranks :], 1)[:, 0],
    )


def solution(mesh):
    return jax.shard_map(
        local,
        mesh=mesh,
        in_specs=(
            P("row", "col"),
            P("row", "col"),
            P(),
            P(),
            P(None, None, "col"),
            P(None, "row", None, "col"),
            P(),
            P(None, None, None, None, "col"),
            P(None, None, "col"),
            P(None, "col"),
            P(None, None, "col", None, None),
            P(None, None, "col"),
            P(None, "col"),
            P(None, "row", "col"),
            P(None, "col", None, None),
            P(),
            P(None, "row", None, "col"),
            P(),
            P(None, None, None, None, "col"),
            P(None, "row", "col"),
            P(None, "col", None, None),
            P(),
        ),
        out_specs=(
            P(None, "row", "col"),
            P("row", "col"),
            P(),
            P(None, None, None, None, "col"),
            P(None, "col", None, None),
            P(),
            P(),
            P(None, None, None, None, "col"),
            P(None, "col", None, None),
            P(),
        ),
        check_vma=False,
    )
```

```python
from functools import partial

import jax
import jax.numpy as jnp
from jax import lax
from jax.experimental import pallas as pl
from jax.experimental.pallas import tpu as pltpu
from jax.sharding import PartitionSpec as P

HS = 256
CONV = 4
LAYERS = 2
SEGS = 8

EPSILON = 1e-06
FLOAT = jnp.float32
BRAIN = jnp.bfloat16
VMEM_BYTES = 48 * 1024 * 1024
CURVE = 0.7978845608028654
CUBIC = 0.044715
LANES = 128
SLABS = HS // LANES
MESH = pl.DeviceIdType.MESH


def nn(left, right):
    return lax.dot_general(left, right, (((1,), (0,)), ((), ())), preferred_element_type=FLOAT)


def nt(left, right):
    return lax.dot_general(left, right, (((1,), (1,)), ((), ())), preferred_element_type=FLOAT)


def tn(left, right):
    return lax.dot_general(left, right, (((0,), (0,)), ((), ())), preferred_element_type=FLOAT)


def gelu_tanh(value):
    return 0.5 * value * (1.0 + jnp.tanh(CURVE * (value + CUBIC * value * value * value)))


def gelu_pair(value):
    square = value * value
    bend = jnp.tanh(CURVE * value * (1.0 + CUBIC * square))
    half = 0.5 * (1.0 + bend)
    slope = half + 0.5 * value * (1.0 - bend * bend) * CURVE * (1.0 + 3.0 * CUBIC * square)
    return value * half, slope


def one_less_square(twice, square):
    series = -twice * (
        1.0 + twice * (0.5 + twice * (1.0 / 6.0 + twice * (1.0 / 24.0 + twice * (1.0 / 120.0))))
    )
    return jnp.where(twice > -0.1, series, 1.0 - square)


def gate_values(conv, gate_w, gate_b, soft):
    rate = jax.nn.sigmoid(nn(conv, gate_w[0]) + gate_b[0:1])
    inward = jax.nn.sigmoid(nn(conv, gate_w[1]) + gate_b[1:2])
    log_decay = (-8.0 * soft) * rate
    raw = jnp.exp(log_decay)
    gap = one_less_square(2.0 * log_decay, raw * raw)
    return rate, inward, raw, gap


def chain(axis_row="row", axis_col="col"):
    blocks_in_row = lax.axis_size(axis_col) // 2
    blocks = lax.axis_size(axis_row) * blocks_in_row
    col = lax.axis_index(axis_col)
    side = col % 2
    here = lax.axis_index(axis_row) * blocks_in_row + col // 2

    def device(by):
        block = (here + by + blocks) % blocks
        return (block // blocks_in_row, (block % blocks_in_row) * 2 + side)

    return blocks, blocks_in_row, here, side, device


def greet(blocks, device):
    barrier = pltpu.get_barrier_semaphore()
    for by in range(1, blocks):
        pl.semaphore_signal(barrier, inc=1, device_id=device(by), device_id_type=MESH)
    pl.semaphore_wait(barrier, blocks - 1)


def share_totals(blocks, device, direction, totals, inbox, send_sems, recv_sems):
    copies = [
        pltpu.make_async_remote_copy(
            src_ref=totals,
            dst_ref=inbox.at[by - 1],
            send_sem=send_sems.at[by - 1],
            recv_sem=recv_sems.at[by - 1],
            device_id=device(direction * by),
            device_id_type=MESH,
        )
        for by in range(1, blocks)
    ]
    for copy in copies:
        copy.start()
    for copy in copies:
        copy.wait()


def folded(blocks, shards, ahead, direction, inbox):
    slabs = inbox.shape[1] // 2
    piece = slabs // shards
    state = jnp.zeros((slabs, LANES), FLOAT)
    for by in reversed(range(1, blocks)):
        turn = (direction * by) % shards * piece
        cum, add = (
            jnp.concatenate([part[turn:], part[:turn]], axis=0) if turn else part
            for part in (inbox[by - 1, 0:slabs], inbox[by - 1, slabs : 2 * slabs])
        )
        state = jnp.where(ahead >= by, cum * state + add, state)
    return state


def forward_kernel(
    lead, gate, offset, conv_w, conv_b, gate_w, gate_b, soft,
    conv_out, decay_out, hidden_out, mixed_out, carry_out,
    ext, drive, state_all, cum_all, seg, totals, halo, inbox,
    halo_sems, send_sems, recv_sems,
):
    rows, width = lead.shape
    heads = width // HS
    half = rows // 2
    span = rows // SEGS
    slabs = width // LANES
    blocks, shards, here, side, device = chain()
    start = pl.multiple_of(side * half, half)
    other = pl.multiple_of(half - side * half, half)
    greet(blocks, device)
    rim = pltpu.make_async_remote_copy(
        src_ref=lead.at[pl.ds(pl.multiple_of(other + half - 8, 8), 8)],
        dst_ref=halo,
        send_sem=halo_sems.at[0],
        recv_sem=halo_sems.at[1],
        device_id=device(1),
        device_id_type=MESH,
    )
    rim.start()
    rim.wait()

    def run_head(head, nothing):
        at = pl.ds(pl.multiple_of(head * HS, HS), HS)
        there = (head + heads // shards) % heads
        ext[0:8] = halo[:, pl.ds(pl.multiple_of(there * HS, HS), HS)]
        ext[8 : 8 + half] = lead[pl.ds(start, half), at]
        ext[8 + half : 8 + rows] = lead[pl.ds(other, half), at]
        place = offset[...]
        total = conv_b[:, at] + conv_w[0:1, at] * ext[8 : 8 + rows]
        for step in range(1, CONV):
            valid = (place >= step).astype(FLOAT)
            total = total + conv_w[step : step + 1, at] * ext[8 - step : 8 - step + rows] * valid
        conv = total.astype(BRAIN)
        conv_out[:, at] = conv
        rate, inward, raw, gap = gate_values(
            conv, (gate_w[0, head], gate_w[1, head]), gate_b[:, at], soft[:, at]
        )
        first = (place == 0).astype(FLOAT)
        keep = 1.0 - first
        decay = raw * keep
        pushed = (keep * jnp.sqrt(gap) + first) * inward * conv.astype(FLOAT)
        for slab in range(SLABS):
            decay_out[head * SLABS + slab] = decay[:, slab * LANES : (slab + 1) * LANES]
            drive[slab] = pushed[:, slab * LANES : (slab + 1) * LANES]

        def advance(step, carried):
            where = pl.ds(step, SEGS, stride=span)
            after = []
            for slab, (state, cum) in enumerate(carried):
                rates = decay_out[head * SLABS + slab, where, :]
                state = rates * state + drive[slab, where, :]
                cum = rates * cum
                state_all[head * SLABS + slab, where, :] = state
                cum_all[head * SLABS + slab, where, :] = cum
                after.append((state, cum))
            return tuple(after)

        fresh = (jnp.zeros((SEGS, LANES), FLOAT), jnp.ones((SEGS, LANES), FLOAT))
        ends = lax.fori_loop(0, span, advance, (fresh,) * SLABS, unroll=8)
        for slab, (state, cum) in enumerate(ends):
            run_state = jnp.zeros((1, LANES), FLOAT)
            run_cum = jnp.ones((1, LANES), FLOAT)
            at_slab = head * SLABS + slab
            for part in range(SEGS):
                seg[at_slab, part : part + 1] = run_state
                seg[at_slab, SEGS + part : SEGS + part + 1] = run_cum
                run_state = cum[part : part + 1] * run_state + state[part : part + 1]
                run_cum = cum[part : part + 1] * run_cum
            totals[pl.ds(at_slab, 1)] = run_cum
            totals[pl.ds(slabs + at_slab, 1)] = run_state
        return nothing

    lax.fori_loop(0, heads, run_head, 0)
    share_totals(blocks, device, 1, totals, inbox, send_sems, recv_sems)
    carry_out[...] = folded(blocks, shards, here, 1, inbox)

    def mix_slab(slab, nothing):
        at = pl.ds(pl.multiple_of(slab * LANES, LANES), LANES)
        entering = seg[slab, 0:SEGS] + seg[slab, SEGS : 2 * SEGS] * carry_out[pl.ds(slab, 1)]
        for part in range(SEGS):
            lines = slice(part * span, (part + 1) * span)
            hidden_out[slab, lines] = (
                state_all[slab, lines] + cum_all[slab, lines] * entering[part : part + 1]
            )
        for place, lines in ((start, slice(0, half)), (other, slice(half, rows))):
            mixed_out[pl.ds(place, half), at] = (
                hidden_out[slab, lines] * gelu_tanh(gate[pl.ds(place, half), at])
            ).astype(BRAIN)
        return nothing

    lax.fori_loop(0, slabs, mix_slab, 0)


def backward_kernel(
    grad, gate, hidden, decay, carry, conv, offset, conv_w, gate_w, gate_b, soft,
    branch_grad,
    ext, prior, grads, chain_decay, local_all, reach_all, seg, totals, arriving, heads_out,
    heads_in, tails, inbox, halo_sems, send_sems, recv_sems,
):
    rows, width = grad.shape
    heads = width // HS
    half = rows // 2
    span = rows // SEGS
    slabs = width // LANES
    blocks, shards, here, side, device = chain()
    start = pl.multiple_of(side * half, half)
    other = pl.multiple_of(half - side * half, half)
    greet(blocks, device)

    def run_slab(slab, nothing):
        at = pl.ds(pl.multiple_of(slab * LANES, LANES), LANES)
        gate_at = pl.ds(pl.multiple_of(width + slab * LANES, LANES), LANES)
        for place, lines in ((start, slice(0, half)), (other, slice(half, rows))):
            value, slope = gelu_pair(gate[pl.ds(place, half), at])
            coming = grad[pl.ds(place, half), at]
            grads[lines] = coming * value
            branch_grad[pl.ds(place, half), gate_at] = (
                coming * hidden[slab, lines] * slope
            ).astype(BRAIN)
        chain_decay[0:rows] = decay[slab]
        chain_decay[rows : rows + 8] = jnp.ones((8, LANES), FLOAT)

        def retreat(turn, carried):
            state, cum = carried
            step = span - 1 - turn
            where = pl.ds(step, SEGS, stride=span)
            rates = chain_decay[pl.ds(step + 1, SEGS, stride=span), :]
            state = rates * state + grads[where, :]
            cum = rates * cum
            local_all[slab, where, :] = state
            reach_all[slab, where, :] = cum
            return state, cum

        fresh = (jnp.zeros((SEGS, LANES), FLOAT), jnp.ones((SEGS, LANES), FLOAT))
        state, cum = lax.fori_loop(0, span, retreat, fresh, unroll=8)
        run_state = jnp.zeros((1, LANES), FLOAT)
        run_cum = jnp.ones((1, LANES), FLOAT)
        for part in reversed(range(SEGS)):
            seg[slab, part : part + 1] = run_state
            seg[slab, SEGS + part : SEGS + part + 1] = run_cum
            run_state = cum[part : part + 1] * run_state + state[part : part + 1]
            run_cum = cum[part : part + 1] * run_cum
        opening = chain_decay[0:1]
        totals[pl.ds(slab, 1)] = run_cum * opening
        totals[pl.ds(slabs + slab, 1)] = run_state * opening
        return nothing

    lax.fori_loop(0, slabs, run_slab, 0)
    share_totals(blocks, device, -1, totals, inbox, send_sems, recv_sems)
    arriving[...] = folded(blocks, shards, blocks - 1 - here, -1, inbox)

    def run_head(head, nothing):
        at = pl.ds(pl.multiple_of(head * HS, HS), HS)
        for slab in range(SLABS):
            slot = head * SLABS + slab
            lanes = slice(slab * LANES, (slab + 1) * LANES)
            entering = seg[slot, 0:SEGS] + seg[slot, SEGS : 2 * SEGS] * arriving[pl.ds(slot, 1)]
            for part in range(SEGS):
                lines = slice(part * span, (part + 1) * span)
                ext[lines, lanes] = (
                    local_all[slot, lines] + reach_all[slot, lines] * entering[part : part + 1]
                )
            prior[7:8, lanes] = carry[pl.ds(slot, 1)]
            prior[8 : 8 + rows, lanes] = hidden[slot]
        carried = ext[0:rows]
        before = prior[7 : 7 + rows]
        low = conv[:, at]
        value = low.astype(FLOAT)
        place = offset[...]
        first = (place == 0).astype(FLOAT)
        keep = 1.0 - first
        softness = soft[:, at]
        weights = (gate_w[0, head], gate_w[1, head])
        rate, inward, raw, gap = gate_values(low, weights, gate_b[:, at], softness)
        root = jnp.sqrt(gap)
        scale = keep * root + first
        pushed = carried * inward
        log_grad = keep * raw * (carried * before - pushed * value * (raw / root))
        rate_grad = ((-8.0 * softness) * log_grad * rate * (1.0 - rate)).astype(BRAIN)
        scaled = carried * scale
        input_grad = (scaled * value * inward * (1.0 - inward)).astype(BRAIN)
        conv_grad = scaled * inward + nt(rate_grad, weights[0]) + nt(input_grad, weights[1])
        ext[rows : rows + 8] = jnp.zeros((8, HS), FLOAT)
        total = conv_w[0:1, at] * conv_grad
        head_sum = jnp.zeros((8, HS), FLOAT)
        lines = lax.broadcasted_iota(jnp.int32, (8, 1), 0)
        for step in range(1, CONV):
            term = conv_w[step : step + 1, at] * conv_grad * (place >= step).astype(FLOAT)
            ext[0:rows] = term
            total = total + ext[step : step + rows]
            moved = pltpu.roll(term[0:8], 8 - step, 0)
            head_sum = head_sum + jnp.where(lines >= 8 - step, moved, 0.0)
        heads_out[:, at] = head_sum
        tails[:, at] = total[rows - 8 : rows]
        branch_grad[pl.ds(start, half), at] = total[0:half].astype(BRAIN)
        branch_grad[pl.ds(other, half), at] = total[half:rows].astype(BRAIN)
        return nothing

    lax.fori_loop(0, heads, run_head, 0)
    rim = pltpu.make_async_remote_copy(
        src_ref=heads_out,
        dst_ref=heads_in,
        send_sem=halo_sems.at[0],
        recv_sem=halo_sems.at[1],
        device_id=device(-1),
        device_id_type=MESH,
    )
    rim.start()
    rim.wait()
    followed = jnp.where(here < blocks - 1, 1.0, 0.0)
    for head in range(heads):
        at = slice(head * HS, (head + 1) * HS)
        there = (head - heads // shards) % heads
        whole = tails[:, at] + heads_in[:, there * HS : (there + 1) * HS] * followed
        kept = branch_grad[pl.ds(pl.multiple_of(other + half - 16, 16), 16), at]
        tails_pair = jnp.concatenate([kept[0:8], whole.astype(BRAIN)], axis=0)
        branch_grad[pl.ds(pl.multiple_of(other + half - 16, 16), 16), at] = tails_pair


def block_call(kernel, ident, operands, outs, scratch):
    whole = pl.BlockSpec(memory_space=pltpu.VMEM)
    return pl.pallas_call(
        kernel,
        out_shape=[jax.ShapeDtypeStruct(*out) for out in outs],
        in_specs=[whole] * len(operands),
        out_specs=[whole] * len(outs),
        scratch_shapes=scratch,
        compiler_params=pltpu.CompilerParams(
            vmem_limit_bytes=VMEM_BYTES, collective_id=ident, has_side_effects=True
        ),
    )(*operands)


def message_scratch(width):
    others = lax.axis_size("row") * lax.axis_size("col") // 2 - 1
    slabs = width // LANES
    return [
        pltpu.VMEM((others, 2 * slabs, LANES), FLOAT),
        pltpu.SemaphoreType.DMA((2,)),
        pltpu.SemaphoreType.DMA((others,)),
        pltpu.SemaphoreType.DMA((others,)),
    ]


def recur_forward(lead, gate, offset, small):
    rows, width = lead.shape
    slabs = width // LANES
    stack = (slabs, rows, LANES)
    return block_call(
        forward_kernel,
        0,
        [lead, gate, offset, small["conv_weight"], small["conv_bias"], small["gate_weight"],
         small["gate_bias"], small["soft"]],
        [((rows, width), BRAIN), (stack, FLOAT), (stack, FLOAT), ((rows, width), BRAIN),
         ((slabs, LANES), FLOAT)],
        [
            pltpu.VMEM((rows + 8, HS), FLOAT),
            pltpu.VMEM((SLABS, rows, LANES), FLOAT),
            pltpu.VMEM(stack, FLOAT),
            pltpu.VMEM(stack, FLOAT),
            pltpu.VMEM((slabs, 2 * SEGS, LANES), FLOAT),
            pltpu.VMEM((2 * slabs, LANES), FLOAT),
            pltpu.VMEM((8, width), FLOAT),
        ]
        + message_scratch(width),
    )


def recur_backward(grad, kept, offset, small):
    rows, width = grad.shape
    slabs = width // LANES
    stack = (slabs, rows, LANES)
    return block_call(
        backward_kernel,
        1,
        [grad, kept["gate"], kept["hidden"], kept["decay"], kept["state_in"], kept["conv"], offset,
         small["conv_weight"], small["gate_weight"], small["gate_bias"], small["soft"]],
        [((rows, 2 * width), BRAIN)],
        [
            pltpu.VMEM((rows + 8, HS), FLOAT),
            pltpu.VMEM((rows + 8, HS), FLOAT),
            pltpu.VMEM((rows, LANES), FLOAT),
            pltpu.VMEM((rows + 8, LANES), FLOAT),
            pltpu.VMEM(stack, FLOAT),
            pltpu.VMEM(stack, FLOAT),
            pltpu.VMEM((slabs, 2 * SEGS, LANES), FLOAT),
            pltpu.VMEM((2 * slabs, LANES), FLOAT),
            pltpu.VMEM((slabs, LANES), FLOAT),
            pltpu.VMEM((8, width), FLOAT),
            pltpu.VMEM((8, width), FLOAT),
            pltpu.VMEM((8, width), FLOAT),
        ]
        + message_scratch(width),
    )[0]


def partner(value):
    peers = lax.axis_size("col")
    return lax.ppermute(value, "col", [(at, at ^ 1) for at in range(peers)])


def from_shard(value, turn):
    peers = lax.axis_size("col")
    return lax.ppermute(value, "col", [((at + 2 * turn) % peers, at) for at in range(peers)])


def to_shard(value, turn):
    peers = lax.axis_size("col")
    return lax.ppermute(value, "col", [(at, (at + 2 * turn) % peers) for at in range(peers)])


def all_shards(value):
    return [value] + [from_shard(value, turn) for turn in range(1, lax.axis_size("col") // 2)]


def after(value, anchor):
    return value if anchor is None else lax.optimization_barrier((value, anchor))[0]


def whole_width(value):
    peers = lax.axis_size("col")
    parts = [value] + [
        lax.ppermute(value, "col", [((at + turn) % peers, at) for at in range(peers)])
        for turn in range(1, peers)
    ]
    stacked = jnp.roll(jnp.stack(parts), lax.axis_index("col"), axis=0)
    return jnp.moveaxis(stacked, 0, -2).reshape(value.shape[:-1] + (-1,))


def to_sequence(value):
    return lax.all_to_all(value, "col", split_axis=0, concat_axis=1, tiled=True)


def from_sequence(value):
    return lax.all_to_all(value, "col", split_axis=1, concat_axis=0, tiled=True)


def both_halves(value):
    return jnp.concatenate([value, partner(value)], axis=0)


def half_share(own, other):
    return own + partner(other.astype(BRAIN)).astype(FLOAT)


def norm_forward(stream, gain):
    scale = lax.rsqrt(jnp.mean(stream * stream, axis=1, keepdims=True) + EPSILON)
    return scale, (stream * scale * gain[None, :]).astype(BRAIN)


def norm_backward(stream, scale, gain, d_normed):
    gained = d_normed * gain[None, :]
    total = jnp.mean(gained * stream, axis=1, keepdims=True)
    return scale * gained - stream * (scale * scale * scale * total)


def masked(value, pick):
    return (value * pick).astype(BRAIN)


def recur_part(stream, wide, small, gains, ctx):
    inlet, outlet = wide
    pick, offset = ctx["pick"], ctx["offset"]
    ranks = pick.shape[1]
    own = stream.shape[0]
    rows = 2 * own
    width = outlet.shape[1]

    scale_one, normed = norm_forward(stream, gains[0])
    normed_full = both_halves(normed)
    low = nt(normed_full, small["inlet_lower"])
    inner = [masked(low[:, b * ranks : (b + 1) * ranks], pick) for b in range(2)]
    branch = nn(normed_full, inlet)
    lead = branch[:, :width] + nn(inner[0], small["inlet_upper"][0])
    gate = branch[:, width:] + nn(inner[1], small["inlet_upper"][1])
    conv, decay, hidden, mixed, state_in = recur_forward(lead, gate, offset, small)
    lowrank = masked(nt(mixed, small["outlet_lower"]), pick)

    def outward(part):
        return nt(mixed[part], outlet) + nn(lowrank[part], small["outlet_upper"])

    middle = stream + half_share(outward(slice(0, own)), outward(slice(own, rows)))
    kept = dict(
        stream=stream, scale_one=scale_one, normed_full=normed_full, inner=inner, lead=lead,
        gate=gate, conv=conv, decay=decay, hidden=hidden, state_in=state_in, mixed=mixed,
        lowrank=lowrank, middle=middle,
    )
    return middle, kept


def hidden_part(middle, wide, small, gains, ctx):
    expand, shrink = wide
    pick = ctx["pick"]
    ranks = pick.shape[1]
    own = middle.shape[0]
    rows = 2 * own
    spread = shrink.shape[1]
    scale_two, normed_two = norm_forward(middle, gains[1])
    normed_two_full = both_halves(normed_two)
    low_two = nt(normed_two_full, small["expand_lower"])
    inner_two = [masked(low_two[:, b * ranks : (b + 1) * ranks], pick) for b in range(2)]
    branch_two = nn(normed_two_full, expand)
    up_gate = branch_two[:, :spread] + nn(inner_two[0], small["expand_upper"][0])
    up_value = branch_two[:, spread:] + nn(inner_two[1], small["expand_upper"][1])
    product = (gelu_tanh(up_gate) * up_value).astype(BRAIN)
    lowrank_two = masked(nt(product, small["shrink_lower"]), pick)

    def downward(part):
        return nt(product[part], shrink) + nn(lowrank_two[part], small["shrink_upper"])

    result = middle + half_share(downward(slice(0, own)), downward(slice(own, rows)))
    kept = dict(
        scale_two=scale_two, normed_two_full=normed_two_full, inner_two=inner_two,
        up_gate=up_gate, up_value=up_value, product=product, lowrank_two=lowrank_two,
    )
    return result, kept


def layer_backward(d_stream, wide, small, gains, kept, ctx):
    inlet, outlet, expand, shrink = wide
    pick, offset = ctx["pick"], ctx["offset"]
    own = d_stream.shape[0]
    rows = 2 * own
    width = outlet.shape[1]
    spread = shrink.shape[1]

    d_out = both_halves(d_stream.astype(BRAIN))
    d_low_two = masked(nt(d_out, small["shrink_upper"]), pick)
    d_product = nn(d_out, shrink) + nn(d_low_two, small["shrink_lower"])
    shrink_upper_grad = tn(kept["lowrank_two"], d_out)
    shrink_lower_grad = tn(d_low_two, kept["product"])
    value, slope = gelu_pair(kept["up_gate"])
    d_branch_two = jnp.concatenate(
        [(slope * kept["up_value"] * d_product).astype(BRAIN), (value * d_product).astype(BRAIN)],
        axis=1,
    )
    d_inner_two = jnp.concatenate(
        [
            masked(nt(d_branch_two[:, b * spread : (b + 1) * spread], small["expand_upper"][b]), pick)
            for b in range(2)
        ],
        axis=1,
    )

    def inward_two(part):
        return nt(d_branch_two[part], expand) + nn(d_inner_two[part], small["expand_lower"])

    d_normed_two = half_share(inward_two(slice(0, own)), inward_two(slice(own, rows)))
    expand_lower_grad = tn(d_inner_two, kept["normed_two_full"])
    expand_upper_grad = jnp.concatenate(
        [
            tn(kept["inner_two"][b], d_branch_two[:, b * spread : (b + 1) * spread])
            for b in range(2)
        ],
        axis=0,
    )
    d_middle = d_stream + norm_backward(kept["middle"], kept["scale_two"], gains[1], d_normed_two)

    d_mid = both_halves(d_middle.astype(BRAIN))
    d_low = masked(nt(d_mid, small["outlet_upper"]), pick)
    d_mixed = nn(d_mid, outlet) + nn(d_low, small["outlet_lower"])
    outlet_upper_grad = tn(kept["lowrank"], d_mid)
    outlet_lower_grad = tn(d_low, kept["mixed"])
    d_branch = recur_backward(d_mixed, kept, offset, small)
    d_inner = jnp.concatenate(
        [
            masked(nt(d_branch[:, b * width : (b + 1) * width], small["inlet_upper"][b]), pick)
            for b in range(2)
        ],
        axis=1,
    )

    def inward(part):
        return nt(d_branch[part], inlet) + nn(d_inner[part], small["inlet_lower"])

    d_normed = half_share(inward(slice(0, own)), inward(slice(own, rows)))
    inlet_lower_grad = tn(d_inner, kept["normed_full"])
    inlet_upper_grad = jnp.concatenate(
        [tn(kept["inner"][b], d_branch[:, b * width : (b + 1) * width]) for b in range(2)], axis=0
    )
    d_input = d_middle + norm_backward(kept["stream"], kept["scale_one"], gains[0], d_normed)
    shared = jnp.concatenate(
        [inlet_lower_grad, outlet_upper_grad, expand_lower_grad, shrink_upper_grad], axis=0
    )
    split = (
        jnp.concatenate([inlet_upper_grad, outlet_lower_grad], axis=0),
        jnp.concatenate([expand_upper_grad, shrink_lower_grad], axis=0),
    )
    return d_input, shared, split


def owned(grad, shards):
    piece = grad.shape[1] // shards
    parts = [grad[:, turn * piece : (turn + 1) * piece].astype(BRAIN) for turn in range(shards)]
    total = parts[0].astype(FLOAT)
    for turn in range(1, shards):
        total = total + to_shard(parts[turn], turn).astype(FLOAT)
    return total.astype(BRAIN)


def local(
    tokens, cotangent, adapter_ids, doc_lengths, norm_gain, inlet_weight, inlet_lower, inlet_upper,
    conv_weight, conv_bias, gate_weight, gate_bias, decay_param, outlet_weight, outlet_lower,
    outlet_upper, expand_weight, expand_lower, expand_upper, shrink_weight, shrink_lower,
    shrink_upper,
):
    row_at, col_at = lax.axis_index("row"), lax.axis_index("col")
    cols = lax.axis_size("col")
    shards = cols // 2
    rows = tokens.shape[0]
    own = rows // cols
    block = 2 * own
    docs = adapter_ids.shape[0]
    adapters, rank = inlet_lower.shape[3:]
    part_width, part_spread = inlet_weight.shape[3], expand_weight.shape[3]
    d_model = inlet_lower.shape[1]

    parity = (col_at % 2).astype(jnp.int32)
    ends = jnp.cumsum(doc_lengths)
    starts = ends - doc_lengths
    ordered = row_at * rows + (col_at // 2) * block + jnp.arange(block, dtype=jnp.int32)
    inside = (ordered[:, None] >= starts[None, :]) & (ordered[:, None] < ends[None, :])
    offset = (ordered - jnp.sum(jnp.where(inside, starts[None, :], 0), axis=1))[:, None]
    halves = (parity * own, own - parity * own)
    at_home = jnp.concatenate(
        [ordered[0] + begin + jnp.arange(own, dtype=jnp.int32) for begin in halves]
    )
    within = (at_home[:, None] >= starts[None, :]) & (at_home[:, None] < ends[None, :])
    pick = jnp.repeat(within.astype(FLOAT), rank, axis=1)
    ctx = dict(pick=pick, offset=offset)

    stream = to_sequence(tokens).astype(FLOAT)
    gains = whole_width(norm_gain)

    def by_doc(factor, axis):
        return jnp.concatenate(
            [lax.dynamic_slice_in_dim(factor, adapter_ids[at], 1, axis) for at in range(docs)], axis
        )

    def lower_t(factor):
        return by_doc(jnp.moveaxis(factor, 1, -1), factor.ndim - 3)

    def upper_t(factor):
        return by_doc(factor, factor.ndim - 3)

    ranks = docs * rank
    lows = dict(
        inlet_lower=lower_t(inlet_lower).reshape(LAYERS, 2 * ranks, d_model),
        outlet_upper=upper_t(outlet_upper).reshape(LAYERS, ranks, d_model),
        expand_lower=lower_t(expand_lower).reshape(LAYERS, 2 * ranks, d_model),
        shrink_upper=upper_t(shrink_upper).reshape(LAYERS, ranks, d_model),
    )
    narrow_own = jnp.concatenate(
        [
            upper_t(inlet_upper).reshape(LAYERS, 2 * ranks, part_width),
            lower_t(outlet_lower).reshape(LAYERS, ranks, part_width),
        ],
        axis=1,
    )
    broad_own = jnp.concatenate(
        [
            upper_t(expand_upper).reshape(LAYERS, 2 * ranks, part_spread),
            lower_t(shrink_lower).reshape(LAYERS, ranks, part_spread),
        ],
        axis=1,
    )
    vectors_own = jnp.concatenate(
        [conv_weight, gate_bias, conv_bias[:, None], decay_param[:, None]], axis=1
    )

    def fetch(pair, single, anchor):
        piece = single.shape[1]
        pack = jnp.concatenate([pair[:, 0], pair[:, 1], single], axis=1)
        parts = all_shards(after(pack, anchor))
        columns = [part[:, at * piece : (at + 1) * piece] for at in range(3) for part in parts]
        whole = lax.all_gather(jnp.concatenate(columns, axis=1), "row", axis=0, tiled=True)
        cut = 2 * shards * piece
        return (whole[:, :cut], whole[:, cut:]), parts[-1]

    def recur_weights(layer, anchor):
        wide, last = fetch(inlet_weight[layer], outlet_weight[layer], anchor)
        narrow, vectors, gates = (
            jnp.concatenate(all_shards(after(value, last)), axis=1)
            for value in (narrow_own[layer], vectors_own[layer], gate_weight[layer])
        )
        small = dict(
            inlet_lower=lows["inlet_lower"][layer],
            inlet_upper=narrow[: 2 * ranks].reshape(2, ranks, -1),
            outlet_lower=narrow[2 * ranks :],
            outlet_upper=lows["outlet_upper"][layer],
            conv_weight=vectors[:CONV],
            gate_bias=vectors[CONV : CONV + 2],
            conv_bias=vectors[CONV + 2 : CONV + 3],
            soft=jax.nn.softplus(vectors[CONV + 3 : CONV + 4]),
            gate_weight=gates,
        )
        return wide, small, last

    def hidden_weights(layer, anchor):
        wide, last = fetch(expand_weight[layer], shrink_weight[layer], anchor)
        broad = jnp.concatenate(all_shards(after(broad_own[layer], last)), axis=1)
        small = dict(
            expand_lower=lows["expand_lower"][layer],
            expand_upper=broad[: 2 * ranks].reshape(2, ranks, -1),
            shrink_lower=broad[2 * ranks :],
            shrink_upper=lows["shrink_upper"][layer],
        )
        return wide, small, last

    outputs, saved, wides, smalls = [], [], [], []
    anchor_one = anchor_two = None
    for layer in range(LAYERS):
        wide_one, small_one, last = recur_weights(layer, anchor_one)
        wide_two, small_two, _ = hidden_weights(layer, last if layer == 0 else anchor_two)
        middle, kept = recur_part(stream, wide_one, small_one, gains[layer], ctx)
        stream, more = hidden_part(middle, wide_two, small_two, gains[layer], ctx)
        anchor_one, anchor_two = kept["lead"], middle
        outputs.append(from_sequence(stream.astype(BRAIN)))
        saved.append({**kept, **more})
        wides.append(wide_one + wide_two)
        smalls.append({**small_one, **small_two})
    d_stream = to_sequence(cotangent).astype(FLOAT)
    shared, narrow, broad = [None] * LAYERS, [None] * LAYERS, [None] * LAYERS
    for layer in reversed(range(LAYERS)):
        d_stream, everywhere, split = layer_backward(
            d_stream, wides[layer], smalls[layer], gains[layer], saved[layer], ctx
        )
        shared[layer] = lax.psum(everywhere.astype(BRAIN), ("row", "col")).astype(FLOAT)
        narrow[layer] = lax.psum(owned(split[0], shards), "row").astype(FLOAT)
        broad[layer] = lax.psum(owned(split[1], shards), "row").astype(FLOAT)
    shared, narrow, broad = jnp.stack(shared), jnp.stack(narrow), jnp.stack(broad)
    spread_out = (adapter_ids[None, :] == jnp.arange(adapters, dtype=jnp.int32)[:, None])

    def by_adapter(grad, count):
        grad = grad.reshape(LAYERS, count, docs, rank, -1)
        total = 0.0
        for doc in range(docs):
            total = total + jnp.where(
                spread_out[None, None, :, doc, None, None], grad[:, :, doc][:, :, None], 0.0
            )
        return total

    def lower_out(grad, count):
        grad = by_adapter(grad, count)
        if count == 1:
            grad = grad[:, 0]
        return jnp.moveaxis(grad, -1, 1)

    return (
        jnp.stack(outputs, axis=0),
        from_sequence(d_stream),
        lower_out(shared[:, : 2 * ranks], 2),
        by_adapter(narrow[:, : 2 * ranks], 2),
        lower_out(narrow[:, 2 * ranks :], 1),
        by_adapter(shared[:, 2 * ranks : 3 * ranks], 1)[:, 0],
        lower_out(shared[:, 3 * ranks : 5 * ranks], 2),
        by_adapter(broad[:, : 2 * ranks], 2),
        lower_out(broad[:, 2 * ranks :], 1),
        by_adapter(shared[:, 5 * ranks :], 1)[:, 0],
    )


def solution(mesh):
    return jax.shard_map(
        local,
        mesh=mesh,
        in_specs=(
            P("row", "col"),
            P("row", "col"),
            P(),
            P(),
            P(None, None, "col"),
            P(None, "row", None, "col"),
            P(),
            P(None, None, None, None, "col"),
            P(None, None, "col"),
            P(None, "col"),
            P(None, None, "col", None, None),
            P(None, None, "col"),
            P(None, "col"),
            P(None, "row", "col"),
            P(None, "col", None, None),
            P(),
            P(None, "row", None, "col"),
            P(),
            P(None, None, None, None, "col"),
            P(None, "row", "col"),
            P(None, "col", None, None),
            P(),
        ),
        out_specs=(
            P(None, "row", "col"),
            P("row", "col"),
            P(),
            P(None, None, None, None, "col"),
            P(None, "col", None, None),
            P(),
            P(),
            P(None, None, None, None, "col"),
            P(None, "col", None, None),
            P(),
        ),
        check_vma=False,
    )
```

```python
from functools import partial

import jax
import jax.numpy as jnp
from jax import lax
from jax.experimental import pallas as pl
from jax.experimental.pallas import tpu as pltpu
from jax.sharding import PartitionSpec as P

HS = 256
CONV = 4
LAYERS = 2
SEGS = 8

EPSILON = 1e-06
FLOAT = jnp.float32
BRAIN = jnp.bfloat16
VMEM_BYTES = 48 * 1024 * 1024
CURVE = 0.7978845608028654
CUBIC = 0.044715
LANES = 128
SLABS = HS // LANES
MESH = pl.DeviceIdType.MESH


def nn(left, right):
    return lax.dot_general(left, right, (((1,), (0,)), ((), ())), preferred_element_type=FLOAT)


def nt(left, right):
    return lax.dot_general(left, right, (((1,), (1,)), ((), ())), preferred_element_type=FLOAT)


def tn(left, right):
    return lax.dot_general(left, right, (((0,), (0,)), ((), ())), preferred_element_type=FLOAT)


def gelu_tanh(value):
    return 0.5 * value * (1.0 + jnp.tanh(CURVE * (value + CUBIC * value * value * value)))


def gelu_pair(value):
    square = value * value
    bend = jnp.tanh(CURVE * value * (1.0 + CUBIC * square))
    half = 0.5 * (1.0 + bend)
    slope = half + 0.5 * value * (1.0 - bend * bend) * CURVE * (1.0 + 3.0 * CUBIC * square)
    return value * half, slope


def one_less_square(twice, square):
    series = -twice * (
        1.0 + twice * (0.5 + twice * (1.0 / 6.0 + twice * (1.0 / 24.0 + twice * (1.0 / 120.0))))
    )
    return jnp.where(twice > -0.1, series, 1.0 - square)


def gate_values(conv, gate_w, gate_b, soft):
    rate = jax.nn.sigmoid(nn(conv, gate_w[0]) + gate_b[0:1])
    inward = jax.nn.sigmoid(nn(conv, gate_w[1]) + gate_b[1:2])
    log_decay = (-8.0 * soft) * rate
    raw = jnp.exp(log_decay)
    gap = one_less_square(2.0 * log_decay, raw * raw)
    return rate, inward, raw, gap


def chain(axis_row="row", axis_col="col"):
    blocks_in_row = lax.axis_size(axis_col) // 2
    blocks = lax.axis_size(axis_row) * blocks_in_row
    col = lax.axis_index(axis_col)
    side = col % 2
    here = lax.axis_index(axis_row) * blocks_in_row + col // 2

    def device(by):
        block = (here + by + blocks) % blocks
        return (block // blocks_in_row, (block % blocks_in_row) * 2 + side)

    return blocks, blocks_in_row, here, side, device


def greet(blocks, device):
    barrier = pltpu.get_barrier_semaphore()
    for by in range(1, blocks):
        pl.semaphore_signal(barrier, inc=1, device_id=device(by), device_id_type=MESH)
    pl.semaphore_wait(barrier, blocks - 1)


def share_totals(blocks, device, direction, totals, inbox, send_sems, recv_sems):
    copies = [
        pltpu.make_async_remote_copy(
            src_ref=totals,
            dst_ref=inbox.at[by - 1],
            send_sem=send_sems.at[by - 1],
            recv_sem=recv_sems.at[by - 1],
            device_id=device(direction * by),
            device_id_type=MESH,
        )
        for by in range(1, blocks)
    ]
    for copy in copies:
        copy.start()
    for copy in copies:
        copy.wait()


def folded(blocks, shards, ahead, direction, inbox):
    slabs = inbox.shape[1] // 2
    piece = slabs // shards
    state = jnp.zeros((slabs, LANES), FLOAT)
    for by in reversed(range(1, blocks)):
        turn = (direction * by) % shards * piece
        cum, add = (
            jnp.concatenate([part[turn:], part[:turn]], axis=0) if turn else part
            for part in (inbox[by - 1, 0:slabs], inbox[by - 1, slabs : 2 * slabs])
        )
        state = jnp.where(ahead >= by, cum * state + add, state)
    return state


def forward_kernel(
    lead, gate, offset, conv_w, conv_b, gate_w, gate_b, soft,
    conv_out, decay_out, hidden_out, mixed_out, carry_out,
    ext, drive, state_all, cum_all, seg, totals, halo, inbox,
    halo_sems, send_sems, recv_sems,
):
    rows, width = lead.shape
    heads = width // HS
    half = rows // 2
    span = rows // SEGS
    slabs = width // LANES
    blocks, shards, here, side, device = chain()
    start = pl.multiple_of(side * half, half)
    other = pl.multiple_of(half - side * half, half)
    greet(blocks, device)
    rim = pltpu.make_async_remote_copy(
        src_ref=lead.at[pl.ds(pl.multiple_of(other + half - 8, 8), 8)],
        dst_ref=halo,
        send_sem=halo_sems.at[0],
        recv_sem=halo_sems.at[1],
        device_id=device(1),
        device_id_type=MESH,
    )
    rim.start()
    rim.wait()

    def run_head(head, nothing):
        at = pl.ds(pl.multiple_of(head * HS, HS), HS)
        there = (head + heads // shards) % heads
        ext[0:8] = halo[:, pl.ds(pl.multiple_of(there * HS, HS), HS)]
        ext[8 : 8 + half] = lead[pl.ds(start, half), at]
        ext[8 + half : 8 + rows] = lead[pl.ds(other, half), at]
        place = offset[...]
        total = conv_b[:, at] + conv_w[0:1, at] * ext[8 : 8 + rows]
        for step in range(1, CONV):
            valid = (place >= step).astype(FLOAT)
            total = total + conv_w[step : step + 1, at] * ext[8 - step : 8 - step + rows] * valid
        conv = total.astype(BRAIN)
        conv_out[:, at] = conv
        rate, inward, raw, gap = gate_values(
            conv, (gate_w[0, head], gate_w[1, head]), gate_b[:, at], soft[:, at]
        )
        first = (place == 0).astype(FLOAT)
        keep = 1.0 - first
        decay = raw * keep
        pushed = (keep * jnp.sqrt(gap) + first) * inward * conv.astype(FLOAT)
        for slab in range(SLABS):
            decay_out[head * SLABS + slab] = decay[:, slab * LANES : (slab + 1) * LANES]
            drive[slab] = pushed[:, slab * LANES : (slab + 1) * LANES]

        def advance(step, carried):
            where = pl.ds(step, SEGS, stride=span)
            after = []
            for slab, (state, cum) in enumerate(carried):
                rates = decay_out[head * SLABS + slab, where, :]
                state = rates * state + drive[slab, where, :]
                cum = rates * cum
                state_all[head * SLABS + slab, where, :] = state
                cum_all[head * SLABS + slab, where, :] = cum
                after.append((state, cum))
            return tuple(after)

        fresh = (jnp.zeros((SEGS, LANES), FLOAT), jnp.ones((SEGS, LANES), FLOAT))
        ends = lax.fori_loop(0, span, advance, (fresh,) * SLABS, unroll=8)
        for slab, (state, cum) in enumerate(ends):
            run_state = jnp.zeros((1, LANES), FLOAT)
            run_cum = jnp.ones((1, LANES), FLOAT)
            at_slab = head * SLABS + slab
            for part in range(SEGS):
                seg[at_slab, part : part + 1] = run_state
                seg[at_slab, SEGS + part : SEGS + part + 1] = run_cum
                run_state = cum[part : part + 1] * run_state + state[part : part + 1]
                run_cum = cum[part : part + 1] * run_cum
            totals[pl.ds(at_slab, 1)] = run_cum
            totals[pl.ds(slabs + at_slab, 1)] = run_state
        return nothing

    lax.fori_loop(0, heads, run_head, 0)
    share_totals(blocks, device, 1, totals, inbox, send_sems, recv_sems)
    carry_out[...] = folded(blocks, shards, here, 1, inbox)

    def mix_slab(slab, nothing):
        at = pl.ds(pl.multiple_of(slab * LANES, LANES), LANES)
        entering = seg[slab, 0:SEGS] + seg[slab, SEGS : 2 * SEGS] * carry_out[pl.ds(slab, 1)]
        for part in range(SEGS):
            lines = slice(part * span, (part + 1) * span)
            hidden_out[slab, lines] = (
                state_all[slab, lines] + cum_all[slab, lines] * entering[part : part + 1]
            )
        for place, lines in ((start, slice(0, half)), (other, slice(half, rows))):
            mixed_out[pl.ds(place, half), at] = (
                hidden_out[slab, lines] * gelu_tanh(gate[pl.ds(place, half), at])
            ).astype(BRAIN)
        return nothing

    lax.fori_loop(0, slabs, mix_slab, 0)


def backward_kernel(
    grad, gate, hidden, decay, carry, conv, offset, conv_w, gate_w, gate_b, soft,
    branch_grad,
    ext, prior, grads, chain_decay, local_all, reach_all, seg, totals, arriving, heads_out,
    heads_in, tails, inbox, halo_sems, send_sems, recv_sems,
):
    rows, width = grad.shape
    heads = width // HS
    half = rows // 2
    span = rows // SEGS
    slabs = width // LANES
    blocks, shards, here, side, device = chain()
    start = pl.multiple_of(side * half, half)
    other = pl.multiple_of(half - side * half, half)
    greet(blocks, device)

    def run_slab(slab, nothing):
        at = pl.ds(pl.multiple_of(slab * LANES, LANES), LANES)
        gate_at = pl.ds(pl.multiple_of(width + slab * LANES, LANES), LANES)
        for place, lines in ((start, slice(0, half)), (other, slice(half, rows))):
            value, slope = gelu_pair(gate[pl.ds(place, half), at])
            coming = grad[pl.ds(place, half), at]
            grads[lines] = coming * value
            branch_grad[pl.ds(place, half), gate_at] = (
                coming * hidden[slab, lines] * slope
            ).astype(BRAIN)
        chain_decay[0:rows] = decay[slab]
        chain_decay[rows : rows + 8] = jnp.ones((8, LANES), FLOAT)

        def retreat(turn, carried):
            state, cum = carried
            step = span - 1 - turn
            where = pl.ds(step, SEGS, stride=span)
            rates = chain_decay[pl.ds(step + 1, SEGS, stride=span), :]
            state = rates * state + grads[where, :]
            cum = rates * cum
            local_all[slab, where, :] = state
            reach_all[slab, where, :] = cum
            return state, cum

        fresh = (jnp.zeros((SEGS, LANES), FLOAT), jnp.ones((SEGS, LANES), FLOAT))
        state, cum = lax.fori_loop(0, span, retreat, fresh, unroll=8)
        run_state = jnp.zeros((1, LANES), FLOAT)
        run_cum = jnp.ones((1, LANES), FLOAT)
        for part in reversed(range(SEGS)):
            seg[slab, part : part + 1] = run_state
            seg[slab, SEGS + part : SEGS + part + 1] = run_cum
            run_state = cum[part : part + 1] * run_state + state[part : part + 1]
            run_cum = cum[part : part + 1] * run_cum
        opening = chain_decay[0:1]
        totals[pl.ds(slab, 1)] = run_cum * opening
        totals[pl.ds(slabs + slab, 1)] = run_state * opening
        return nothing

    lax.fori_loop(0, slabs, run_slab, 0)
    share_totals(blocks, device, -1, totals, inbox, send_sems, recv_sems)
    arriving[...] = folded(blocks, shards, blocks - 1 - here, -1, inbox)

    def run_head(head, nothing):
        at = pl.ds(pl.multiple_of(head * HS, HS), HS)
        for slab in range(SLABS):
            slot = head * SLABS + slab
            lanes = slice(slab * LANES, (slab + 1) * LANES)
            entering = seg[slot, 0:SEGS] + seg[slot, SEGS : 2 * SEGS] * arriving[pl.ds(slot, 1)]
            for part in range(SEGS):
                lines = slice(part * span, (part + 1) * span)
                ext[lines, lanes] = (
                    local_all[slot, lines] + reach_all[slot, lines] * entering[part : part + 1]
                )
            prior[7:8, lanes] = carry[pl.ds(slot, 1)]
            prior[8 : 8 + rows, lanes] = hidden[slot]
        carried = ext[0:rows]
        before = prior[7 : 7 + rows]
        low = conv[:, at]
        value = low.astype(FLOAT)
        place = offset[...]
        first = (place == 0).astype(FLOAT)
        keep = 1.0 - first
        softness = soft[:, at]
        weights = (gate_w[0, head], gate_w[1, head])
        rate, inward, raw, gap = gate_values(low, weights, gate_b[:, at], softness)
        root = jnp.sqrt(gap)
        scale = keep * root + first
        pushed = carried * inward
        log_grad = keep * raw * (carried * before - pushed * value * (raw / root))
        rate_grad = ((-8.0 * softness) * log_grad * rate * (1.0 - rate)).astype(BRAIN)
        scaled = carried * scale
        input_grad = (scaled * value * inward * (1.0 - inward)).astype(BRAIN)
        conv_grad = scaled * inward + nt(rate_grad, weights[0]) + nt(input_grad, weights[1])
        ext[rows : rows + 8] = jnp.zeros((8, HS), FLOAT)
        total = conv_w[0:1, at] * conv_grad
        head_sum = jnp.zeros((8, HS), FLOAT)
        lines = lax.broadcasted_iota(jnp.int32, (8, 1), 0)
        for step in range(1, CONV):
            term = conv_w[step : step + 1, at] * conv_grad * (place >= step).astype(FLOAT)
            ext[0:rows] = term
            total = total + ext[step : step + rows]
            moved = pltpu.roll(term[0:8], 8 - step, 0)
            head_sum = head_sum + jnp.where(lines >= 8 - step, moved, 0.0)
        heads_out[:, at] = head_sum
        tails[:, at] = total[rows - 8 : rows]
        branch_grad[pl.ds(start, half), at] = total[0:half].astype(BRAIN)
        branch_grad[pl.ds(other, half), at] = total[half:rows].astype(BRAIN)
        return nothing

    lax.fori_loop(0, heads, run_head, 0)
    rim = pltpu.make_async_remote_copy(
        src_ref=heads_out,
        dst_ref=heads_in,
        send_sem=halo_sems.at[0],
        recv_sem=halo_sems.at[1],
        device_id=device(-1),
        device_id_type=MESH,
    )
    rim.start()
    rim.wait()
    followed = jnp.where(here < blocks - 1, 1.0, 0.0)
    for head in range(heads):
        at = slice(head * HS, (head + 1) * HS)
        there = (head - heads // shards) % heads
        whole = tails[:, at] + heads_in[:, there * HS : (there + 1) * HS] * followed
        kept = branch_grad[pl.ds(pl.multiple_of(other + half - 16, 16), 16), at]
        tails_pair = jnp.concatenate([kept[0:8], whole.astype(BRAIN)], axis=0)
        branch_grad[pl.ds(pl.multiple_of(other + half - 16, 16), 16), at] = tails_pair


def block_call(kernel, ident, operands, outs, scratch):
    whole = pl.BlockSpec(memory_space=pltpu.VMEM)
    return pl.pallas_call(
        kernel,
        out_shape=[jax.ShapeDtypeStruct(*out) for out in outs],
        in_specs=[whole] * len(operands),
        out_specs=[whole] * len(outs),
        scratch_shapes=scratch,
        compiler_params=pltpu.CompilerParams(
            vmem_limit_bytes=VMEM_BYTES, collective_id=ident, has_side_effects=True
        ),
    )(*operands)


def message_scratch(width):
    others = lax.axis_size("row") * lax.axis_size("col") // 2 - 1
    slabs = width // LANES
    return [
        pltpu.VMEM((others, 2 * slabs, LANES), FLOAT),
        pltpu.SemaphoreType.DMA((2,)),
        pltpu.SemaphoreType.DMA((others,)),
        pltpu.SemaphoreType.DMA((others,)),
    ]


def recur_forward(lead, gate, offset, small):
    rows, width = lead.shape
    slabs = width // LANES
    stack = (slabs, rows, LANES)
    return block_call(
        forward_kernel,
        0,
        [lead, gate, offset, small["conv_weight"], small["conv_bias"], small["gate_weight"],
         small["gate_bias"], small["soft"]],
        [((rows, width), BRAIN), (stack, FLOAT), (stack, FLOAT), ((rows, width), BRAIN),
         ((slabs, LANES), FLOAT)],
        [
            pltpu.VMEM((rows + 8, HS), FLOAT),
            pltpu.VMEM((SLABS, rows, LANES), FLOAT),
            pltpu.VMEM(stack, FLOAT),
            pltpu.VMEM(stack, FLOAT),
            pltpu.VMEM((slabs, 2 * SEGS, LANES), FLOAT),
            pltpu.VMEM((2 * slabs, LANES), FLOAT),
            pltpu.VMEM((8, width), FLOAT),
        ]
        + message_scratch(width),
    )


def recur_backward(grad, kept, offset, small):
    rows, width = grad.shape
    slabs = width // LANES
    stack = (slabs, rows, LANES)
    return block_call(
        backward_kernel,
        1,
        [grad, kept["gate"], kept["hidden"], kept["decay"], kept["state_in"], kept["conv"], offset,
         small["conv_weight"], small["gate_weight"], small["gate_bias"], small["soft"]],
        [((rows, 2 * width), BRAIN)],
        [
            pltpu.VMEM((rows + 8, HS), FLOAT),
            pltpu.VMEM((rows + 8, HS), FLOAT),
            pltpu.VMEM((rows, LANES), FLOAT),
            pltpu.VMEM((rows + 8, LANES), FLOAT),
            pltpu.VMEM(stack, FLOAT),
            pltpu.VMEM(stack, FLOAT),
            pltpu.VMEM((slabs, 2 * SEGS, LANES), FLOAT),
            pltpu.VMEM((2 * slabs, LANES), FLOAT),
            pltpu.VMEM((slabs, LANES), FLOAT),
            pltpu.VMEM((8, width), FLOAT),
            pltpu.VMEM((8, width), FLOAT),
            pltpu.VMEM((8, width), FLOAT),
        ]
        + message_scratch(width),
    )[0]


def line_plan(pieces, unit):
    plan, line = [], 0
    for at, (rows, columns) in enumerate(pieces):
        for begin in range(0, columns, LANES):
            done = 0
            while done < rows:
                index, inner = divmod(line, unit)
                count = min(rows - done, unit - inner)
                plan.append(
                    (at, slice(done, done + count), slice(begin, begin + LANES), index,
                     slice(inner, inner + count))
                )
                done += count
                line += count
    return plan


def closing_sizes(shared, split, peers, cols, shards):
    shared_lines = sum(rows * columns for rows, columns in shared) // LANES
    split_lines = sum(rows * columns for rows, columns in split) // LANES // shards
    unit = -(-shared_lines // (peers * cols * 16)) * 16
    part = -(-split_lines // (peers * 16)) * 16
    return unit, part


def remote(source, target, sems, slot, device):
    return pltpu.make_async_remote_copy(
        src_ref=source,
        dst_ref=target,
        send_sem=sems.at[0, slot],
        recv_sem=sems.at[1, slot],
        device_id=device,
        device_id_type=MESH,
    )


def closing_kernel(
    own_part, other_part, stream, d_middle, gain,
    shared_a, shared_b, shared_c, shared_d, split_a, split_b, split_c, split_d,
    tokens_out, shared_out_a, shared_out_b, shared_out_c, shared_out_d,
    split_out_a, split_out_b, split_out_c, split_out_d,
    received, outgoing, flat, inbox, red, red_split, zbox, sbox, zfull, sfull, shared_all,
    split_all, pair_sems, row_sems, col_sems, turn_sems, spread_sems, shared_sems, split_sems,
    token_sems,
):
    shared = (shared_a, shared_b, shared_c, shared_d)
    split = (split_a, split_b, split_c, split_d)
    shared_out = (shared_out_a, shared_out_b, shared_out_c, shared_out_d)
    split_out = (split_out_a, split_out_b, split_out_c, split_out_d)
    peers, cols = lax.axis_size("row"), lax.axis_size("col")
    shards = cols // 2
    row, col = lax.axis_index("row"), lax.axis_index("col")
    own, d_model = stream.shape
    piece = d_model // cols
    unit, part = zbox.shape[1], sbox.shape[1]
    shared_lines = cols * unit

    barrier = pltpu.get_barrier_semaphore()
    for by in range(1, peers):
        pl.semaphore_signal(
            barrier, inc=1, device_id=((row + by) % peers, col), device_id_type=MESH
        )
    for by in range(1, cols):
        pl.semaphore_signal(barrier, inc=1, device_id=(row, (col + by) % cols), device_id_type=MESH)

    sizes = [value.shape for value in shared]
    shared_plan = line_plan(sizes, unit)
    thin = [(value.shape[0], value.shape[1] // shards) for value in split]
    split_plan = line_plan(thin, part)
    flat[...] = jnp.zeros(flat.shape, BRAIN)
    for at, rows, lanes, index, lines in shared_plan:
        begin = index % cols * unit
        flat[index // cols, begin + lines.start : begin + lines.stop] = shared[at][
            rows, lanes
        ].astype(BRAIN)
    for turn in range(shards):
        for at, rows, lanes, index, lines in split_plan:
            begin = shared_lines + turn * part
            skip = turn * thin[at][1]
            flat[index, begin + lines.start : begin + lines.stop] = split[at][
                rows, skip + lanes.start : skip + lanes.stop
            ].astype(BRAIN)
    pl.semaphore_wait(barrier, peers + cols - 2)

    pair = remote(other_part, received, pair_sems, 0, (row, col + 1 - 2 * (col % 2)))
    pair.start()
    scattered = []
    for by in range(1, peers):
        to = (row + by) % peers
        copy = remote(flat.at[to], inbox.at[by - 1], row_sems, by - 1, (to, col))
        copy.start()
        scattered.append(copy)

    pair.wait()

    def norm_rows(at, nothing):
        lines = pl.ds(pl.multiple_of(at * 16, 16), 16)
        value = stream[lines]
        scale = lax.rsqrt(jnp.mean(value * value, axis=1, keepdims=True) + EPSILON)
        gained = (own_part[lines] + received[lines].astype(FLOAT)) * gain[...]
        total = jnp.mean(gained * value, axis=1, keepdims=True)
        result = d_middle[lines] + scale * gained - value * (scale * scale * scale * total)
        for to in range(cols):
            outgoing[to, lines] = result[:, to * piece : (to + 1) * piece]
        return nothing

    lax.fori_loop(0, own // 16, norm_rows, 0)
    mine = pl.ds(pl.multiple_of(col * own, own), own)
    returned = []
    for by in range(1, cols):
        to = (col + by) % cols
        copy = remote(outgoing.at[to], tokens_out.at[mine], token_sems, by - 1, (row, to))
        copy.start()
        returned.append(copy)
    tokens_out[mine] = outgoing[col]

    for copy in scattered:
        copy.wait()
    total = flat[row].astype(FLOAT)
    for by in range(1, peers):
        total = total + inbox[by - 1].astype(FLOAT)
    for at in range(cols):
        red[at] = total[at * unit : (at + 1) * unit].astype(BRAIN)
    for turn in range(shards):
        begin = shared_lines + turn * part
        red_split[turn] = total[begin : begin + part].astype(BRAIN)

    copies = []
    for by in range(1, cols):
        to = (col + by) % cols
        copies.append(remote(red.at[to], zbox.at[by - 1], col_sems, by - 1, (row, to)))
    for turn in range(1, shards):
        to = (col + 2 * turn) % cols
        copies.append(remote(red_split.at[turn], sbox.at[turn - 1], turn_sems, turn - 1, (row, to)))
    for copy in copies:
        copy.start()
    for copy in copies:
        copy.wait()
    total = red[col].astype(FLOAT)
    for by in range(1, cols):
        total = total + zbox[by - 1].astype(FLOAT)
    zfull[col] = total.astype(BRAIN)
    total = red_split[0].astype(FLOAT)
    for turn in range(1, shards):
        total = total + sbox[turn - 1].astype(FLOAT)
    sfull[...] = total.astype(BRAIN)

    spread = []
    for by in range(1, cols):
        to = (col + by) % cols
        copy = remote(zfull.at[col], zfull.at[col], spread_sems, by - 1, (row, to))
        copy.start()
        spread.append(copy)
    last = []
    for by in range(1, peers):
        to = (row + by) % peers
        copy = remote(sfull, split_all.at[row], split_sems, by - 1, (to, col))
        copy.start()
        last.append(copy)
    split_all[row] = sfull[...]
    for copy in spread:
        copy.wait()
    for by in range(1, peers):
        to = (row + by) % peers
        copy = remote(zfull, shared_all.at[row], shared_sems, by - 1, (to, col))
        copy.start()
        last.append(copy)
    shared_all[row] = zfull[...]
    for copy in last:
        copy.wait()
    for at, rows, lanes, index, lines in shared_plan:
        shared_out[at][rows, lanes] = shared_all[index // cols, index % cols, lines].astype(FLOAT)
    for at, rows, lanes, index, lines in split_plan:
        split_out[at][rows, lanes] = split_all[index, lines].astype(FLOAT)
    for copy in returned:
        copy.wait()


def close(own_part, other_part, stream, d_middle, gain, shared, split):
    peers, cols = lax.axis_size("row"), lax.axis_size("col")
    shards = cols // 2
    own, d_model = stream.shape
    pieces = [value.shape[1] // shards for value in split]

    def widened(value):
        cut = value.reshape(value.shape[0], shards, -1)
        short = -cut.shape[2] % LANES
        return jnp.pad(cut, ((0, 0), (0, 0), (0, short))).reshape(value.shape[0], -1)

    split = [widened(value) if piece % LANES else value for value, piece in zip(split, pieces)]
    shared_sizes = [value.shape for value in shared]
    split_sizes = [value.shape for value in split]
    unit, part = closing_sizes(shared_sizes, split_sizes, peers, cols, shards)
    lines = cols * unit + shards * part
    sems = [
        pltpu.SemaphoreType.DMA((2, count))
        for count in (1, peers - 1, cols - 1, max(shards - 1, 1), cols - 1, peers - 1, peers - 1,
                      cols - 1)
    ]
    result = block_call(
        closing_kernel,
        2,
        [own_part, other_part, stream, d_middle, gain, *shared, *split],
        [((own * cols, d_model // cols), FLOAT)]
        + [(size, FLOAT) for size in shared_sizes]
        + [((rows, columns // shards), FLOAT) for rows, columns in split_sizes],
        [
            pltpu.VMEM((own, d_model), BRAIN),
            pltpu.VMEM((cols, own, d_model // cols), FLOAT),
            pltpu.VMEM((peers, lines, LANES), BRAIN),
            pltpu.VMEM((peers - 1, lines, LANES), BRAIN),
            pltpu.VMEM((cols, unit, LANES), BRAIN),
            pltpu.VMEM((shards, part, LANES), BRAIN),
            pltpu.VMEM((cols - 1, unit, LANES), BRAIN),
            pltpu.VMEM((max(shards - 1, 1), part, LANES), BRAIN),
            pltpu.VMEM((cols, unit, LANES), BRAIN),
            pltpu.VMEM((part, LANES), BRAIN),
            pltpu.VMEM((peers, cols, unit, LANES), BRAIN),
            pltpu.VMEM((peers, part, LANES), BRAIN),
        ]
        + sems,
    )
    split = [value[:, :piece] for value, piece in zip(result[5:9], pieces)]
    return result[0], result[1:5], split


def partner(value):
    peers = lax.axis_size("col")
    return lax.ppermute(value, "col", [(at, at ^ 1) for at in range(peers)])


def from_shard(value, turn):
    peers = lax.axis_size("col")
    return lax.ppermute(value, "col", [((at + 2 * turn) % peers, at) for at in range(peers)])


def to_shard(value, turn):
    peers = lax.axis_size("col")
    return lax.ppermute(value, "col", [(at, (at + 2 * turn) % peers) for at in range(peers)])


def all_shards(value):
    return [value] + [from_shard(value, turn) for turn in range(1, lax.axis_size("col") // 2)]


def after(value, anchor):
    return value if anchor is None else lax.optimization_barrier((value, anchor))[0]


def whole_width(value):
    peers = lax.axis_size("col")
    parts = [value] + [
        lax.ppermute(value, "col", [((at + turn) % peers, at) for at in range(peers)])
        for turn in range(1, peers)
    ]
    stacked = jnp.roll(jnp.stack(parts), lax.axis_index("col"), axis=0)
    return jnp.moveaxis(stacked, 0, -2).reshape(value.shape[:-1] + (-1,))


def to_sequence(value):
    return lax.all_to_all(value, "col", split_axis=0, concat_axis=1, tiled=True)


def from_sequence(value):
    return lax.all_to_all(value, "col", split_axis=1, concat_axis=0, tiled=True)


def both_halves(value):
    return jnp.concatenate([value, partner(value)], axis=0)


def half_share(own, other):
    return own + partner(other.astype(BRAIN)).astype(FLOAT)


def norm_forward(stream, gain):
    scale = lax.rsqrt(jnp.mean(stream * stream, axis=1, keepdims=True) + EPSILON)
    return scale, (stream * scale * gain[None, :]).astype(BRAIN)


def norm_backward(stream, scale, gain, d_normed):
    gained = d_normed * gain[None, :]
    total = jnp.mean(gained * stream, axis=1, keepdims=True)
    return scale * gained - stream * (scale * scale * scale * total)


def masked(value, pick):
    return (value * pick).astype(BRAIN)


def entry(stream, gain):
    scale, normed = norm_forward(stream, gain)
    return scale, both_halves(normed)


def recur_branch(normed_full, inlet, small, ctx):
    pick = ctx["pick"]
    ranks = pick.shape[1]
    width = inlet.shape[1] // 2
    low = nt(normed_full, small["inlet_lower"])
    inner = [masked(low[:, b * ranks : (b + 1) * ranks], pick) for b in range(2)]
    branch = nn(normed_full, inlet)
    lead = branch[:, :width] + nn(inner[0], small["inlet_upper"][0])
    gate = branch[:, width:] + nn(inner[1], small["inlet_upper"][1])
    return lead, gate, inner


def recur_part(stream, lead, gate, outlet, small, ctx):
    pick, offset = ctx["pick"], ctx["offset"]
    own = stream.shape[0]
    rows = 2 * own
    conv, decay, hidden, mixed, state_in = recur_forward(lead, gate, offset, small)
    lowrank = masked(nt(mixed, small["outlet_lower"]), pick)

    def outward(part):
        return nt(mixed[part], outlet) + nn(lowrank[part], small["outlet_upper"])

    middle = stream + half_share(outward(slice(0, own)), outward(slice(own, rows)))
    kept = dict(
        conv=conv, decay=decay, hidden=hidden, state_in=state_in, mixed=mixed, lowrank=lowrank,
        middle=middle,
    )
    return middle, kept


def hidden_part(middle, normed_two_full, wide, small, ctx):
    expand, shrink = wide
    pick = ctx["pick"]
    ranks = pick.shape[1]
    own = middle.shape[0]
    rows = 2 * own
    spread = shrink.shape[1]
    low_two = nt(normed_two_full, small["expand_lower"])
    inner_two = [masked(low_two[:, b * ranks : (b + 1) * ranks], pick) for b in range(2)]
    branch_two = nn(normed_two_full, expand)
    up_gate = branch_two[:, :spread] + nn(inner_two[0], small["expand_upper"][0])
    up_value = branch_two[:, spread:] + nn(inner_two[1], small["expand_upper"][1])
    product = (gelu_tanh(up_gate) * up_value).astype(BRAIN)
    lowrank_two = masked(nt(product, small["shrink_lower"]), pick)

    def downward(part):
        return nt(product[part], shrink) + nn(lowrank_two[part], small["shrink_upper"])

    result = middle + half_share(downward(slice(0, own)), downward(slice(own, rows)))
    kept = dict(
        inner_two=inner_two,
        up_gate=up_gate, up_value=up_value, product=product, lowrank_two=lowrank_two,
    )
    return result, kept


def layer_backward(d_stream, wide, small, gains, kept, ctx):
    inlet, outlet, expand, shrink = wide
    pick, offset = ctx["pick"], ctx["offset"]
    own = d_stream.shape[0]
    rows = 2 * own
    width = outlet.shape[1]
    spread = shrink.shape[1]

    d_out = both_halves(d_stream.astype(BRAIN))
    d_low_two = masked(nt(d_out, small["shrink_upper"]), pick)
    d_product = nn(d_out, shrink) + nn(d_low_two, small["shrink_lower"])
    shrink_upper_grad = tn(kept["lowrank_two"], d_out)
    shrink_lower_grad = tn(d_low_two, kept["product"])
    value, slope = gelu_pair(kept["up_gate"])
    d_branch_two = jnp.concatenate(
        [(slope * kept["up_value"] * d_product).astype(BRAIN), (value * d_product).astype(BRAIN)],
        axis=1,
    )
    d_inner_two = jnp.concatenate(
        [
            masked(nt(d_branch_two[:, b * spread : (b + 1) * spread], small["expand_upper"][b]), pick)
            for b in range(2)
        ],
        axis=1,
    )

    def inward_two(part):
        return nt(d_branch_two[part], expand) + nn(d_inner_two[part], small["expand_lower"])

    d_normed_two = half_share(inward_two(slice(0, own)), inward_two(slice(own, rows)))
    expand_lower_grad = tn(d_inner_two, kept["normed_two_full"])
    expand_upper_grad = jnp.concatenate(
        [
            tn(kept["inner_two"][b], d_branch_two[:, b * spread : (b + 1) * spread])
            for b in range(2)
        ],
        axis=0,
    )
    d_middle = d_stream + norm_backward(kept["middle"], kept["scale_two"], gains[1], d_normed_two)

    d_mid = both_halves(d_middle.astype(BRAIN))
    d_low = masked(nt(d_mid, small["outlet_upper"]), pick)
    d_mixed = nn(d_mid, outlet) + nn(d_low, small["outlet_lower"])
    outlet_upper_grad = tn(kept["lowrank"], d_mid)
    outlet_lower_grad = tn(d_low, kept["mixed"])
    d_branch = recur_backward(d_mixed, kept, offset, small)
    d_inner = jnp.concatenate(
        [
            masked(nt(d_branch[:, b * width : (b + 1) * width], small["inlet_upper"][b]), pick)
            for b in range(2)
        ],
        axis=1,
    )

    def inward(part):
        return nt(d_branch[part], inlet) + nn(d_inner[part], small["inlet_lower"])

    inlet_lower_grad = tn(d_inner, kept["normed_full"])
    inlet_upper_grad = jnp.concatenate(
        [tn(kept["inner"][b], d_branch[:, b * width : (b + 1) * width]) for b in range(2)], axis=0
    )
    shared = (inlet_lower_grad, outlet_upper_grad, expand_lower_grad, shrink_upper_grad)
    split = (inlet_upper_grad, outlet_lower_grad, expand_upper_grad, shrink_lower_grad)
    partial_sums = (inward(slice(0, own)), inward(slice(own, rows)))
    return d_middle, partial_sums, shared, split


def start_sums(shared, split):
    return (
        lax.psum(jnp.concatenate(shared, axis=0).astype(BRAIN), ("row", "col")),
        [
            lax.psum(jnp.concatenate(pair, axis=0).astype(BRAIN), "row")
            for pair in (split[:2], split[2:])
        ],
    )


def end_sums(shared, split, shards, anchor):
    shared = after(shared, anchor).astype(FLOAT)
    totals = []
    for whole in split:
        whole = after(whole, anchor)
        piece = whole.shape[1] // shards
        parts = [whole[:, turn * piece : (turn + 1) * piece] for turn in range(shards)]
        total = parts[0].astype(FLOAT)
        for turn in range(1, shards):
            total = total + to_shard(parts[turn], turn).astype(FLOAT)
        totals.append(total)
    return shared, totals


def local(
    tokens, cotangent, adapter_ids, doc_lengths, norm_gain, inlet_weight, inlet_lower, inlet_upper,
    conv_weight, conv_bias, gate_weight, gate_bias, decay_param, outlet_weight, outlet_lower,
    outlet_upper, expand_weight, expand_lower, expand_upper, shrink_weight, shrink_lower,
    shrink_upper,
):
    row_at, col_at = lax.axis_index("row"), lax.axis_index("col")
    cols = lax.axis_size("col")
    shards = cols // 2
    rows = tokens.shape[0]
    own = rows // cols
    block = 2 * own
    docs = adapter_ids.shape[0]
    adapters, rank = inlet_lower.shape[3:]
    part_width, part_spread = inlet_weight.shape[3], expand_weight.shape[3]
    d_model = inlet_lower.shape[1]

    parity = (col_at % 2).astype(jnp.int32)
    ends = jnp.cumsum(doc_lengths)
    starts = ends - doc_lengths
    ordered = row_at * rows + (col_at // 2) * block + jnp.arange(block, dtype=jnp.int32)
    inside = (ordered[:, None] >= starts[None, :]) & (ordered[:, None] < ends[None, :])
    offset = (ordered - jnp.sum(jnp.where(inside, starts[None, :], 0), axis=1))[:, None]
    halves = (parity * own, own - parity * own)
    at_home = jnp.concatenate(
        [ordered[0] + begin + jnp.arange(own, dtype=jnp.int32) for begin in halves]
    )
    within = (at_home[:, None] >= starts[None, :]) & (at_home[:, None] < ends[None, :])
    pick = jnp.repeat(within.astype(FLOAT), rank, axis=1)
    ctx = dict(pick=pick, offset=offset)

    stream = to_sequence(tokens).astype(FLOAT)
    gains = whole_width(norm_gain)

    def by_doc(factor, axis):
        return jnp.concatenate(
            [lax.dynamic_slice_in_dim(factor, adapter_ids[at], 1, axis) for at in range(docs)], axis
        )

    def lower_t(factor):
        return by_doc(jnp.moveaxis(factor, 1, -1), factor.ndim - 3)

    def upper_t(factor):
        return by_doc(factor, factor.ndim - 3)

    ranks = docs * rank
    lows = dict(
        inlet_lower=lower_t(inlet_lower).reshape(LAYERS, 2 * ranks, d_model),
        outlet_upper=upper_t(outlet_upper).reshape(LAYERS, ranks, d_model),
        expand_lower=lower_t(expand_lower).reshape(LAYERS, 2 * ranks, d_model),
        shrink_upper=upper_t(shrink_upper).reshape(LAYERS, ranks, d_model),
    )
    narrow_own = jnp.concatenate(
        [
            upper_t(inlet_upper).reshape(LAYERS, 2 * ranks, part_width),
            lower_t(outlet_lower).reshape(LAYERS, ranks, part_width),
        ],
        axis=1,
    )
    broad_own = jnp.concatenate(
        [
            upper_t(expand_upper).reshape(LAYERS, 2 * ranks, part_spread),
            lower_t(shrink_lower).reshape(LAYERS, ranks, part_spread),
        ],
        axis=1,
    )
    vectors_own = jnp.concatenate(
        [conv_weight, gate_bias, conv_bias[:, None], decay_param[:, None]], axis=1
    )

    def start(pair, single, anchor):
        return all_shards(after(jnp.concatenate([pair[:, 0], pair[:, 1], single], axis=1), anchor))

    def gathered(parts, anchor):
        piece = parts[0].shape[1] // 3
        parts = [parts[0]] + [after(part, anchor) for part in parts[1:]]
        columns = [part[:, at * piece : (at + 1) * piece] for at in range(3) for part in parts]
        whole = lax.all_gather(jnp.concatenate(columns, axis=1), "row", axis=0, tiled=True)
        cut = 2 * shards * piece
        return whole[:, :cut], whole[:, cut:]

    def joined(parts, anchor):
        return jnp.concatenate([parts[0]] + [after(part, anchor) for part in parts[1:]], axis=1)

    def start_recur_small(layer, anchor):
        return [
            all_shards(after(value, anchor))
            for value in (narrow_own[layer], vectors_own[layer], gate_weight[layer])
        ]

    def recur_small(layer, parts, anchor):
        narrow, vectors, gates = (joined(part, anchor) for part in parts)
        return dict(
            inlet_lower=lows["inlet_lower"][layer],
            inlet_upper=narrow[: 2 * ranks].reshape(2, ranks, -1),
            outlet_lower=narrow[2 * ranks :],
            outlet_upper=lows["outlet_upper"][layer],
            conv_weight=vectors[:CONV],
            gate_bias=vectors[CONV : CONV + 2],
            conv_bias=vectors[CONV + 2 : CONV + 3],
            soft=jax.nn.softplus(vectors[CONV + 3 : CONV + 4]),
            gate_weight=gates,
        )

    def hidden_small(layer, parts, anchor):
        broad = joined(parts, anchor)
        return dict(
            expand_lower=lows["expand_lower"][layer],
            expand_upper=broad[: 2 * ranks].reshape(2, ranks, -1),
            shrink_lower=broad[2 * ranks :],
            shrink_upper=lows["shrink_upper"][layer],
        )

    outputs, saved, wides, smalls = [], [], [], []
    recur_pack = start(inlet_weight[0], outlet_weight[0], None)
    recur_bits = start_recur_small(0, recur_pack[-1])
    hidden_pack = start(expand_weight[0], shrink_weight[0], recur_pack[-1])
    wide_one = gathered(recur_pack, None)
    for layer in range(LAYERS):
        more_layers = layer + 1 < LAYERS
        scale_one, normed_full = entry(stream, gains[layer][0])
        small_one = recur_small(layer, recur_bits, normed_full)
        lead, gate, inner = recur_branch(normed_full, wide_one[0], small_one, ctx)
        if layer == 0:
            wide_two = gathered(hidden_pack, lead)
        hidden_bits = all_shards(after(broad_own[layer], lead))
        if more_layers:
            recur_pack = start(inlet_weight[layer + 1], outlet_weight[layer + 1], lead)
        middle, kept = recur_part(stream, lead, gate, wide_one[1], small_one, ctx)
        kept.update(
            stream=stream, scale_one=scale_one, normed_full=normed_full, inner=inner, gate=gate
        )
        if more_layers:
            wide_next = gathered(recur_pack, middle)
            recur_bits = start_recur_small(layer + 1, middle)
            hidden_pack = start(expand_weight[layer + 1], shrink_weight[layer + 1], middle)
        scale_two, normed_two_full = entry(middle, gains[layer][1])
        small_two = hidden_small(layer, hidden_bits, normed_two_full)
        stream, more = hidden_part(middle, normed_two_full, wide_two, small_two, ctx)
        more.update(scale_two=scale_two, normed_two_full=normed_two_full)
        if more_layers:
            wide_two_next = gathered(hidden_pack, more["product"])
        outputs.append(from_sequence(stream.astype(BRAIN)))
        saved.append({**kept, **more})
        wides.append(wide_one + wide_two)
        smalls.append({**small_one, **small_two})
        if more_layers:
            wide_one, wide_two = wide_next, wide_two_next
    d_stream = to_sequence(cotangent).astype(FLOAT)
    shared, narrow, broad = [None] * LAYERS, [None] * LAYERS, [None] * LAYERS
    started = {}
    for layer in reversed(range(LAYERS)):
        kept = saved[layer]
        d_middle, parts, shared_parts, split_parts = layer_backward(
            d_stream, wides[layer], smalls[layer], gains[layer], kept, ctx
        )
        if layer:
            d_normed = half_share(*parts)
            d_stream = d_middle + norm_backward(
                kept["stream"], kept["scale_one"], gains[layer][0], d_normed
            )
            started[layer] = start_sums(shared_parts, split_parts)
        else:
            tokens_grad, shared_parts, split_parts = close(
                parts[0], parts[1].astype(BRAIN), kept["stream"], d_middle, gains[layer][:1],
                shared_parts, split_parts,
            )
            shared[layer] = jnp.concatenate(shared_parts, axis=0)
            narrow[layer] = jnp.concatenate(split_parts[:2], axis=0)
            broad[layer] = jnp.concatenate(split_parts[2:], axis=0)
    for layer, (whole, pairs) in started.items():
        shared[layer], (narrow[layer], broad[layer]) = end_sums(whole, pairs, shards, tokens_grad)
    shared, narrow, broad = jnp.stack(shared), jnp.stack(narrow), jnp.stack(broad)
    spread_out = (adapter_ids[None, :] == jnp.arange(adapters, dtype=jnp.int32)[:, None])

    def by_adapter(grad, count):
        grad = grad.reshape(LAYERS, count, docs, rank, -1)
        total = 0.0
        for doc in range(docs):
            total = total + jnp.where(
                spread_out[None, None, :, doc, None, None], grad[:, :, doc][:, :, None], 0.0
            )
        return total

    def lower_out(grad, count):
        grad = by_adapter(grad, count)
        if count == 1:
            grad = grad[:, 0]
        return jnp.moveaxis(grad, -1, 1)

    return (
        jnp.stack(outputs, axis=0),
        tokens_grad,
        lower_out(shared[:, : 2 * ranks], 2),
        by_adapter(narrow[:, : 2 * ranks], 2),
        lower_out(narrow[:, 2 * ranks :], 1),
        by_adapter(shared[:, 2 * ranks : 3 * ranks], 1)[:, 0],
        lower_out(shared[:, 3 * ranks : 5 * ranks], 2),
        by_adapter(broad[:, : 2 * ranks], 2),
        lower_out(broad[:, 2 * ranks :], 1),
        by_adapter(shared[:, 5 * ranks :], 1)[:, 0],
    )


def solution(mesh):
    return jax.shard_map(
        local,
        mesh=mesh,
        in_specs=(
            P("row", "col"),
            P("row", "col"),
            P(),
            P(),
            P(None, None, "col"),
            P(None, "row", None, "col"),
            P(),
            P(None, None, None, None, "col"),
            P(None, None, "col"),
            P(None, "col"),
            P(None, None, "col", None, None),
            P(None, None, "col"),
            P(None, "col"),
            P(None, "row", "col"),
            P(None, "col", None, None),
            P(),
            P(None, "row", None, "col"),
            P(),
            P(None, None, None, None, "col"),
            P(None, "row", "col"),
            P(None, "col", None, None),
            P(),
        ),
        out_specs=(
            P(None, "row", "col"),
            P("row", "col"),
            P(),
            P(None, None, None, None, "col"),
            P(None, "col", None, None),
            P(),
            P(),
            P(None, None, None, None, "col"),
            P(None, "col", None, None),
            P(),
        ),
        check_vma=False,
    )
```

```python
from functools import partial

import jax
import jax.numpy as jnp
from jax import lax
from jax.experimental import pallas as pl
from jax.experimental.pallas import tpu as pltpu
from jax.sharding import PartitionSpec as P

HS = 256
CONV = 4
LAYERS = 2
SEGS = 8

EPSILON = 1e-06
FLOAT = jnp.float32
BRAIN = jnp.bfloat16
VMEM_BYTES = 48 * 1024 * 1024
CURVE = 0.7978845608028654
CUBIC = 0.044715
LANES = 128
SLABS = HS // LANES
MESH = pl.DeviceIdType.MESH


def nn(left, right):
    return lax.dot_general(left, right, (((1,), (0,)), ((), ())), preferred_element_type=FLOAT)


def nt(left, right):
    return lax.dot_general(left, right, (((1,), (1,)), ((), ())), preferred_element_type=FLOAT)


def tn(left, right):
    return lax.dot_general(left, right, (((0,), (0,)), ((), ())), preferred_element_type=FLOAT)


def gelu_tanh(value):
    return 0.5 * value * (1.0 + jnp.tanh(CURVE * (value + CUBIC * value * value * value)))


def gelu_pair(value):
    square = value * value
    bend = jnp.tanh(CURVE * value * (1.0 + CUBIC * square))
    half = 0.5 * (1.0 + bend)
    slope = half + 0.5 * value * (1.0 - bend * bend) * CURVE * (1.0 + 3.0 * CUBIC * square)
    return value * half, slope


def one_less_square(twice, square):
    series = -twice * (
        1.0 + twice * (0.5 + twice * (1.0 / 6.0 + twice * (1.0 / 24.0 + twice * (1.0 / 120.0))))
    )
    return jnp.where(twice > -0.1, series, 1.0 - square)


def gate_values(conv, gate_w, gate_b, soft):
    rate = jax.nn.sigmoid(nn(conv, gate_w[0]) + gate_b[0:1])
    inward = jax.nn.sigmoid(nn(conv, gate_w[1]) + gate_b[1:2])
    log_decay = (-8.0 * soft) * rate
    raw = jnp.exp(log_decay)
    gap = one_less_square(2.0 * log_decay, raw * raw)
    return rate, inward, raw, gap


def chain(axis_row="row", axis_col="col"):
    blocks_in_row = lax.axis_size(axis_col) // 2
    blocks = lax.axis_size(axis_row) * blocks_in_row
    col = lax.axis_index(axis_col)
    side = col % 2
    here = lax.axis_index(axis_row) * blocks_in_row + col // 2

    def device(by):
        block = (here + by + blocks) % blocks
        return (block // blocks_in_row, (block % blocks_in_row) * 2 + side)

    return blocks, blocks_in_row, here, side, device


def greet(blocks, device):
    barrier = pltpu.get_barrier_semaphore()
    for by in range(1, blocks):
        pl.semaphore_signal(barrier, inc=1, device_id=device(by), device_id_type=MESH)
    pl.semaphore_wait(barrier, blocks - 1)


def share_totals(blocks, device, direction, totals, inbox, send_sems, recv_sems):
    copies = [
        pltpu.make_async_remote_copy(
            src_ref=totals,
            dst_ref=inbox.at[by - 1],
            send_sem=send_sems.at[by - 1],
            recv_sem=recv_sems.at[by - 1],
            device_id=device(direction * by),
            device_id_type=MESH,
        )
        for by in range(1, blocks)
    ]
    for copy in copies:
        copy.start()
    for copy in copies:
        copy.wait()


def folded(blocks, shards, ahead, direction, inbox):
    slabs = inbox.shape[1] // 2
    piece = slabs // shards
    state = jnp.zeros((slabs, LANES), FLOAT)
    for by in reversed(range(1, blocks)):
        turn = (direction * by) % shards * piece
        cum, add = (
            jnp.concatenate([part[turn:], part[:turn]], axis=0) if turn else part
            for part in (inbox[by - 1, 0:slabs], inbox[by - 1, slabs : 2 * slabs])
        )
        state = jnp.where(ahead >= by, cum * state + add, state)
    return state


def forward_kernel(
    lead, gate, offset, conv_w, conv_b, gate_w, gate_b, soft,
    conv_out, decay_out, hidden_out, mixed_out, carry_out,
    ext, drive, state_all, cum_all, seg, totals, halo, inbox,
    halo_sems, send_sems, recv_sems,
):
    rows, width = lead.shape
    heads = width // HS
    half = rows // 2
    span = rows // SEGS
    slabs = width // LANES
    blocks, shards, here, side, device = chain()
    start = pl.multiple_of(side * half, half)
    other = pl.multiple_of(half - side * half, half)
    greet(blocks, device)
    rim = pltpu.make_async_remote_copy(
        src_ref=lead.at[pl.ds(pl.multiple_of(other + half - 8, 8), 8)],
        dst_ref=halo,
        send_sem=halo_sems.at[0],
        recv_sem=halo_sems.at[1],
        device_id=device(1),
        device_id_type=MESH,
    )
    rim.start()
    rim.wait()

    def run_head(head, nothing):
        at = pl.ds(pl.multiple_of(head * HS, HS), HS)
        there = (head + heads // shards) % heads
        ext[0:8] = halo[:, pl.ds(pl.multiple_of(there * HS, HS), HS)]
        ext[8 : 8 + half] = lead[pl.ds(start, half), at]
        ext[8 + half : 8 + rows] = lead[pl.ds(other, half), at]
        place = offset[...]
        total = conv_b[:, at] + conv_w[0:1, at] * ext[8 : 8 + rows]
        for step in range(1, CONV):
            valid = (place >= step).astype(FLOAT)
            total = total + conv_w[step : step + 1, at] * ext[8 - step : 8 - step + rows] * valid
        conv = total.astype(BRAIN)
        conv_out[:, at] = conv
        rate, inward, raw, gap = gate_values(
            conv, (gate_w[0, head], gate_w[1, head]), gate_b[:, at], soft[:, at]
        )
        first = (place == 0).astype(FLOAT)
        keep = 1.0 - first
        decay = raw * keep
        pushed = (keep * jnp.sqrt(gap) + first) * inward * conv.astype(FLOAT)
        for slab in range(SLABS):
            decay_out[head * SLABS + slab] = decay[:, slab * LANES : (slab + 1) * LANES]
            drive[slab] = pushed[:, slab * LANES : (slab + 1) * LANES]

        def advance(step, carried):
            where = pl.ds(step, SEGS, stride=span)
            after = []
            for slab, (state, cum) in enumerate(carried):
                rates = decay_out[head * SLABS + slab, where, :]
                state = rates * state + drive[slab, where, :]
                cum = rates * cum
                state_all[head * SLABS + slab, where, :] = state
                cum_all[head * SLABS + slab, where, :] = cum
                after.append((state, cum))
            return tuple(after)

        fresh = (jnp.zeros((SEGS, LANES), FLOAT), jnp.ones((SEGS, LANES), FLOAT))
        ends = lax.fori_loop(0, span, advance, (fresh,) * SLABS, unroll=8)
        for slab, (state, cum) in enumerate(ends):
            run_state = jnp.zeros((1, LANES), FLOAT)
            run_cum = jnp.ones((1, LANES), FLOAT)
            at_slab = head * SLABS + slab
            for part in range(SEGS):
                seg[at_slab, part : part + 1] = run_state
                seg[at_slab, SEGS + part : SEGS + part + 1] = run_cum
                run_state = cum[part : part + 1] * run_state + state[part : part + 1]
                run_cum = cum[part : part + 1] * run_cum
            totals[pl.ds(at_slab, 1)] = run_cum
            totals[pl.ds(slabs + at_slab, 1)] = run_state
        return nothing

    lax.fori_loop(0, heads, run_head, 0)
    share_totals(blocks, device, 1, totals, inbox, send_sems, recv_sems)
    carry_out[...] = folded(blocks, shards, here, 1, inbox)

    def mix_slab(slab, nothing):
        at = pl.ds(pl.multiple_of(slab * LANES, LANES), LANES)
        entering = seg[slab, 0:SEGS] + seg[slab, SEGS : 2 * SEGS] * carry_out[pl.ds(slab, 1)]
        for part in range(SEGS):
            lines = slice(part * span, (part + 1) * span)
            hidden_out[slab, lines] = (
                state_all[slab, lines] + cum_all[slab, lines] * entering[part : part + 1]
            )
        for place, lines in ((start, slice(0, half)), (other, slice(half, rows))):
            mixed_out[pl.ds(place, half), at] = (
                hidden_out[slab, lines] * gelu_tanh(gate[pl.ds(place, half), at])
            ).astype(BRAIN)
        return nothing

    lax.fori_loop(0, slabs, mix_slab, 0)


def backward_kernel(
    grad, gate, hidden, decay, carry, conv, offset, conv_w, gate_w, gate_b, soft,
    branch_grad,
    ext, prior, grads, chain_decay, local_all, reach_all, seg, totals, arriving, heads_out,
    heads_in, tails, inbox, halo_sems, send_sems, recv_sems,
):
    rows, width = grad.shape
    heads = width // HS
    half = rows // 2
    span = rows // SEGS
    slabs = width // LANES
    blocks, shards, here, side, device = chain()
    start = pl.multiple_of(side * half, half)
    other = pl.multiple_of(half - side * half, half)
    greet(blocks, device)

    def run_slab(slab, nothing):
        at = pl.ds(pl.multiple_of(slab * LANES, LANES), LANES)
        gate_at = pl.ds(pl.multiple_of(width + slab * LANES, LANES), LANES)
        for place, lines in ((start, slice(0, half)), (other, slice(half, rows))):
            value, slope = gelu_pair(gate[pl.ds(place, half), at])
            coming = grad[pl.ds(place, half), at]
            grads[lines] = coming * value
            branch_grad[pl.ds(place, half), gate_at] = (
                coming * hidden[slab, lines] * slope
            ).astype(BRAIN)
        chain_decay[0:rows] = decay[slab]
        chain_decay[rows : rows + 8] = jnp.ones((8, LANES), FLOAT)

        def retreat(turn, carried):
            state, cum = carried
            step = span - 1 - turn
            where = pl.ds(step, SEGS, stride=span)
            rates = chain_decay[pl.ds(step + 1, SEGS, stride=span), :]
            state = rates * state + grads[where, :]
            cum = rates * cum
            local_all[slab, where, :] = state
            reach_all[slab, where, :] = cum
            return state, cum

        fresh = (jnp.zeros((SEGS, LANES), FLOAT), jnp.ones((SEGS, LANES), FLOAT))
        state, cum = lax.fori_loop(0, span, retreat, fresh, unroll=8)
        run_state = jnp.zeros((1, LANES), FLOAT)
        run_cum = jnp.ones((1, LANES), FLOAT)
        for part in reversed(range(SEGS)):
            seg[slab, part : part + 1] = run_state
            seg[slab, SEGS + part : SEGS + part + 1] = run_cum
            run_state = cum[part : part + 1] * run_state + state[part : part + 1]
            run_cum = cum[part : part + 1] * run_cum
        opening = chain_decay[0:1]
        totals[pl.ds(slab, 1)] = run_cum * opening
        totals[pl.ds(slabs + slab, 1)] = run_state * opening
        return nothing

    lax.fori_loop(0, slabs, run_slab, 0)
    share_totals(blocks, device, -1, totals, inbox, send_sems, recv_sems)
    arriving[...] = folded(blocks, shards, blocks - 1 - here, -1, inbox)

    def run_head(head, nothing):
        at = pl.ds(pl.multiple_of(head * HS, HS), HS)
        for slab in range(SLABS):
            slot = head * SLABS + slab
            lanes = slice(slab * LANES, (slab + 1) * LANES)
            entering = seg[slot, 0:SEGS] + seg[slot, SEGS : 2 * SEGS] * arriving[pl.ds(slot, 1)]
            for part in range(SEGS):
                lines = slice(part * span, (part + 1) * span)
                ext[lines, lanes] = (
                    local_all[slot, lines] + reach_all[slot, lines] * entering[part : part + 1]
                )
            prior[7:8, lanes] = carry[pl.ds(slot, 1)]
            prior[8 : 8 + rows, lanes] = hidden[slot]
        carried = ext[0:rows]
        before = prior[7 : 7 + rows]
        low = conv[:, at]
        value = low.astype(FLOAT)
        place = offset[...]
        first = (place == 0).astype(FLOAT)
        keep = 1.0 - first
        softness = soft[:, at]
        weights = (gate_w[0, head], gate_w[1, head])
        rate, inward, raw, gap = gate_values(low, weights, gate_b[:, at], softness)
        root = jnp.sqrt(gap)
        scale = keep * root + first
        pushed = carried * inward
        log_grad = keep * raw * (carried * before - pushed * value * (raw / root))
        rate_grad = ((-8.0 * softness) * log_grad * rate * (1.0 - rate)).astype(BRAIN)
        scaled = carried * scale
        input_grad = (scaled * value * inward * (1.0 - inward)).astype(BRAIN)
        conv_grad = scaled * inward + nt(rate_grad, weights[0]) + nt(input_grad, weights[1])
        ext[rows : rows + 8] = jnp.zeros((8, HS), FLOAT)
        total = conv_w[0:1, at] * conv_grad
        head_sum = jnp.zeros((8, HS), FLOAT)
        lines = lax.broadcasted_iota(jnp.int32, (8, 1), 0)
        for step in range(1, CONV):
            term = conv_w[step : step + 1, at] * conv_grad * (place >= step).astype(FLOAT)
            ext[0:rows] = term
            total = total + ext[step : step + rows]
            moved = pltpu.roll(term[0:8], 8 - step, 0)
            head_sum = head_sum + jnp.where(lines >= 8 - step, moved, 0.0)
        heads_out[:, at] = head_sum
        tails[:, at] = total[rows - 8 : rows]
        branch_grad[pl.ds(start, half), at] = total[0:half].astype(BRAIN)
        branch_grad[pl.ds(other, half), at] = total[half:rows].astype(BRAIN)
        return nothing

    lax.fori_loop(0, heads, run_head, 0)
    rim = pltpu.make_async_remote_copy(
        src_ref=heads_out,
        dst_ref=heads_in,
        send_sem=halo_sems.at[0],
        recv_sem=halo_sems.at[1],
        device_id=device(-1),
        device_id_type=MESH,
    )
    rim.start()
    rim.wait()
    followed = jnp.where(here < blocks - 1, 1.0, 0.0)
    for head in range(heads):
        at = slice(head * HS, (head + 1) * HS)
        there = (head - heads // shards) % heads
        whole = tails[:, at] + heads_in[:, there * HS : (there + 1) * HS] * followed
        kept = branch_grad[pl.ds(pl.multiple_of(other + half - 16, 16), 16), at]
        tails_pair = jnp.concatenate([kept[0:8], whole.astype(BRAIN)], axis=0)
        branch_grad[pl.ds(pl.multiple_of(other + half - 16, 16), 16), at] = tails_pair


def lasting(microseconds):
    return pl.CostEstimate(
        flops=int(microseconds * 1.1e9), bytes_accessed=int(microseconds * 3e6), transcendentals=0
    )


def block_call(kernel, ident, operands, outs, scratch, microseconds, anywhere=0):
    whole, open_place = pl.BlockSpec(memory_space=pltpu.VMEM), pl.BlockSpec(memory_space=pl.ANY)
    return pl.pallas_call(
        kernel,
        out_shape=[jax.ShapeDtypeStruct(*out) for out in outs],
        in_specs=[whole] * (len(operands) - anywhere) + [open_place] * anywhere,
        out_specs=[whole] * (len(outs) - anywhere) + [open_place] * anywhere,
        scratch_shapes=scratch,
        cost_estimate=lasting(microseconds),
        compiler_params=pltpu.CompilerParams(
            vmem_limit_bytes=VMEM_BYTES, collective_id=ident, has_side_effects=True
        ),
    )(*operands)


def message_scratch(width):
    others = lax.axis_size("row") * lax.axis_size("col") // 2 - 1
    slabs = width // LANES
    return [
        pltpu.VMEM((others, 2 * slabs, LANES), FLOAT),
        pltpu.SemaphoreType.DMA((2,)),
        pltpu.SemaphoreType.DMA((others,)),
        pltpu.SemaphoreType.DMA((others,)),
    ]


def recur_forward(lead, gate, offset, small):
    rows, width = lead.shape
    slabs = width // LANES
    stack = (slabs, rows, LANES)
    return block_call(
        forward_kernel,
        0,
        [lead, gate, offset, small["conv_weight"], small["conv_bias"], small["gate_weight"],
         small["gate_bias"], small["soft"]],
        [((rows, width), BRAIN), (stack, FLOAT), (stack, FLOAT), ((rows, width), BRAIN),
         ((slabs, LANES), FLOAT)],
        [
            pltpu.VMEM((rows + 8, HS), FLOAT),
            pltpu.VMEM((SLABS, rows, LANES), FLOAT),
            pltpu.VMEM(stack, FLOAT),
            pltpu.VMEM(stack, FLOAT),
            pltpu.VMEM((slabs, 2 * SEGS, LANES), FLOAT),
            pltpu.VMEM((2 * slabs, LANES), FLOAT),
            pltpu.VMEM((8, width), FLOAT),
        ]
        + message_scratch(width),
        27,
    )


def recur_backward(grad, kept, offset, small):
    rows, width = grad.shape
    slabs = width // LANES
    stack = (slabs, rows, LANES)
    return block_call(
        backward_kernel,
        1,
        [grad, kept["gate"], kept["hidden"], kept["decay"], kept["state_in"], kept["conv"], offset,
         small["conv_weight"], small["gate_weight"], small["gate_bias"], small["soft"]],
        [((rows, 2 * width), BRAIN)],
        [
            pltpu.VMEM((rows + 8, HS), FLOAT),
            pltpu.VMEM((rows + 8, HS), FLOAT),
            pltpu.VMEM((rows, LANES), FLOAT),
            pltpu.VMEM((rows + 8, LANES), FLOAT),
            pltpu.VMEM(stack, FLOAT),
            pltpu.VMEM(stack, FLOAT),
            pltpu.VMEM((slabs, 2 * SEGS, LANES), FLOAT),
            pltpu.VMEM((2 * slabs, LANES), FLOAT),
            pltpu.VMEM((slabs, LANES), FLOAT),
            pltpu.VMEM((8, width), FLOAT),
            pltpu.VMEM((8, width), FLOAT),
            pltpu.VMEM((8, width), FLOAT),
        ]
        + message_scratch(width),
        30,
    )[0]


def line_plan(pieces, unit):
    plan, line = [], 0
    for at, (rows, columns) in enumerate(pieces):
        for begin in range(0, columns, LANES):
            done = 0
            while done < rows:
                index, inner = divmod(line, unit)
                count = min(rows - done, unit - inner)
                plan.append(
                    (at, slice(done, done + count), slice(begin, begin + LANES), index,
                     slice(inner, inner + count))
                )
                done += count
                line += count
    return plan


def closing_sizes(shared, split, peers, cols, shards):
    shared_lines = sum(rows * columns for rows, columns in shared) // LANES
    split_lines = sum(rows * columns for rows, columns in split) // LANES // shards
    unit = -(-shared_lines // (peers * cols * 16)) * 16
    part = -(-split_lines // (peers * 16)) * 16
    return unit, part


def remote(source, target, sems, slot, device):
    return pltpu.make_async_remote_copy(
        src_ref=source,
        dst_ref=target,
        send_sem=sems.at[0, slot],
        recv_sem=sems.at[1, slot],
        device_id=device,
        device_id_type=MESH,
    )


def closing_kernel(count, *refs):
    own_part, other_part, stream, d_middle, gain = refs[:5]
    shared, split = refs[5 : 5 + count], refs[5 + count : 5 + 2 * count]
    tokens_out, *refs = refs[5 + 2 * count :]
    shared_out, split_out = refs[:count], refs[count : 2 * count]
    (
        received, outgoing, homing, flat, beside_in, both, inbox, red, red_split, zbox, sbox, zfull,
        sfull, shared_all, split_all, pair_sems, beside_sems, row_sems, col_sems, turn_sems,
        spread_sems, shared_sems, split_sems, token_sems,
    ) = refs[2 * count :]
    peers, cols = lax.axis_size("row"), lax.axis_size("col")
    shards = cols // 2
    row, col = lax.axis_index("row"), lax.axis_index("col")
    own, d_model = stream.shape
    piece = d_model // cols
    unit, part = zbox.shape[1], sbox.shape[1]
    shared_lines = cols * unit

    side, place, places = row % 2, row // 2, peers // 2
    beside = (row + 1 - 2 * side, col)

    def along(by):
        return (((place + by) % places) * 2 + side, col)

    barrier = pltpu.get_barrier_semaphore()
    greeted = [beside]
    greeted += [along(by) for by in range(1, places)]
    greeted += [(row, (col + by) % cols) for by in range(1, cols)]
    for to in greeted:
        pl.semaphore_signal(barrier, inc=1, device_id=to, device_id_type=MESH)

    sizes = [value.shape for value in shared]
    shared_plan = line_plan(sizes, unit)
    thin = [(value.shape[0], value.shape[1] // shards) for value in split]
    split_plan = line_plan(thin, part)
    flat[...] = jnp.zeros(flat.shape, BRAIN)
    for at, rows, lanes, index, lines in shared_plan:
        begin, owner = index % cols * unit, index // cols
        flat[owner % 2, owner // 2, begin + lines.start : begin + lines.stop] = shared[at][
            rows, lanes
        ].astype(BRAIN)
    for turn in range(shards):
        for at, rows, lanes, index, lines in split_plan:
            begin = shared_lines + turn * part
            skip = turn * thin[at][1]
            flat[index % 2, index // 2, begin + lines.start : begin + lines.stop] = split[at][
                rows, skip + lanes.start : skip + lanes.stop
            ].astype(BRAIN)
    pl.semaphore_wait(barrier, len(greeted))

    paired = remote(flat.at[1 - side], beside_in, beside_sems, 0, beside)
    paired.start()
    pair = remote(other_part, received, pair_sems, 0, (row, col + 1 - 2 * (col % 2)))
    pair.start()
    paired.wait()

    def add_pair(at, nothing):
        both[at] = (flat[side, at].astype(FLOAT) + beside_in[at].astype(FLOAT)).astype(BRAIN)
        return nothing

    lax.fori_loop(0, places, add_pair, 0)
    scattered = []
    for by in range(1, places):
        to = (place + by) % places
        copy = remote(both.at[to], inbox.at[by - 1], row_sems, by - 1, along(by))
        copy.start()
        scattered.append(copy)
    pair.wait()

    def norm_rows(at, nothing):
        lines = pl.ds(pl.multiple_of(at * 16, 16), 16)
        value = stream[lines]
        scale = lax.rsqrt(jnp.mean(value * value, axis=1, keepdims=True) + EPSILON)
        gained = (own_part[lines] + received[lines].astype(FLOAT)) * gain[...]
        total = jnp.mean(gained * value, axis=1, keepdims=True)
        result = d_middle[lines] + scale * gained - value * (scale * scale * scale * total)
        for to in range(cols):
            outgoing[to, lines] = result[:, to * piece : (to + 1) * piece].astype(BRAIN)
        return nothing

    lax.fori_loop(0, own // 16, norm_rows, 0)
    for copy in scattered:
        copy.wait()
    total = both[place].astype(FLOAT)
    for by in range(1, places):
        total = total + inbox[by - 1].astype(FLOAT)
    for at in range(cols):
        red[at] = total[at * unit : (at + 1) * unit].astype(BRAIN)
    for turn in range(shards):
        begin = shared_lines + turn * part
        red_split[turn] = total[begin : begin + part].astype(BRAIN)

    copies = []
    for by in range(1, cols):
        to = (col + by) % cols
        copies.append(remote(red.at[to], zbox.at[by - 1], col_sems, by - 1, (row, to)))
    for turn in range(1, shards):
        to = (col + 2 * turn) % cols
        copies.append(remote(red_split.at[turn], sbox.at[turn - 1], turn_sems, turn - 1, (row, to)))
    for copy in copies:
        copy.start()
    for copy in copies:
        copy.wait()
    total = red[col].astype(FLOAT)
    for by in range(1, cols):
        total = total + zbox[by - 1].astype(FLOAT)
    zfull[col] = total.astype(BRAIN)
    total = red_split[0].astype(FLOAT)
    for turn in range(1, shards):
        total = total + sbox[turn - 1].astype(FLOAT)
    sfull[...] = total.astype(BRAIN)

    spread = []
    for by in range(1, cols):
        to = (col + by) % cols
        copy = remote(zfull.at[col], zfull.at[col], spread_sems, by - 1, (row, to))
        copy.start()
        spread.append(copy)
    last = []
    for by in range(1, places):
        copy = remote(sfull, split_all.at[side, place], split_sems, by - 1, along(by))
        copy.start()
        last.append(copy)
    split_all[side, place] = sfull[...]
    for copy in spread:
        copy.wait()
    for by in range(1, places):
        copy = remote(zfull, shared_all.at[side, place], shared_sems, by - 1, along(by))
        copy.start()
        last.append(copy)
    shared_all[side, place] = zfull[...]
    returned = []
    for by in range(1, cols):
        to = (col + by) % cols
        copy = remote(outgoing.at[to], homing.at[col], token_sems, by - 1, (row, to))
        copy.start()
        returned.append(copy)
    homing[col] = outgoing[col]
    for copy in last:
        copy.wait()
    lanes_over = [
        remote(split_all.at[side], split_all.at[side], beside_sems, 1, beside),
        remote(shared_all.at[side], shared_all.at[side], beside_sems, 2, beside),
    ]
    for copy in lanes_over:
        copy.start()
    for copy in lanes_over:
        copy.wait()
    for at, rows, lanes, index, lines in shared_plan:
        owner = index // cols
        shared_out[at][rows, lanes] = shared_all[
            owner % 2, owner // 2, index % cols, lines
        ].astype(FLOAT)
    for at, rows, lanes, index, lines in split_plan:
        split_out[at][rows, lanes] = split_all[index % 2, index // 2, lines].astype(FLOAT)
    for copy in returned:
        copy.wait()
    for at in range(cols):
        tokens_out[at * own : (at + 1) * own] = homing[at].astype(FLOAT)


def close(own_part, other_part, stream, d_middle, gain, shared, split):
    peers, cols = lax.axis_size("row"), lax.axis_size("col")
    shards = cols // 2
    own, d_model = stream.shape
    pieces = [value.shape[1] // shards for value in split]

    def widened(value):
        cut = value.reshape(value.shape[0], shards, -1)
        short = -cut.shape[2] % LANES
        return jnp.pad(cut, ((0, 0), (0, 0), (0, short))).reshape(value.shape[0], -1)

    split = [widened(value) if piece % LANES else value for value, piece in zip(split, pieces)]
    shared_sizes = [value.shape for value in shared]
    split_sizes = [value.shape for value in split]
    places = peers // 2
    unit, part = closing_sizes(shared_sizes, split_sizes, peers, cols, shards)
    lines = cols * unit + shards * part
    sems = [
        pltpu.SemaphoreType.DMA((2, count))
        for count in (1, 3, places - 1, cols - 1, max(shards - 1, 1), cols - 1, places - 1,
                      places - 1, cols - 1)
    ]
    result = block_call(
        partial(closing_kernel, len(shared)),
        2,
        [own_part, other_part, stream, d_middle, gain, *shared, *split],
        [((own * cols, d_model // cols), FLOAT)]
        + [(size, FLOAT) for size in shared_sizes]
        + [((rows, columns // shards), FLOAT) for rows, columns in split_sizes],
        [
            pltpu.VMEM((own, d_model), BRAIN),
            pltpu.VMEM((cols, own, d_model // cols), BRAIN),
            pltpu.VMEM((cols, own, d_model // cols), BRAIN),
            pltpu.VMEM((2, places, lines, LANES), BRAIN),
            pltpu.VMEM((places, lines, LANES), BRAIN),
            pltpu.VMEM((places, lines, LANES), BRAIN),
            pltpu.VMEM((places - 1, lines, LANES), BRAIN),
            pltpu.VMEM((cols, unit, LANES), BRAIN),
            pltpu.VMEM((shards, part, LANES), BRAIN),
            pltpu.VMEM((cols - 1, unit, LANES), BRAIN),
            pltpu.VMEM((max(shards - 1, 1), part, LANES), BRAIN),
            pltpu.VMEM((cols, unit, LANES), BRAIN),
            pltpu.VMEM((part, LANES), BRAIN),
            pltpu.VMEM((2, places, cols, unit, LANES), BRAIN),
            pltpu.VMEM((2, places, part, LANES), BRAIN),
        ]
        + sems,
        80,
    )
    count = len(shared)
    split = [value[:, :piece] for value, piece in zip(result[1 + count :], pieces)]
    return result[0], result[1 : 1 + count], split


def opening_kernel(count, routes, *refs):
    small, refs = refs[:count], refs[count:]
    tokens, gains, vectors, pack, *refs = refs
    small_out, refs = refs[:count], refs[count:]
    tokens_out, gains_out, vectors_out, packs_out, *refs = refs
    flat, got, others, across_sems, spread_sems, *refs = refs
    peers, cols = lax.axis_size("row"), lax.axis_size("col")
    shards = cols // 2
    row, col = lax.axis_index("row"), lax.axis_index("col")
    plan = line_plan([value.shape for value in small], flat.shape[1])
    barrier = pltpu.get_barrier_semaphore()
    signals = [(row, (col + by) % cols) for by in range(1, cols)]
    signals += [((row + by) % peers, col) for by in range(1, peers)]
    for to in signals:
        pl.semaphore_signal(barrier, inc=1, device_id=to, device_id_type=MESH)
    flat[...] = jnp.zeros(flat.shape, BRAIN)
    for at, rows, lanes, index, lines in plan:
        flat[index, lines] = small[at][rows, lanes]
    pl.semaphore_wait(barrier, len(signals))

    across, copies = [], []
    for turn in range(1, shards):
        to = (row, (col + cols - 2 * turn) % cols)
        across.append(remote(flat.at[row], got.at[turn - 1], across_sems, turn - 1, to))
    for copy in across:
        copy.start()
    token_got, vector_got, token_sems, gain_sems, vector_sems, pack_sems = refs
    own, piece = tokens_out.shape[0], tokens.shape[1]
    for turn in range(1, shards):
        to = (row, (col + cols - 2 * turn) % cols)
        copies.append(remote(vectors, vector_got.at[turn - 1], vector_sems, turn - 1, to))
    copies += shipped(routes, [pack], [packs_out], pack_sems)
    for by in range(1, cols):
        to = (col + by) % cols
        there = pl.ds(pl.multiple_of(to * own, own), own)
        copies.append(remote(tokens.at[there], token_got.at[col], token_sems, by - 1, (row, to)))
        copies.append(remote(gains, gains_out.at[col], gain_sems, by - 1, (row, to)))
    for copy in copies:
        copy.start()
    token_got[col] = tokens[pl.ds(pl.multiple_of(col * own, own), own)]
    gains_out[col] = gains[...]
    spread = []
    for turn in range(1, shards):
        across[turn - 1].wait()
        for by in range(1, peers):
            to = ((row + by) % peers, col)
            slot = (turn - 1) * (peers - 1) + by - 1
            copy = remote(got.at[turn - 1], others.at[turn - 1, row], spread_sems, slot, to)
            copy.start()
            spread.append(copy)
        others[turn - 1, row] = got[turn - 1]
    for at in range(count):
        small_out[at][0] = small[at][...]
    for copy in copies:
        copy.wait()
    for at in range(cols):
        tokens_out[:, at * piece : (at + 1) * piece] = token_got[at]
    vectors_out[0] = vectors[...]
    for turn in range(1, shards):
        vectors_out[turn] = vector_got[turn - 1]
    for copy in spread:
        copy.wait()
    for turn in range(1, shards):
        for at, rows, lanes, index, lines in plan:
            small_out[at][turn, rows, lanes] = others[turn - 1, index, lines]


def open_up(ident, small, tokens, gains, vectors, pack):
    peers, cols = lax.axis_size("row"), lax.axis_size("col")
    shards = cols // 2
    rest = max(shards - 1, 1)
    kept = [value.shape[1] for value in small]
    small = [
        jnp.pad(value, ((0, 0), (0, -value.shape[1] % LANES))) if value.shape[1] % LANES else value
        for value in small
    ]
    lines = sum(value.shape[0] * value.shape[1] for value in small) // LANES
    unit = -(-lines // (peers * 16)) * 16
    rows, piece = tokens.shape
    own = rows // cols
    routes = routes_of(pack.shape[1], range(PARTS), 0, 0)
    operands = [*small, tokens, gains, vectors, pack]
    outs = [((shards,) + value.shape, BRAIN) for value in small]
    outs += [
        ((own, piece * cols), BRAIN),
        ((cols,) + gains.shape, FLOAT),
        ((shards,) + vectors.shape, FLOAT),
        ((pack.shape[0], pack.shape[1] * shards), BRAIN),
    ]
    scratch = [
        pltpu.VMEM((peers, unit, LANES), BRAIN),
        pltpu.VMEM((rest, unit, LANES), BRAIN),
        pltpu.VMEM((rest, peers, unit, LANES), BRAIN),
        pltpu.SemaphoreType.DMA((2, rest)),
        pltpu.SemaphoreType.DMA((2, rest * (peers - 1))),
        pltpu.VMEM((cols, own, piece), BRAIN),
        pltpu.VMEM((rest,) + vectors.shape, FLOAT),
    ]
    scratch += [
        pltpu.SemaphoreType.DMA((2, size)) for size in (cols - 1, cols - 1, rest, len(routes))
    ]
    result = block_call(
        partial(opening_kernel, len(small), routes), ident, operands, outs, scratch, 30,
        anywhere=1,
    )
    values = [value[:, :, :size] for value, size in zip(result, kept)]
    return values, result[len(small) :]


PARTS = 3


def routes_of(pack_width, parts, source, target, begin=0):
    shards = lax.axis_size("col") // 2
    piece = pack_width // PARTS
    return [
        (source, part * piece, piece, target, ((part - begin) * shards + shard) * piece, shard)
        for part in parts
        for shard in range(shards)
    ]


def shipped(routes, sources, targets, sems):
    cols = lax.axis_size("col")
    row, col = lax.axis_index("row"), lax.axis_index("col")
    copies = []
    for slot, (source, begin, width, target, place, shard) in enumerate(routes):
        held = sources[source].at[:, pl.ds(begin, width)]
        there = targets[target].at[:, pl.ds(place, width)]
        if shard:
            to = (row, (col + cols - 2 * shard) % cols)
            copies.append(remote(held, there, sems, slot, to))
        else:
            copies.append(pltpu.make_async_copy(held, there, sems.at[0, slot]))
    return copies


TILE = 256
LINES = 64


def turn_kernel(backward, offset, plan, sources, counts, routes, *refs):
    (x, wide, x2, w2, stream, gain, d_stream), refs = refs[:7], refs[7:]
    extra, refs = refs[:sources], refs[sources:]
    cargo, refs = refs[: counts[0]], refs[counts[0] :]
    (new_out, full_out), refs = refs[:2], refs[2:]
    grad_outs, refs = refs[: len(plan)], refs[len(plan) :]
    cargo_outs, refs = refs[: counts[1]], refs[counts[1] :]
    weights, sending, received, mine, weight_sems, share_sems, spread_sems, cargo_sems = refs
    cols = lax.axis_size("col")
    shards = cols // 2
    own = stream.shape[0]
    depth = x.shape[1]
    tiles = sending.shape[0]
    row, col = lax.axis_index("row"), lax.axis_index("col")
    peer = (row, col + 1 - 2 * (col % 2))

    barrier = pltpu.get_barrier_semaphore()
    greeted = [peer]
    if routes:
        greeted += [(row, (col + 2 * other) % cols) for other in range(1, shards)]
    for to in greeted:
        pl.semaphore_signal(barrier, inc=1, device_id=to, device_id_type=MESH)

    def weight_copy(tile):
        lines = pl.ds(pl.multiple_of(tile * TILE, TILE), TILE)
        return pltpu.make_async_copy(
            wide.at[lines, pl.ds(offset, depth)], weights.at[tile], weight_sems.at[tile]
        )

    def share_copy(tile):
        return remote(sending.at[tile], received.at[tile], share_sems, tile, peer)

    def spread_copy(at):
        lines = pl.multiple_of(at * LINES, LINES)
        return pltpu.make_async_remote_copy(
            src_ref=full_out.at[pl.ds(lines, LINES)],
            dst_ref=full_out.at[pl.ds(pl.multiple_of(own + lines, LINES), LINES)],
            send_sem=spread_sems.at[0, at],
            recv_sem=spread_sems.at[1, at],
            device_id=peer,
            device_id_type=MESH,
        )

    def begin(tile, nothing):
        weight_copy(tile).start()
        return nothing

    lax.fori_loop(0, tiles, begin, 0)
    pl.semaphore_wait(barrier, len(greeted))
    carried = shipped(routes, cargo, cargo_outs, cargo_sems)
    for copy in carried:
        copy.start()

    def project(tile, nothing):
        weight_copy(tile).wait()
        at = pl.ds(pl.multiple_of(tile * TILE, TILE), TILE)
        total = nt(x[...], weights[tile]) + nn(x2[...], w2[:, at])
        sending[tile] = total[own:].astype(BRAIN)
        mine[tile] = total[:own]
        share_copy(tile).start()
        return nothing

    lax.fori_loop(0, tiles, project, 0)

    def gradients(part):
        for (left, right, lanes), out in part:
            value = (x if right is None else extra[right])[:, lanes]
            out[...] = tn(extra[left][...], value)

    pairs = list(zip(plan, grad_outs))
    gradients(pairs[: len(pairs) // 2])

    def arrive(tile, nothing):
        share_copy(tile).wait()
        return nothing

    lax.fori_loop(0, tiles, arrive, 0)

    def finish(at, nothing):
        lines = pl.ds(pl.multiple_of(at * LINES, LINES), LINES)
        total = jnp.concatenate(
            [mine[tile, lines] + received[tile, lines].astype(FLOAT) for tile in range(tiles)],
            axis=1,
        )
        value = stream[lines]
        if backward:
            scale = lax.rsqrt(jnp.mean(value * value, axis=1, keepdims=True) + EPSILON)
            gained = total * gain[...]
            shift = jnp.mean(gained * value, axis=1, keepdims=True)
            result = d_stream[lines] + scale * gained - value * (scale * scale * scale * shift)
            new_out[lines] = result
            full_out[lines] = result.astype(BRAIN)
        else:
            result = value + total
            scale = lax.rsqrt(jnp.mean(result * result, axis=1, keepdims=True) + EPSILON)
            new_out[lines] = result
            full_out[lines] = (result * scale * gain[...]).astype(BRAIN)
        spread_copy(at).start()
        return nothing

    lax.fori_loop(0, own // LINES, finish, 0)
    gradients(pairs[len(pairs) // 2 :])

    def leave(at, nothing):
        spread_copy(at).wait()
        return nothing

    lax.fori_loop(0, own // LINES, leave, 0)
    for copy in carried:
        copy.wait()


def turn(
    ident, x, wide, offset, x2, w2, stream, gain, d_stream=None, extra=(), plan=(), cargo=(),
    widths=(), routes=(),
):
    own, d_model = stream.shape
    depth = x.shape[1]
    tiles = d_model // TILE
    whole = pl.BlockSpec(memory_space=pltpu.VMEM)
    backward = d_stream is not None
    operands = [x, wide, x2, w2, stream, gain, d_stream if backward else gain, *extra]
    specs = [whole] * len(operands)
    anywhere = pl.BlockSpec(memory_space=pl.ANY)
    specs[1] = anywhere
    operands += cargo
    specs += [anywhere] * len(cargo)
    plan = tuple(plan)
    sizes = []
    for left, right, lanes in plan:
        wide_by = (x if right is None else extra[right]).shape[1]
        sizes.append((extra[left].shape[1], len(range(wide_by)[lanes])))
    return pl.pallas_call(
        partial(turn_kernel, backward, offset, plan, len(extra), (len(cargo), len(widths)), tuple(routes)),
        out_shape=[
            jax.ShapeDtypeStruct((own, d_model), FLOAT),
            jax.ShapeDtypeStruct((2 * own, d_model), BRAIN),
        ]
        + [jax.ShapeDtypeStruct(size, FLOAT) for size in sizes]
        + [jax.ShapeDtypeStruct((cargo[0].shape[0], size), cargo[0].dtype) for size in widths],
        in_specs=specs,
        out_specs=[whole] * (2 + len(plan)) + [anywhere] * len(widths),
        scratch_shapes=[
            pltpu.VMEM((tiles, TILE, depth), BRAIN),
            pltpu.VMEM((tiles, own, TILE), BRAIN),
            pltpu.VMEM((tiles, own, TILE), BRAIN),
            pltpu.VMEM((tiles, own, TILE), FLOAT),
            pltpu.SemaphoreType.DMA((tiles,)),
            pltpu.SemaphoreType.DMA((2, tiles)),
            pltpu.SemaphoreType.DMA((2, own // LINES)),
            pltpu.SemaphoreType.DMA((2, max(len(routes), 1))),
        ],
        cost_estimate=lasting(40),
        compiler_params=pltpu.CompilerParams(
            vmem_limit_bytes=VMEM_BYTES, collective_id=ident, has_side_effects=True
        ),
    )(*operands)


def partner(value):
    peers = lax.axis_size("col")
    return lax.ppermute(value, "col", [(at, at ^ 1) for at in range(peers)])


def from_shard(value, turn):
    peers = lax.axis_size("col")
    return lax.ppermute(value, "col", [((at + 2 * turn) % peers, at) for at in range(peers)])


def to_shard(value, turn):
    peers = lax.axis_size("col")
    return lax.ppermute(value, "col", [(at, (at + 2 * turn) % peers) for at in range(peers)])


def all_shards(value):
    return [value] + [from_shard(value, turn) for turn in range(1, lax.axis_size("col") // 2)]


def after(value, anchor):
    return lax.optimization_barrier((value, anchor))[0] if jax.tree.leaves(anchor) else value


def to_sequence(value):
    return lax.all_to_all(value, "col", split_axis=0, concat_axis=1, tiled=True)


def from_sequence(value):
    return lax.all_to_all(value, "col", split_axis=1, concat_axis=0, tiled=True)


def both_halves(value):
    return jnp.concatenate([value, partner(value)], axis=0)


def half_share(own, other):
    return own + partner(other.astype(BRAIN)).astype(FLOAT)


def norm_forward(stream, gain):
    scale = lax.rsqrt(jnp.mean(stream * stream, axis=1, keepdims=True) + EPSILON)
    return scale, (stream * scale * gain[None, :]).astype(BRAIN)


def masked(value, pick):
    return (value * pick).astype(BRAIN)


def recur_branch(normed_full, wide, small, ctx):
    pick = ctx["pick"]
    ranks = pick.shape[1]
    width = wide.shape[1] // 3
    low = nt(normed_full, small["inlet_lower"])
    inner = [masked(low[:, b * ranks : (b + 1) * ranks], pick) for b in range(2)]
    branch = nn(normed_full, wide[:, : 2 * width])
    lead = branch[:, :width] + nn(inner[0], small["inlet_upper"][0])
    gate = branch[:, width:] + nn(inner[1], small["inlet_upper"][1])
    return lead, gate, inner


def recur_part(
    ident, stream, lead, gate, wide, small, gain, ctx, ready, cargo, widths, routes
):
    pick, offset = ctx["pick"], ctx["offset"]
    width = lead.shape[1]
    conv, decay, hidden, mixed, state_in = recur_forward(lead, gate, offset, small)
    mixed = after(mixed, ready)
    lowrank = masked(nt(mixed, small["outlet_lower"]), pick)
    middle, normed_two_full, *parts = turn(
        ident, mixed, wide, 2 * width, lowrank, small["outlet_upper"], stream, gain, cargo=cargo,
        widths=widths, routes=routes,
    )
    kept = dict(
        conv=conv, decay=decay, hidden=hidden, state_in=state_in, mixed=mixed, lowrank=lowrank,
        middle=middle, normed_two_full=normed_two_full,
    )
    return middle, normed_two_full, kept, parts


def hidden_part(normed_two_full, wide, small, ctx):
    pick = ctx["pick"]
    ranks = pick.shape[1]
    spread = wide.shape[1] // 3
    low_two = nt(normed_two_full, small["expand_lower"])
    inner_two = [masked(low_two[:, b * ranks : (b + 1) * ranks], pick) for b in range(2)]
    branch_two = nn(normed_two_full, wide[:, : 2 * spread])
    up_gate = branch_two[:, :spread] + nn(inner_two[0], small["expand_upper"][0])
    up_value = branch_two[:, spread:] + nn(inner_two[1], small["expand_upper"][1])
    product = (gelu_tanh(up_gate) * up_value).astype(BRAIN)
    lowrank_two = masked(nt(product, small["shrink_lower"]), pick)
    return dict(
        inner_two=inner_two, up_gate=up_gate, up_value=up_value, product=product,
        lowrank_two=lowrank_two,
    )


def layer_backward(ident, d_stream, d_out, wide, small, gains, kept, ctx, first, pending):
    recur_wide, hidden_wide = wide
    pick, offset = ctx["pick"], ctx["offset"]
    own = d_stream.shape[0]
    rows = 2 * own
    width = recur_wide.shape[1] // 3
    spread = hidden_wide.shape[1] // 3

    d_low_two = masked(nt(d_out, small["shrink_upper"]), pick)
    d_product = nn(d_out, hidden_wide[:, 2 * spread :]) + nn(d_low_two, small["shrink_lower"])
    value, slope = gelu_pair(kept["up_gate"])
    d_branch_two = jnp.concatenate(
        [(slope * kept["up_value"] * d_product).astype(BRAIN), (value * d_product).astype(BRAIN)],
        axis=1,
    )
    d_inner_two = jnp.concatenate(
        [
            masked(nt(d_branch_two[:, b * spread : (b + 1) * spread], small["expand_upper"][b]), pick)
            for b in range(2)
        ],
        axis=1,
    )
    halves = (slice(0, spread), slice(spread, 2 * spread))
    every = slice(None)
    d_middle, d_mid, shrink_upper, shrink_lower, expand_lower, expand_a, expand_b = turn(
        ident, d_branch_two, hidden_wide, 0, d_inner_two, small["expand_lower"], kept["middle"],
        gains[1:2], d_stream,
        [kept["lowrank_two"], d_out, d_low_two, kept["product"], d_inner_two,
         kept["normed_two_full"], *kept["inner_two"]],
        [(0, 1, every), (2, 3, every), (4, 5, every), (6, None, halves[0]), (7, None, halves[1])],
    )
    expand_upper = jnp.concatenate([expand_a, expand_b], axis=0)

    d_mid, ctx["last"] = lax.optimization_barrier((d_mid, pending))
    d_low = masked(nt(d_mid, small["outlet_upper"]), pick)
    d_mixed = nn(d_mid, recur_wide[:, 2 * width :]) + nn(d_low, small["outlet_lower"])
    d_branch = recur_backward(d_mixed, kept, offset, small)
    d_inner = jnp.concatenate(
        [
            masked(nt(d_branch[:, b * width : (b + 1) * width], small["inlet_upper"][b]), pick)
            for b in range(2)
        ],
        axis=1,
    )
    halves = (slice(0, width), slice(width, 2 * width))
    if first:
        outlet_upper = tn(kept["lowrank"], d_mid)
        outlet_lower = tn(d_low, kept["mixed"])
        inlet_lower = tn(d_inner, kept["normed_full"])
        inlet_a, inlet_b = (tn(kept["inner"][b], d_branch[:, halves[b]]) for b in range(2))
        result = tuple(
            nt(d_branch[part], recur_wide[:, : 2 * width]) + nn(d_inner[part], small["inlet_lower"])
            for part in (slice(0, own), slice(own, rows))
        )
    else:
        d_before, d_out_before, outlet_upper, outlet_lower, inlet_lower, inlet_a, inlet_b = turn(
            ident + 1, d_branch, recur_wide, 0, d_inner, small["inlet_lower"], kept["stream"],
            gains[0:1], d_middle,
            [kept["lowrank"], d_mid, d_low, kept["mixed"], d_inner, kept["normed_full"],
             *kept["inner"]],
            [(0, 1, every), (2, 3, every), (4, 5, every), (6, None, halves[0]),
             (7, None, halves[1])],
        )
        result = (d_before, d_out_before)
    inlet_upper = jnp.concatenate([inlet_a, inlet_b], axis=0)
    shared = (inlet_lower, outlet_upper, expand_lower, shrink_upper)
    split = (inlet_upper, outlet_lower, expand_upper, shrink_lower)
    return d_middle, result, shared, split


def local(
    tokens, cotangent, adapter_ids, doc_lengths, norm_gain, inlet_weight, inlet_lower, inlet_upper,
    conv_weight, conv_bias, gate_weight, gate_bias, decay_param, outlet_weight, outlet_lower,
    outlet_upper, expand_weight, expand_lower, expand_upper, shrink_weight, shrink_lower,
    shrink_upper,
):
    row_at, col_at = lax.axis_index("row"), lax.axis_index("col")
    cols = lax.axis_size("col")
    shards = cols // 2
    rows = tokens.shape[0]
    own = rows // cols
    block = 2 * own
    docs = adapter_ids.shape[0]
    adapters, rank = inlet_lower.shape[3:]
    part_width, part_spread = inlet_weight.shape[3], expand_weight.shape[3]
    d_model = inlet_lower.shape[1]

    parity = (col_at % 2).astype(jnp.int32)
    ends = jnp.cumsum(doc_lengths)
    starts = ends - doc_lengths
    ordered = row_at * rows + (col_at // 2) * block + jnp.arange(block, dtype=jnp.int32)
    inside = (ordered[:, None] >= starts[None, :]) & (ordered[:, None] < ends[None, :])
    offset = (ordered - jnp.sum(jnp.where(inside, starts[None, :], 0), axis=1))[:, None]
    halves = (parity * own, own - parity * own)
    at_home = jnp.concatenate(
        [ordered[0] + begin + jnp.arange(own, dtype=jnp.int32) for begin in halves]
    )
    within = (at_home[:, None] >= starts[None, :]) & (at_home[:, None] < ends[None, :])
    pick = jnp.repeat(within.astype(FLOAT), rank, axis=1)
    ctx = dict(pick=pick, offset=offset, pending={})


    def by_doc(factor, axis):
        return jnp.concatenate(
            [lax.dynamic_slice_in_dim(factor, adapter_ids[at], 1, axis) for at in range(docs)], axis
        )

    def lower_t(factor):
        return by_doc(jnp.moveaxis(factor, 1, -1), factor.ndim - 3)

    def upper_t(factor):
        return by_doc(factor, factor.ndim - 3)

    ranks = docs * rank
    lows = dict(
        inlet_lower=lower_t(inlet_lower).reshape(LAYERS, 2 * ranks, d_model),
        outlet_upper=upper_t(outlet_upper).reshape(LAYERS, ranks, d_model),
        expand_lower=lower_t(expand_lower).reshape(LAYERS, 2 * ranks, d_model),
        shrink_upper=upper_t(shrink_upper).reshape(LAYERS, ranks, d_model),
    )
    narrow_own = jnp.concatenate(
        [
            upper_t(inlet_upper).reshape(LAYERS, 2 * ranks, part_width),
            lower_t(outlet_lower).reshape(LAYERS, ranks, part_width),
        ],
        axis=1,
    )
    broad_own = jnp.concatenate(
        [
            upper_t(expand_upper).reshape(LAYERS, 2 * ranks, part_spread),
            lower_t(shrink_lower).reshape(LAYERS, ranks, part_spread),
        ],
        axis=1,
    )
    vectors_own = jnp.concatenate(
        [conv_weight, gate_bias, conv_bias[:, None], decay_param[:, None]], axis=1
    )

    def rows_of(value):
        return value.reshape(-1, value.shape[-1])

    def packed(pair, single):
        pack = jnp.concatenate([pair[:, 0], pair[:, 1], single], axis=1)
        short = -single.shape[1] % LANES
        if short:
            pack = jnp.pad(pack.reshape(pack.shape[0], PARTS, -1), ((0, 0), (0, 0), (0, short)))
            pack = pack.reshape(pack.shape[0], -1)
        return pack

    def side_packs(pack):
        parts = all_shards(pack)
        piece = pack.shape[1] // PARTS
        columns = [part[:, at * piece : (at + 1) * piece] for at in range(PARTS) for part in parts]
        return jnp.concatenate(columns, axis=1)

    def gathered(packs, piece):
        whole = lax.all_gather(packs, "row", axis=0, tiled=True)
        if piece % LANES:
            whole = whole.reshape(whole.shape[0], PARTS * shards, -1)[:, :, :piece]
            whole = whole.reshape(whole.shape[0], -1)
        return whole

    def recur_small(layer, narrow, gates):
        return dict(
            inlet_lower=lows["inlet_lower"][layer],
            inlet_upper=narrow[: 2 * ranks].reshape(2, ranks, -1),
            outlet_lower=narrow[2 * ranks :],
            outlet_upper=lows["outlet_upper"][layer],
            conv_weight=vectors_all[layer, :CONV],
            gate_bias=vectors_all[layer, CONV : CONV + 2],
            conv_bias=vectors_all[layer, CONV + 2 : CONV + 3],
            soft=jax.nn.softplus(vectors_all[layer, CONV + 3 : CONV + 4]),
            gate_weight=gates,
        )

    def hidden_small(layer, broad):
        return dict(
            expand_lower=lows["expand_lower"][layer],
            expand_upper=broad[: 2 * ranks].reshape(2, ranks, -1),
            shrink_lower=broad[2 * ranks :],
            shrink_upper=lows["shrink_upper"][layer],
        )

    outputs, saved, wides, smalls = [], [], [], []
    recur_packs = [packed(inlet_weight[at], outlet_weight[at]) for at in range(LAYERS)]
    hidden_packs = [packed(expand_weight[at], shrink_weight[at]) for at in range(LAYERS)]
    def side_by_side(value):
        return jnp.concatenate([value[at] for at in range(shards)], axis=1)

    def heads_in_turn(value):
        return jnp.concatenate(
            [value[at].reshape((2, -1) + gate_weight.shape[3:]) for at in range(shards)], axis=1
        )

    (narrow, gates, broad), (stream, gains, vectors_all, recur_side) = open_up(
        20, [narrow_own[0], rows_of(gate_weight[0]), broad_own[0]], tokens, rows_of(norm_gain),
        rows_of(vectors_own), recur_packs[0],
    )
    narrow, gates, broad = side_by_side(narrow), heads_in_turn(gates), side_by_side(broad)
    gains = jnp.moveaxis(gains, 0, 1).reshape(LAYERS, 2, d_model)
    vectors_all = side_by_side(vectors_all).reshape(LAYERS, -1, shards * part_width)
    wide_one = gathered(recur_side, part_width)
    hidden_side = side_packs(after(hidden_packs[0], stream))
    stream = stream.astype(FLOAT)
    _, normed = norm_forward(stream, gains[0][0])
    normed_full = both_halves(normed)
    normed_full, hidden_side = lax.optimization_barrier((normed_full, hidden_side))
    for layer in range(LAYERS):
        more_layers = layer + 1 < LAYERS
        kept = dict(stream=stream, normed_full=normed_full)
        small_one = recur_small(layer, narrow, gates)
        lead, gate, inner = recur_branch(normed_full, wide_one, small_one, ctx)
        ready, cargo, widths, routes = [], [], [], []
        if layer == 0:
            wide_two = gathered(after(hidden_side, lead), part_spread)
        if more_layers:
            narrow_parts, gate_parts = (
                all_shards(after(value[layer + 1], lead)) for value in (narrow_own, gate_weight)
            )
            ready = [narrow_parts[1:], gate_parts[1:]]
            cargo = [recur_packs[layer + 1], hidden_packs[layer + 1]]
            spans = [pack.shape[1] for pack in cargo]
            widths = [spans[0] * shards, spans[1] // PARTS * shards]
            routes = routes_of(spans[0], range(PARTS), 0, 0) + routes_of(spans[1], [0], 1, 1)
        elif layer:
            ending = to_sequence(after(cotangent, lead))
            ready = [ending]
            cargo = [broad_own[layer]]
            spread_piece = cargo[0].shape[1]
            if spread_piece % LANES:
                cargo = [jnp.pad(cargo[0], ((0, 0), (0, -spread_piece % LANES)))]
            span = cargo[0].shape[1]
            widths = [span * shards]
            routes = [(0, 0, span, 0, shard * span, shard) for shard in range(shards)]
        middle, normed_two_full, more, sides = recur_part(
            3 + 2 * layer, stream, lead, gate, wide_one, small_one, gains[layer][1:2], ctx, ready,
            cargo, widths, routes,
        )
        if layer and not more_layers:
            broad = sides[0].reshape(sides[0].shape[0], shards, -1)[:, :, :spread_piece]
            broad = broad.reshape(broad.shape[0], -1)
        kept.update(inner=inner, gate=gate, **more)
        if more_layers:
            wide_next = gathered(sides[0], part_width)
        small_two = hidden_small(layer, broad)
        more = hidden_part(normed_two_full, wide_two, small_two, ctx)
        kept.update(more)
        wides.append((wide_one, wide_two))
        smalls.append({**small_one, **small_two})
        saved.append(kept)
        product, lowrank, upper = more["product"], more["lowrank_two"], small_two["shrink_upper"]
        spread = product.shape[1]
        if more_layers:
            pack = hidden_packs[layer + 1]
            span, early = pack.shape[1], sides[1].shape[1]
            routes = routes_of(span, range(1, PARTS), 0, 0) + [(1, 0, early, 0, 0, 0)]
            stream, normed_full, hidden_side = turn(
                4 + 2 * layer, product, wide_two, 2 * spread, lowrank, upper, middle,
                gains[layer + 1][0:1], cargo=[pack, sides[1]], widths=[span * shards],
                routes=routes,
            )
            wide_two_next = gathered(hidden_side, part_spread)
            narrow, gates = (jnp.concatenate(part, axis=1) for part in (narrow_parts, gate_parts))
            wide_one, wide_two = wide_next, wide_two_next
        else:
            shrink = wide_two[:, 2 * spread :]
            parts = [
                nt(product[part], shrink) + nn(lowrank[part], upper)
                for part in (slice(0, own), slice(own, 2 * own))
            ]
            stream = middle + half_share(*parts)
            last_stream = stream
        outputs.append(from_sequence(stream.astype(BRAIN)))
    ctx["pending"] = {LAYERS - 1: last_stream, LAYERS - 2: outputs.pop()}
    d_stream, d_out = ending.astype(FLOAT), both_halves(after(ending, normed_two_full))
    shared_parts, split_parts = [], []
    for layer in reversed(range(LAYERS)):
        kept = saved[layer]
        d_middle, result, shared_more, split_more = layer_backward(
            3 + 2 * LAYERS + 2 * layer, d_stream, d_out, wides[layer], smalls[layer], gains[layer],
            kept, ctx, layer == 0, ctx["pending"].get(layer),
        )
        shared_parts = [*shared_more, *shared_parts]
        split_parts = [*split_more, *split_parts]
        if layer:
            d_stream, d_out = result
    tokens_grad, shared_parts, split_parts = close(
        result[0], result[1].astype(BRAIN), kept["stream"], d_middle, gains[0][:1], shared_parts,
        split_parts,
    )
    inlet_low, outlet_up, expand_low, shrink_up = (
        jnp.stack(shared_parts[at::4]) for at in range(4)
    )
    inlet_up, outlet_low, expand_up, shrink_low = (jnp.stack(split_parts[at::4]) for at in range(4))
    spread_out = (adapter_ids[None, :] == jnp.arange(adapters, dtype=jnp.int32)[:, None])

    def by_adapter(grad, count):
        grad = grad.reshape(LAYERS, count, docs, rank, -1)
        total = 0.0
        for doc in range(docs):
            total = total + jnp.where(
                spread_out[None, None, :, doc, None, None], grad[:, :, doc][:, :, None], 0.0
            )
        return total

    def lower_out(grad, count):
        grad = by_adapter(grad, count)
        if count == 1:
            grad = grad[:, 0]
        return jnp.moveaxis(grad, -1, 1)

    return (
        jnp.stack([*outputs, ctx["last"]], axis=0),
        tokens_grad,
        lower_out(inlet_low, 2),
        by_adapter(inlet_up, 2),
        lower_out(outlet_low, 1),
        by_adapter(outlet_up, 1)[:, 0],
        lower_out(expand_low, 2),
        by_adapter(expand_up, 2),
        lower_out(shrink_low, 1),
        by_adapter(shrink_up, 1)[:, 0],
    )


def solution(mesh):
    return jax.shard_map(
        local,
        mesh=mesh,
        in_specs=(
            P("row", "col"),
            P("row", "col"),
            P(),
            P(),
            P(None, None, "col"),
            P(None, "row", None, "col"),
            P(),
            P(None, None, None, None, "col"),
            P(None, None, "col"),
            P(None, "col"),
            P(None, None, "col", None, None),
            P(None, None, "col"),
            P(None, "col"),
            P(None, "row", "col"),
            P(None, "col", None, None),
            P(),
            P(None, "row", None, "col"),
            P(),
            P(None, None, None, None, "col"),
            P(None, "row", "col"),
            P(None, "col", None, None),
            P(),
        ),
        out_specs=(
            P(None, "row", "col"),
            P("row", "col"),
            P(),
            P(None, None, None, None, "col"),
            P(None, "col", None, None),
            P(),
            P(),
            P(None, None, None, None, "col"),
            P(None, "col", None, None),
            P(),
        ),
        check_vma=False,
    )
```

```python
from functools import partial

import jax
import jax.numpy as jnp
from jax import lax
from jax.experimental import pallas as pl
from jax.experimental.pallas import tpu as pltpu
from jax.sharding import PartitionSpec as P

HS = 256
CONV = 4
LAYERS = 2
SEGS = 8

EPSILON = 1e-06
FLOAT = jnp.float32
BRAIN = jnp.bfloat16
VMEM_BYTES = 48 * 1024 * 1024
CURVE = 0.7978845608028654
CUBIC = 0.044715
LANES = 128
SLABS = HS // LANES
MESH = pl.DeviceIdType.MESH


def nn(left, right):
    return lax.dot_general(left, right, (((1,), (0,)), ((), ())), preferred_element_type=FLOAT)


def nt(left, right):
    return lax.dot_general(left, right, (((1,), (1,)), ((), ())), preferred_element_type=FLOAT)


def tn(left, right):
    return lax.dot_general(left, right, (((0,), (0,)), ((), ())), preferred_element_type=FLOAT)


def gelu_tanh(value):
    return 0.5 * value * (1.0 + jnp.tanh(CURVE * (value + CUBIC * value * value * value)))


def gelu_pair(value):
    square = value * value
    bend = jnp.tanh(CURVE * value * (1.0 + CUBIC * square))
    half = 0.5 * (1.0 + bend)
    slope = half + 0.5 * value * (1.0 - bend * bend) * CURVE * (1.0 + 3.0 * CUBIC * square)
    return value * half, slope


def one_less_square(twice, square):
    series = -twice * (
        1.0 + twice * (0.5 + twice * (1.0 / 6.0 + twice * (1.0 / 24.0 + twice * (1.0 / 120.0))))
    )
    return jnp.where(twice > -0.1, series, 1.0 - square)


def gate_values(conv, gate_w, gate_b, soft):
    rate = jax.nn.sigmoid(nn(conv, gate_w[0]) + gate_b[0:1])
    inward = jax.nn.sigmoid(nn(conv, gate_w[1]) + gate_b[1:2])
    log_decay = (-8.0 * soft) * rate
    raw = jnp.exp(log_decay)
    gap = one_less_square(2.0 * log_decay, raw * raw)
    return rate, inward, raw, gap


def chain(axis_row="row", axis_col="col"):
    blocks_in_row = lax.axis_size(axis_col) // 2
    blocks = lax.axis_size(axis_row) * blocks_in_row
    col = lax.axis_index(axis_col)
    side = col % 2
    here = lax.axis_index(axis_row) * blocks_in_row + col // 2

    def device(by):
        block = (here + by + blocks) % blocks
        return (block // blocks_in_row, (block % blocks_in_row) * 2 + side)

    return blocks, blocks_in_row, here, side, device


def greet(blocks, device):
    barrier = pltpu.get_barrier_semaphore()
    for by in range(1, blocks):
        pl.semaphore_signal(barrier, inc=1, device_id=device(by), device_id_type=MESH)
    pl.semaphore_wait(barrier, blocks - 1)


def share_totals(blocks, device, direction, totals, inbox, send_sems, recv_sems):
    copies = [
        pltpu.make_async_remote_copy(
            src_ref=totals,
            dst_ref=inbox.at[by - 1],
            send_sem=send_sems.at[by - 1],
            recv_sem=recv_sems.at[by - 1],
            device_id=device(direction * by),
            device_id_type=MESH,
        )
        for by in range(1, blocks)
    ]
    for copy in copies:
        copy.start()
    for copy in copies:
        copy.wait()


def folded(blocks, shards, ahead, direction, inbox):
    slabs = inbox.shape[1] // 2
    piece = slabs // shards
    state = jnp.zeros((slabs, LANES), FLOAT)
    for by in reversed(range(1, blocks)):
        turn = (direction * by) % shards * piece
        cum, add = (
            jnp.concatenate([part[turn:], part[:turn]], axis=0) if turn else part
            for part in (inbox[by - 1, 0:slabs], inbox[by - 1, slabs : 2 * slabs])
        )
        state = jnp.where(ahead >= by, cum * state + add, state)
    return state


def forward_kernel(
    lead, gate, offset, conv_w, conv_b, gate_w, gate_b, soft,
    conv_out, decay_out, hidden_out, mixed_out, carry_out,
    ext, drive, state_all, cum_all, seg, totals, halo, inbox,
    halo_sems, send_sems, recv_sems,
):
    rows, width = lead.shape
    heads = width // HS
    half = rows // 2
    span = rows // SEGS
    slabs = width // LANES
    blocks, shards, here, side, device = chain()
    start = pl.multiple_of(side * half, half)
    other = pl.multiple_of(half - side * half, half)
    greet(blocks, device)
    rim = pltpu.make_async_remote_copy(
        src_ref=lead.at[pl.ds(pl.multiple_of(other + half - 8, 8), 8)],
        dst_ref=halo,
        send_sem=halo_sems.at[0],
        recv_sem=halo_sems.at[1],
        device_id=device(1),
        device_id_type=MESH,
    )
    rim.start()
    rim.wait()

    def run_head(head, nothing):
        at = pl.ds(pl.multiple_of(head * HS, HS), HS)
        there = (head + heads // shards) % heads
        ext[0:8] = halo[:, pl.ds(pl.multiple_of(there * HS, HS), HS)]
        ext[8 : 8 + half] = lead[pl.ds(start, half), at]
        ext[8 + half : 8 + rows] = lead[pl.ds(other, half), at]
        place = offset[...]
        total = conv_b[:, at] + conv_w[0:1, at] * ext[8 : 8 + rows]
        for step in range(1, CONV):
            valid = (place >= step).astype(FLOAT)
            total = total + conv_w[step : step + 1, at] * ext[8 - step : 8 - step + rows] * valid
        conv = total.astype(BRAIN)
        conv_out[:, at] = conv
        rate, inward, raw, gap = gate_values(
            conv, (gate_w[0, head], gate_w[1, head]), gate_b[:, at], soft[:, at]
        )
        first = (place == 0).astype(FLOAT)
        keep = 1.0 - first
        decay = raw * keep
        pushed = (keep * jnp.sqrt(gap) + first) * inward * conv.astype(FLOAT)
        for slab in range(SLABS):
            decay_out[head * SLABS + slab] = decay[:, slab * LANES : (slab + 1) * LANES]
            drive[slab] = pushed[:, slab * LANES : (slab + 1) * LANES]

        def advance(step, carried):
            where = pl.ds(step, SEGS, stride=span)
            after = []
            for slab, (state, cum) in enumerate(carried):
                rates = decay_out[head * SLABS + slab, where, :]
                state = rates * state + drive[slab, where, :]
                cum = rates * cum
                state_all[head * SLABS + slab, where, :] = state
                cum_all[head * SLABS + slab, where, :] = cum
                after.append((state, cum))
            return tuple(after)

        fresh = (jnp.zeros((SEGS, LANES), FLOAT), jnp.ones((SEGS, LANES), FLOAT))
        ends = lax.fori_loop(0, span, advance, (fresh,) * SLABS, unroll=8)
        for slab, (state, cum) in enumerate(ends):
            run_state = jnp.zeros((1, LANES), FLOAT)
            run_cum = jnp.ones((1, LANES), FLOAT)
            at_slab = head * SLABS + slab
            for part in range(SEGS):
                seg[at_slab, part : part + 1] = run_state
                seg[at_slab, SEGS + part : SEGS + part + 1] = run_cum
                run_state = cum[part : part + 1] * run_state + state[part : part + 1]
                run_cum = cum[part : part + 1] * run_cum
            totals[pl.ds(at_slab, 1)] = run_cum
            totals[pl.ds(slabs + at_slab, 1)] = run_state
        return nothing

    lax.fori_loop(0, heads, run_head, 0)
    share_totals(blocks, device, 1, totals, inbox, send_sems, recv_sems)
    carry_out[...] = folded(blocks, shards, here, 1, inbox)

    def mix_slab(slab, nothing):
        at = pl.ds(pl.multiple_of(slab * LANES, LANES), LANES)
        entering = seg[slab, 0:SEGS] + seg[slab, SEGS : 2 * SEGS] * carry_out[pl.ds(slab, 1)]
        for part in range(SEGS):
            lines = slice(part * span, (part + 1) * span)
            hidden_out[slab, lines] = (
                state_all[slab, lines] + cum_all[slab, lines] * entering[part : part + 1]
            )
        for place, lines in ((start, slice(0, half)), (other, slice(half, rows))):
            mixed_out[pl.ds(place, half), at] = (
                hidden_out[slab, lines] * gelu_tanh(gate[pl.ds(place, half), at])
            ).astype(BRAIN)
        return nothing

    lax.fori_loop(0, slabs, mix_slab, 0)


def backward_kernel(
    grad, gate, hidden, decay, carry, conv, offset, conv_w, gate_w, gate_b, soft,
    lead_grad, gate_grad,
    ext, prior, grads, chain_decay, local_all, reach_all, seg, totals, arriving, heads_out,
    heads_in, tails, inbox, halo_sems, send_sems, recv_sems,
):
    rows, width = grad.shape
    heads = width // HS
    half = rows // 2
    span = rows // SEGS
    slabs = width // LANES
    blocks, shards, here, side, device = chain()
    start = pl.multiple_of(side * half, half)
    other = pl.multiple_of(half - side * half, half)
    greet(blocks, device)

    def run_slab(slab, nothing):
        at = pl.ds(pl.multiple_of(slab * LANES, LANES), LANES)
        for place, lines in ((start, slice(0, half)), (other, slice(half, rows))):
            value, slope = gelu_pair(gate[pl.ds(place, half), at])
            coming = grad[pl.ds(place, half), at]
            grads[lines] = coming * value
            gate_grad[pl.ds(place, half), at] = (
                coming * hidden[slab, lines] * slope
            ).astype(BRAIN)
        chain_decay[0:rows] = decay[slab]
        chain_decay[rows : rows + 8] = jnp.ones((8, LANES), FLOAT)

        def retreat(turn, carried):
            state, cum = carried
            step = span - 1 - turn
            where = pl.ds(step, SEGS, stride=span)
            rates = chain_decay[pl.ds(step + 1, SEGS, stride=span), :]
            state = rates * state + grads[where, :]
            cum = rates * cum
            local_all[slab, where, :] = state
            reach_all[slab, where, :] = cum
            return state, cum

        fresh = (jnp.zeros((SEGS, LANES), FLOAT), jnp.ones((SEGS, LANES), FLOAT))
        state, cum = lax.fori_loop(0, span, retreat, fresh, unroll=8)
        run_state = jnp.zeros((1, LANES), FLOAT)
        run_cum = jnp.ones((1, LANES), FLOAT)
        for part in reversed(range(SEGS)):
            seg[slab, part : part + 1] = run_state
            seg[slab, SEGS + part : SEGS + part + 1] = run_cum
            run_state = cum[part : part + 1] * run_state + state[part : part + 1]
            run_cum = cum[part : part + 1] * run_cum
        opening = chain_decay[0:1]
        totals[pl.ds(slab, 1)] = run_cum * opening
        totals[pl.ds(slabs + slab, 1)] = run_state * opening
        return nothing

    lax.fori_loop(0, slabs, run_slab, 0)
    share_totals(blocks, device, -1, totals, inbox, send_sems, recv_sems)
    arriving[...] = folded(blocks, shards, blocks - 1 - here, -1, inbox)

    def run_head(head, nothing):
        at = pl.ds(pl.multiple_of(head * HS, HS), HS)
        for slab in range(SLABS):
            slot = head * SLABS + slab
            lanes = slice(slab * LANES, (slab + 1) * LANES)
            entering = seg[slot, 0:SEGS] + seg[slot, SEGS : 2 * SEGS] * arriving[pl.ds(slot, 1)]
            for part in range(SEGS):
                lines = slice(part * span, (part + 1) * span)
                ext[lines, lanes] = (
                    local_all[slot, lines] + reach_all[slot, lines] * entering[part : part + 1]
                )
            prior[7:8, lanes] = carry[pl.ds(slot, 1)]
            prior[8 : 8 + rows, lanes] = hidden[slot]
        carried = ext[0:rows]
        before = prior[7 : 7 + rows]
        low = conv[:, at]
        value = low.astype(FLOAT)
        place = offset[...]
        first = (place == 0).astype(FLOAT)
        keep = 1.0 - first
        softness = soft[:, at]
        weights = (gate_w[0, head], gate_w[1, head])
        rate, inward, raw, gap = gate_values(low, weights, gate_b[:, at], softness)
        root = jnp.sqrt(gap)
        scale = keep * root + first
        pushed = carried * inward
        log_grad = keep * raw * (carried * before - pushed * value * (raw / root))
        rate_grad = ((-8.0 * softness) * log_grad * rate * (1.0 - rate)).astype(BRAIN)
        scaled = carried * scale
        input_grad = (scaled * value * inward * (1.0 - inward)).astype(BRAIN)
        conv_grad = scaled * inward + nt(rate_grad, weights[0]) + nt(input_grad, weights[1])
        ext[rows : rows + 8] = jnp.zeros((8, HS), FLOAT)
        total = conv_w[0:1, at] * conv_grad
        head_sum = jnp.zeros((8, HS), FLOAT)
        lines = lax.broadcasted_iota(jnp.int32, (8, 1), 0)
        for step in range(1, CONV):
            term = conv_w[step : step + 1, at] * conv_grad * (place >= step).astype(FLOAT)
            ext[0:rows] = term
            total = total + ext[step : step + rows]
            moved = pltpu.roll(term[0:8], 8 - step, 0)
            head_sum = head_sum + jnp.where(lines >= 8 - step, moved, 0.0)
        heads_out[:, at] = head_sum
        tails[:, at] = total[rows - 8 : rows]
        lead_grad[pl.ds(start, half), at] = total[0:half].astype(BRAIN)
        lead_grad[pl.ds(other, half), at] = total[half:rows].astype(BRAIN)
        return nothing

    lax.fori_loop(0, heads, run_head, 0)
    rim = pltpu.make_async_remote_copy(
        src_ref=heads_out,
        dst_ref=heads_in,
        send_sem=halo_sems.at[0],
        recv_sem=halo_sems.at[1],
        device_id=device(-1),
        device_id_type=MESH,
    )
    rim.start()
    rim.wait()
    followed = jnp.where(here < blocks - 1, 1.0, 0.0)
    for head in range(heads):
        at = slice(head * HS, (head + 1) * HS)
        there = (head - heads // shards) % heads
        whole = tails[:, at] + heads_in[:, there * HS : (there + 1) * HS] * followed
        kept = lead_grad[pl.ds(pl.multiple_of(other + half - 16, 16), 16), at]
        tails_pair = jnp.concatenate([kept[0:8], whole.astype(BRAIN)], axis=0)
        lead_grad[pl.ds(pl.multiple_of(other + half - 16, 16), 16), at] = tails_pair


def lasting(microseconds):
    return pl.CostEstimate(
        flops=int(microseconds * 1.1e9), bytes_accessed=int(microseconds * 3e6), transcendentals=0
    )


def block_call(kernel, ident, operands, outs, scratch, microseconds, anywhere=0):
    whole, open_place = pl.BlockSpec(memory_space=pltpu.VMEM), pl.BlockSpec(memory_space=pl.ANY)
    return pl.pallas_call(
        kernel,
        out_shape=[jax.ShapeDtypeStruct(*out) for out in outs],
        in_specs=[whole] * (len(operands) - anywhere) + [open_place] * anywhere,
        out_specs=[whole] * (len(outs) - anywhere) + [open_place] * anywhere,
        scratch_shapes=scratch,
        cost_estimate=lasting(microseconds),
        compiler_params=pltpu.CompilerParams(
            vmem_limit_bytes=VMEM_BYTES, collective_id=ident, has_side_effects=True
        ),
    )(*operands)


def message_scratch(width):
    others = lax.axis_size("row") * lax.axis_size("col") // 2 - 1
    slabs = width // LANES
    return [
        pltpu.VMEM((others, 2 * slabs, LANES), FLOAT),
        pltpu.SemaphoreType.DMA((2,)),
        pltpu.SemaphoreType.DMA((others,)),
        pltpu.SemaphoreType.DMA((others,)),
    ]


def recur_forward(lead, gate, offset, small):
    rows, width = lead.shape
    slabs = width // LANES
    stack = (slabs, rows, LANES)
    return block_call(
        forward_kernel,
        0,
        [lead, gate, offset, small["conv_weight"], small["conv_bias"], small["gate_weight"],
         small["gate_bias"], small["soft"]],
        [((rows, width), BRAIN), (stack, FLOAT), (stack, FLOAT), ((rows, width), BRAIN),
         ((slabs, LANES), FLOAT)],
        [
            pltpu.VMEM((rows + 8, HS), FLOAT),
            pltpu.VMEM((SLABS, rows, LANES), FLOAT),
            pltpu.VMEM(stack, FLOAT),
            pltpu.VMEM(stack, FLOAT),
            pltpu.VMEM((slabs, 2 * SEGS, LANES), FLOAT),
            pltpu.VMEM((2 * slabs, LANES), FLOAT),
            pltpu.VMEM((8, width), FLOAT),
        ]
        + message_scratch(width),
        27,
    )


def recur_backward(grad, kept, offset, small):
    rows, width = grad.shape
    slabs = width // LANES
    stack = (slabs, rows, LANES)
    return block_call(
        backward_kernel,
        1,
        [grad, kept["gate"], kept["hidden"], kept["decay"], kept["state_in"], kept["conv"], offset,
         small["conv_weight"], small["gate_weight"], small["gate_bias"], small["soft"]],
        [((rows, width), BRAIN), ((rows, width), BRAIN)],
        [
            pltpu.VMEM((rows + 8, HS), FLOAT),
            pltpu.VMEM((rows + 8, HS), FLOAT),
            pltpu.VMEM((rows, LANES), FLOAT),
            pltpu.VMEM((rows + 8, LANES), FLOAT),
            pltpu.VMEM(stack, FLOAT),
            pltpu.VMEM(stack, FLOAT),
            pltpu.VMEM((slabs, 2 * SEGS, LANES), FLOAT),
            pltpu.VMEM((2 * slabs, LANES), FLOAT),
            pltpu.VMEM((slabs, LANES), FLOAT),
            pltpu.VMEM((8, width), FLOAT),
            pltpu.VMEM((8, width), FLOAT),
            pltpu.VMEM((8, width), FLOAT),
        ]
        + message_scratch(width),
        30,
    )


def line_plan(pieces, unit):
    plan, line = [], 0
    for at, (rows, columns) in enumerate(pieces):
        for begin in range(0, columns, LANES):
            done = 0
            while done < rows:
                index, inner = divmod(line, unit)
                count = min(rows - done, unit - inner)
                plan.append(
                    (at, slice(done, done + count), slice(begin, begin + LANES), index,
                     slice(inner, inner + count))
                )
                done += count
                line += count
    return plan


def closing_sizes(shared, split, peers, cols, shards):
    shared_lines = sum(rows * columns for rows, columns in shared) // LANES
    split_lines = sum(rows * columns for rows, columns in split) // LANES // shards
    unit = -(-shared_lines // (peers * cols * 16)) * 16
    part = -(-split_lines // (peers * 16)) * 16
    return unit, part


def remote(source, target, sems, slot, device):
    return pltpu.make_async_remote_copy(
        src_ref=source,
        dst_ref=target,
        send_sem=sems.at[0, slot],
        recv_sem=sems.at[1, slot],
        device_id=device,
        device_id_type=MESH,
    )


def closing_kernel(count, layers, *refs):
    streams, refs = refs[:layers], refs[layers:]
    own_part, other_part, stream, d_middle, gain = refs[:5]
    shared, split = refs[5 : 5 + count], refs[5 + count : 5 + 2 * count]
    tokens_out, states_out, *refs = refs[5 + 2 * count :]
    shared_out, split_out = refs[:count], refs[count : 2 * count]
    (
        received, outgoing, homing, flat, beside_in, both, inbox, red, red_split, zbox, sbox, zfull,
        sfull, shared_all, split_all, pair_sems, beside_sems, row_sems, col_sems, turn_sems,
        spread_sems, shared_sems, split_sems, token_sems, leaving, state_sems,
    ) = refs[2 * count :]
    peers, cols = lax.axis_size("row"), lax.axis_size("col")
    shards = cols // 2
    row, col = lax.axis_index("row"), lax.axis_index("col")
    own, d_model = stream.shape
    piece = d_model // cols
    unit, part = zbox.shape[1], sbox.shape[1]
    shared_lines = cols * unit

    side, place, places = row % 2, row // 2, peers // 2
    beside = (row + 1 - 2 * side, col)

    def along(by):
        return (((place + by) % places) * 2 + side, col)

    barrier = pltpu.get_barrier_semaphore()
    greeted = [beside]
    greeted += [along(by) for by in range(1, places)]
    greeted += [(row, (col + by) % cols) for by in range(1, cols)]
    for to in greeted:
        pl.semaphore_signal(barrier, inc=1, device_id=to, device_id_type=MESH)

    sizes = [value.shape for value in shared]
    shared_plan = line_plan(sizes, unit)
    thin = [(value.shape[0], value.shape[1] // shards) for value in split]
    split_plan = line_plan(thin, part)
    flat[...] = jnp.zeros(flat.shape, BRAIN)
    for at, rows, lanes, index, lines in shared_plan:
        begin, owner = index % cols * unit, index // cols
        flat[owner % 2, owner // 2, begin + lines.start : begin + lines.stop] = shared[at][
            rows, lanes
        ].astype(BRAIN)
    for turn in range(shards):
        for at, rows, lanes, index, lines in split_plan:
            begin = shared_lines + turn * part
            skip = turn * thin[at][1]
            flat[index % 2, index // 2, begin + lines.start : begin + lines.stop] = split[at][
                rows, skip + lanes.start : skip + lanes.stop
            ].astype(BRAIN)
    pl.semaphore_wait(barrier, len(greeted))

    paired = remote(flat.at[1 - side], beside_in, beside_sems, 0, beside)
    paired.start()
    mine = pl.ds(pl.multiple_of(col * own, own), own)
    for layer in range(layers):
        for at in range(cols):
            leaving[layer, at] = streams[layer][:, at * piece : (at + 1) * piece].astype(BRAIN)
    states = []
    for by in range(1, cols):
        to = (col + by) % cols
        for layer in range(layers):
            slot = layer * (cols - 1) + by - 1
            there = states_out.at[layer, mine]
            copy = remote(leaving.at[layer, to], there, state_sems, slot, (row, to))
            states.append(copy)
    for layer in range(layers):
        states_out[layer, mine] = leaving[layer, col]
    pair = remote(other_part, received, pair_sems, 0, (row, col + 1 - 2 * (col % 2)))
    pair.start()
    for copy in states:
        copy.start()
    paired.wait()

    def add_pair(at, nothing):
        both[at] = (flat[side, at].astype(FLOAT) + beside_in[at].astype(FLOAT)).astype(BRAIN)
        return nothing

    lax.fori_loop(0, places, add_pair, 0)
    scattered = []
    for by in range(1, places):
        to = (place + by) % places
        copy = remote(both.at[to], inbox.at[by - 1], row_sems, by - 1, along(by))
        copy.start()
        scattered.append(copy)
    pair.wait()

    def norm_rows(at, nothing):
        lines = pl.ds(pl.multiple_of(at * 16, 16), 16)
        value = stream[lines]
        scale = lax.rsqrt(jnp.mean(value * value, axis=1, keepdims=True) + EPSILON)
        gained = (own_part[lines] + received[lines].astype(FLOAT)) * gain[...]
        total = jnp.mean(gained * value, axis=1, keepdims=True)
        result = d_middle[lines] + scale * gained - value * (scale * scale * scale * total)
        for to in range(cols):
            outgoing[to, lines] = result[:, to * piece : (to + 1) * piece].astype(BRAIN)
        return nothing

    lax.fori_loop(0, own // 16, norm_rows, 0)
    for copy in scattered:
        copy.wait()
    total = both[place].astype(FLOAT)
    for by in range(1, places):
        total = total + inbox[by - 1].astype(FLOAT)
    for at in range(cols):
        red[at] = total[at * unit : (at + 1) * unit].astype(BRAIN)
    for turn in range(shards):
        begin = shared_lines + turn * part
        red_split[turn] = total[begin : begin + part].astype(BRAIN)

    copies = []
    for by in range(1, cols):
        to = (col + by) % cols
        copies.append(remote(red.at[to], zbox.at[by - 1], col_sems, by - 1, (row, to)))
    for turn in range(1, shards):
        to = (col + 2 * turn) % cols
        copies.append(remote(red_split.at[turn], sbox.at[turn - 1], turn_sems, turn - 1, (row, to)))
    for copy in copies:
        copy.start()
    for copy in copies:
        copy.wait()
    total = red[col].astype(FLOAT)
    for by in range(1, cols):
        total = total + zbox[by - 1].astype(FLOAT)
    zfull[col] = total.astype(BRAIN)
    total = red_split[0].astype(FLOAT)
    for turn in range(1, shards):
        total = total + sbox[turn - 1].astype(FLOAT)
    sfull[...] = total.astype(BRAIN)

    spread = []
    for by in range(1, cols):
        to = (col + by) % cols
        copy = remote(zfull.at[col], zfull.at[col], spread_sems, by - 1, (row, to))
        copy.start()
        spread.append(copy)
    last = []
    for by in range(1, places):
        copy = remote(sfull, split_all.at[side, place], split_sems, by - 1, along(by))
        copy.start()
        last.append(copy)
    split_all[side, place] = sfull[...]
    for copy in spread:
        copy.wait()
    for by in range(1, places):
        copy = remote(zfull, shared_all.at[side, place], shared_sems, by - 1, along(by))
        copy.start()
        last.append(copy)
    shared_all[side, place] = zfull[...]
    returned = []
    for by in range(1, cols):
        to = (col + by) % cols
        copy = remote(outgoing.at[to], homing.at[col], token_sems, by - 1, (row, to))
        copy.start()
        returned.append(copy)
    homing[col] = outgoing[col]
    for copy in last:
        copy.wait()
    lanes_over = [
        remote(split_all.at[side], split_all.at[side], beside_sems, 1, beside),
        remote(shared_all.at[side], shared_all.at[side], beside_sems, 2, beside),
    ]
    for copy in lanes_over:
        copy.start()
    for copy in lanes_over:
        copy.wait()
    for at, rows, lanes, index, lines in shared_plan:
        owner = index // cols
        shared_out[at][rows, lanes] = shared_all[
            owner % 2, owner // 2, index % cols, lines
        ].astype(FLOAT)
    for at, rows, lanes, index, lines in split_plan:
        split_out[at][rows, lanes] = split_all[index % 2, index // 2, lines].astype(FLOAT)
    for copy in returned + states:
        copy.wait()
    for at in range(cols):
        tokens_out[at * own : (at + 1) * own] = homing[at].astype(FLOAT)


def close(streams, own_part, other_part, stream, d_middle, gain, shared, split):
    peers, cols = lax.axis_size("row"), lax.axis_size("col")
    shards = cols // 2
    own, d_model = stream.shape
    pieces = [value.shape[1] // shards for value in split]

    def widened(value):
        cut = value.reshape(value.shape[0], shards, -1)
        short = -cut.shape[2] % LANES
        return jnp.pad(cut, ((0, 0), (0, 0), (0, short))).reshape(value.shape[0], -1)

    split = [widened(value) if piece % LANES else value for value, piece in zip(split, pieces)]
    shared_sizes = [value.shape for value in shared]
    split_sizes = [value.shape for value in split]
    places = peers // 2
    unit, part = closing_sizes(shared_sizes, split_sizes, peers, cols, shards)
    lines = cols * unit + shards * part
    sems = [
        pltpu.SemaphoreType.DMA((2, count))
        for count in (1, 3, places - 1, cols - 1, max(shards - 1, 1), cols - 1, places - 1,
                      places - 1, cols - 1)
    ]
    result = block_call(
        partial(closing_kernel, len(shared), len(streams)),
        2,
        [*streams, own_part, other_part, stream, d_middle, gain, *shared, *split],
        [((own * cols, d_model // cols), FLOAT)]
        + [((len(streams), own * cols, d_model // cols), BRAIN)]
        + [(size, FLOAT) for size in shared_sizes]
        + [((rows, columns // shards), FLOAT) for rows, columns in split_sizes],
        [
            pltpu.VMEM((own, d_model), BRAIN),
            pltpu.VMEM((cols, own, d_model // cols), BRAIN),
            pltpu.VMEM((cols, own, d_model // cols), BRAIN),
            pltpu.VMEM((2, places, lines, LANES), BRAIN),
            pltpu.VMEM((places, lines, LANES), BRAIN),
            pltpu.VMEM((places, lines, LANES), BRAIN),
            pltpu.VMEM((places - 1, lines, LANES), BRAIN),
            pltpu.VMEM((cols, unit, LANES), BRAIN),
            pltpu.VMEM((shards, part, LANES), BRAIN),
            pltpu.VMEM((cols - 1, unit, LANES), BRAIN),
            pltpu.VMEM((max(shards - 1, 1), part, LANES), BRAIN),
            pltpu.VMEM((cols, unit, LANES), BRAIN),
            pltpu.VMEM((part, LANES), BRAIN),
            pltpu.VMEM((2, places, cols, unit, LANES), BRAIN),
            pltpu.VMEM((2, places, part, LANES), BRAIN),
        ]
        + sems
        + [
            pltpu.VMEM((len(streams), cols, own, d_model // cols), BRAIN),
            pltpu.SemaphoreType.DMA((2, len(streams) * (cols - 1))),
        ],
        80,
    )
    count = len(shared)
    split = [value[:, :piece] for value, piece in zip(result[2 + count :], pieces)]
    return result[0], result[1], result[2 : 2 + count], split


PARTS = 3


def routes_of(pack_width, parts, source, target, begin=0):
    shards = lax.axis_size("col") // 2
    piece = pack_width // PARTS
    return [
        (source, part * piece, piece, target, ((part - begin) * shards + shard) * piece, shard)
        for part in parts
        for shard in range(shards)
    ]


def shipped(routes, sources, targets, sems):
    cols = lax.axis_size("col")
    row, col = lax.axis_index("row"), lax.axis_index("col")
    copies = []
    for slot, (source, begin, width, target, place, shard) in enumerate(routes):
        held = sources[source].at[:, pl.ds(begin, width)]
        there = targets[target].at[:, pl.ds(place, width)]
        if shard:
            to = (row, (col + cols - 2 * shard) % cols)
            copies.append(remote(held, there, sems, slot, to))
        else:
            copies.append(pltpu.make_async_copy(held, there, sems.at[0, slot]))
    return copies


def opening_kernel(
    routes, tokens, gains, vectors, pack,
    tokens_out, gains_out, vectors_out, packs_out,
    token_got, token_sems, gain_sems, vector_sems, pack_sems,
):
    cols = lax.axis_size("col")
    shards = cols // 2
    row, col = lax.axis_index("row"), lax.axis_index("col")
    own, piece = tokens_out.shape[0], tokens.shape[1]
    barrier = pltpu.get_barrier_semaphore()
    for by in range(1, cols):
        pl.semaphore_signal(barrier, inc=1, device_id=(row, (col + by) % cols), device_id_type=MESH)
    pl.semaphore_wait(barrier, cols - 1)
    copies = shipped(routes, [pack], [packs_out], pack_sems)
    for turn in range(1, shards):
        to = (row, (col + cols - 2 * turn) % cols)
        copies.append(remote(vectors, vectors_out.at[turn], vector_sems, turn - 1, to))
    for by in range(1, cols):
        to = (col + by) % cols
        there = pl.ds(pl.multiple_of(to * own, own), own)
        copies.append(remote(tokens.at[there], token_got.at[col], token_sems, by - 1, (row, to)))
        copies.append(remote(gains, gains_out.at[col], gain_sems, by - 1, (row, to)))
    for copy in copies:
        copy.start()
    token_got[col] = tokens[pl.ds(pl.multiple_of(col * own, own), own)]
    gains_out[col] = gains[...]
    vectors_out[0] = vectors[...]
    for copy in copies:
        copy.wait()
    for at in range(cols):
        tokens_out[:, at * piece : (at + 1) * piece] = token_got[at]


def open_up(ident, tokens, gains, vectors, pack):
    cols = lax.axis_size("col")
    shards = cols // 2
    rows, piece = tokens.shape
    own = rows // cols
    routes = routes_of(pack.shape[1], range(PARTS), 0, 0)
    outs = [
        ((own, piece * cols), BRAIN),
        ((cols,) + gains.shape, FLOAT),
        ((shards,) + vectors.shape, FLOAT),
        ((pack.shape[0], pack.shape[1] * shards), BRAIN),
    ]
    sizes = (cols - 1, cols - 1, max(shards - 1, 1), len(routes))
    scratch = [pltpu.VMEM((cols, own, piece), BRAIN)]
    scratch += [pltpu.SemaphoreType.DMA((2, size)) for size in sizes]
    return block_call(
        partial(opening_kernel, routes), ident, [tokens, gains, vectors, pack], outs, scratch, 30,
        anywhere=1,
    )


def settling_kernel(count, routes, *refs):
    normed, small, pack, refs = refs[0], refs[1 : 1 + count], refs[1 + count], refs[2 + count :]
    full_out, small_out, packs_out, refs = refs[0], refs[1 : 1 + count], refs[1 + count], refs[2 + count :]
    flat, got, others, pair_sems, across_sems, spread_sems, pack_sems = refs
    peers, cols = lax.axis_size("row"), lax.axis_size("col")
    shards = cols // 2
    row, col = lax.axis_index("row"), lax.axis_index("col")
    own = normed.shape[0]
    plan = line_plan([value.shape for value in small], flat.shape[1])
    peer = (row, col + 1 - 2 * (col % 2))
    signals = [peer] + [(row, (col + 2 * turn) % cols) for turn in range(1, shards)]
    signals += [((row + by) % peers, col) for by in range(1, peers)]
    barrier = pltpu.get_barrier_semaphore()
    for to in signals:
        pl.semaphore_signal(barrier, inc=1, device_id=to, device_id_type=MESH)
    flat[...] = jnp.zeros(flat.shape, BRAIN)
    for at, rows, lanes, index, lines in plan:
        flat[index, lines] = small[at][rows, lanes]
    pl.semaphore_wait(barrier, len(signals))

    across = []
    for turn in range(1, shards):
        to = (row, (col + cols - 2 * turn) % cols)
        across.append(remote(flat.at[row], got.at[turn - 1], across_sems, turn - 1, to))
    pair = remote(normed, full_out.at[pl.ds(own, own)], pair_sems, 0, peer)
    copies = [pair] + shipped(routes, [pack], [packs_out], pack_sems)
    for copy in across + copies:
        copy.start()
    full_out[0:own] = normed[...]
    for at in range(count):
        small_out[at][0] = small[at][...]
    spread = []
    for turn in range(1, shards):
        across[turn - 1].wait()
        for by in range(1, peers):
            to = ((row + by) % peers, col)
            slot = (turn - 1) * (peers - 1) + by - 1
            copy = remote(got.at[turn - 1], others.at[turn - 1, row], spread_sems, slot, to)
            copy.start()
            spread.append(copy)
        others[turn - 1, row] = got[turn - 1]
    for copy in spread:
        copy.wait()
    for turn in range(1, shards):
        for at, rows, lanes, index, lines in plan:
            small_out[at][turn, rows, lanes] = others[turn - 1, index, lines]
    for copy in copies:
        copy.wait()


def settle(ident, normed, small, pack):
    peers, shards = lax.axis_size("row"), lax.axis_size("col") // 2
    rest = max(shards - 1, 1)
    kept = [value.shape[1] for value in small]
    small = [
        jnp.pad(value, ((0, 0), (0, -value.shape[1] % LANES))) if value.shape[1] % LANES else value
        for value in small
    ]
    lines = sum(value.shape[0] * value.shape[1] for value in small) // LANES
    unit = -(-lines // (peers * 16)) * 16
    own, d_model = normed.shape
    routes = routes_of(pack.shape[1], range(PARTS), 0, 0)
    outs = [((2 * own, d_model), BRAIN)]
    outs += [((shards,) + value.shape, BRAIN) for value in small]
    outs += [((pack.shape[0], pack.shape[1] * shards), BRAIN)]
    scratch = [
        pltpu.VMEM((peers, unit, LANES), BRAIN),
        pltpu.VMEM((rest, unit, LANES), BRAIN),
        pltpu.VMEM((rest, peers, unit, LANES), BRAIN),
    ]
    sizes = (1, rest, rest * (peers - 1), len(routes))
    scratch += [pltpu.SemaphoreType.DMA((2, size)) for size in sizes]
    full, *values, packs = block_call(
        partial(settling_kernel, len(small), routes), ident, [normed, *small, pack], outs, scratch,
        40, anywhere=1,
    )
    return full, [value[:, :, :size] for value, size in zip(values, kept)], packs


TILE = 256
LINES = 64


def turn_kernel(backward, lefts, offset, plan, sources, counts, routes, *refs):
    xs, refs = refs[:lefts], refs[lefts:]
    (wide, x2, w2, stream, gain, d_stream, factor, mask), refs = refs[:8], refs[8:]
    extra, refs = refs[:sources], refs[sources:]
    cargo, refs = refs[: counts[0]], refs[counts[0] :]
    (new_out, full_out, low_out), refs = refs[:3], refs[3:]
    grad_outs, refs = refs[: len(plan)], refs[len(plan) :]
    cargo_outs, refs = refs[: counts[1]], refs[counts[1] :]
    weights, sending, received, mine, weight_sems, share_sems, spread_sems, cargo_sems = refs
    cols = lax.axis_size("col")
    shards = cols // 2
    own = stream.shape[0]
    depths = [x.shape[1] for x in xs]
    depth = sum(depths)
    tiles = sending.shape[0]
    row, col = lax.axis_index("row"), lax.axis_index("col")
    peer = (row, col + 1 - 2 * (col % 2))

    barrier = pltpu.get_barrier_semaphore()
    greeted = [peer]
    if any(route[-1] for route in routes):
        greeted += [(row, (col + 2 * other) % cols) for other in range(1, shards)]
    for to in greeted:
        pl.semaphore_signal(barrier, inc=1, device_id=to, device_id_type=MESH)

    def weight_copy(tile):
        lines = pl.ds(pl.multiple_of(tile * TILE, TILE), TILE)
        return pltpu.make_async_copy(
            wide.at[lines, pl.ds(offset, depth)], weights.at[tile], weight_sems.at[tile]
        )

    def share_copy(tile):
        return remote(sending.at[tile], received.at[tile], share_sems, tile, peer)

    def spread_copy(at):
        lines = pl.multiple_of(at * LINES, LINES)
        return pltpu.make_async_remote_copy(
            src_ref=full_out.at[pl.ds(lines, LINES)],
            dst_ref=full_out.at[pl.ds(pl.multiple_of(own + lines, LINES), LINES)],
            send_sem=spread_sems.at[0, at],
            recv_sem=spread_sems.at[1, at],
            device_id=peer,
            device_id_type=MESH,
        )

    def begin(tile, nothing):
        weight_copy(tile).start()
        return nothing

    lax.fori_loop(0, tiles, begin, 0)
    pl.semaphore_wait(barrier, len(greeted))
    carried = shipped(routes, cargo, cargo_outs, cargo_sems)
    for copy in carried:
        copy.start()

    def project(tile, nothing):
        weight_copy(tile).wait()
        at = pl.ds(pl.multiple_of(tile * TILE, TILE), TILE)
        total = nn(x2[...], w2[:, at])
        begin = 0
        for x, size in zip(xs, depths):
            total = total + nt(x[...], weights[tile, :, begin : begin + size])
            begin += size
        sending[tile] = total[own:].astype(BRAIN)
        mine[tile] = total[:own]
        share_copy(tile).start()
        return nothing

    lax.fori_loop(0, tiles, project, 0)

    def gradients(part):
        for (left, right), out in part:
            out[...] = tn(extra[left][...], (*extra, *xs)[right][...])

    pairs = list(zip(plan, grad_outs))
    gradients(pairs[: len(pairs) // 2])

    def arrive(tile, nothing):
        share_copy(tile).wait()
        return nothing

    lax.fori_loop(0, tiles, arrive, 0)

    def finish(at, nothing):
        lines = pl.ds(pl.multiple_of(at * LINES, LINES), LINES)
        total = jnp.concatenate(
            [mine[tile, lines] + received[tile, lines].astype(FLOAT) for tile in range(tiles)],
            axis=1,
        )
        value = stream[lines]
        if backward:
            scale = lax.rsqrt(jnp.mean(value * value, axis=1, keepdims=True) + EPSILON)
            gained = total * gain[...]
            shift = jnp.mean(gained * value, axis=1, keepdims=True)
            result = d_stream[lines] + scale * gained - value * (scale * scale * scale * shift)
            new_out[lines] = result
            full_out[lines] = result.astype(BRAIN)
        else:
            result = value + total
            scale = lax.rsqrt(jnp.mean(result * result, axis=1, keepdims=True) + EPSILON)
            new_out[lines] = result
            full_out[lines] = (result * scale * gain[...]).astype(BRAIN)
        spread_copy(at).start()
        return nothing

    lax.fori_loop(0, own // LINES, finish, 0)
    gradients(pairs[len(pairs) // 2 :])

    def lower(lines):
        low_out[lines] = (nt(full_out[lines], factor[...]) * mask[lines]).astype(BRAIN)

    lower(slice(0, own))

    def leave(at, nothing):
        spread_copy(at).wait()
        return nothing

    lax.fori_loop(0, own // LINES, leave, 0)
    lower(slice(own, 2 * own))
    for copy in carried:
        copy.wait()


def turn(
    ident, xs, wide, offset, x2, w2, stream, gain, factor, mask, d_stream=None, extra=(), plan=(),
    cargo=(), widths=(), routes=(),
):
    own, d_model = stream.shape
    depth = sum(x.shape[1] for x in xs)
    tiles = d_model // TILE
    whole = pl.BlockSpec(memory_space=pltpu.VMEM)
    backward = d_stream is not None
    operands = [*xs, wide, x2, w2, stream, gain, d_stream if backward else gain, factor, mask]
    operands += extra
    specs = [whole] * len(operands)
    anywhere = pl.BlockSpec(memory_space=pl.ANY)
    specs[len(xs)] = anywhere
    operands += cargo
    specs += [anywhere] * len(cargo)
    plan = tuple(plan)
    sizes = []
    for left, right in plan:
        sizes.append((extra[left].shape[1], [*extra, *xs][right].shape[1]))
    return pl.pallas_call(
        partial(turn_kernel, backward, len(xs), offset, plan, len(extra), (len(cargo), len(widths)), tuple(routes)),
        out_shape=[
            jax.ShapeDtypeStruct((own, d_model), FLOAT),
            jax.ShapeDtypeStruct((2 * own, d_model), BRAIN),
            jax.ShapeDtypeStruct((2 * own, factor.shape[0]), BRAIN),
        ]
        + [jax.ShapeDtypeStruct(size, FLOAT) for size in sizes]
        + [jax.ShapeDtypeStruct((cargo[0].shape[0], size), cargo[0].dtype) for size in widths],
        in_specs=specs,
        out_specs=[whole] * (3 + len(plan)) + [anywhere] * len(widths),
        scratch_shapes=[
            pltpu.VMEM((tiles, TILE, depth), BRAIN),
            pltpu.VMEM((tiles, own, TILE), BRAIN),
            pltpu.VMEM((tiles, own, TILE), BRAIN),
            pltpu.VMEM((tiles, own, TILE), FLOAT),
            pltpu.SemaphoreType.DMA((tiles,)),
            pltpu.SemaphoreType.DMA((2, tiles)),
            pltpu.SemaphoreType.DMA((2, own // LINES)),
            pltpu.SemaphoreType.DMA((2, max(len(routes), 1))),
        ],
        cost_estimate=lasting(40),
        compiler_params=pltpu.CompilerParams(
            vmem_limit_bytes=VMEM_BYTES, collective_id=ident, has_side_effects=True
        ),
    )(*operands)


def partner(value):
    peers = lax.axis_size("col")
    return lax.ppermute(value, "col", [(at, at ^ 1) for at in range(peers)])


def from_shard(value, turn):
    peers = lax.axis_size("col")
    return lax.ppermute(value, "col", [((at + 2 * turn) % peers, at) for at in range(peers)])


def to_shard(value, turn):
    peers = lax.axis_size("col")
    return lax.ppermute(value, "col", [(at, (at + 2 * turn) % peers) for at in range(peers)])


def all_shards(value):
    return [value] + [from_shard(value, turn) for turn in range(1, lax.axis_size("col") // 2)]


def after(value, anchor):
    return lax.optimization_barrier((value, anchor))[0] if jax.tree.leaves(anchor) else value


def to_sequence(value):
    return lax.all_to_all(value, "col", split_axis=0, concat_axis=1, tiled=True)


def half_share(own, other):
    return own + partner(other.astype(BRAIN)).astype(FLOAT)


def norm_forward(stream, gain):
    scale = lax.rsqrt(jnp.mean(stream * stream, axis=1, keepdims=True) + EPSILON)
    return scale, (stream * scale * gain[None, :]).astype(BRAIN)


def masked(value, pick):
    return (value * pick).astype(BRAIN)


def recur_branch(normed_full, low, wide, small, ctx):
    ranks = ctx["pick"].shape[1]
    width = wide.shape[1] // 3
    inner = [low[:, b * ranks : (b + 1) * ranks] for b in range(2)]
    branch = nn(normed_full, wide[:, : 2 * width])
    lead = branch[:, :width] + nn(inner[0], small["inlet_upper"][0])
    gate = branch[:, width:] + nn(inner[1], small["inlet_upper"][1])
    return lead, gate, inner


def recur_part(
    ident, stream, lead, gate, wide, small, gain, factor, ctx, ready, cargo, widths, routes
):
    pick, offset = ctx["pick"], ctx["offset"]
    width = lead.shape[1]
    conv, decay, hidden, mixed, state_in = recur_forward(lead, gate, offset, small)
    mixed = after(mixed, ready)
    lowrank = masked(nt(mixed, small["outlet_lower"]), pick)
    middle, normed_two_full, low_two, *parts = turn(
        ident, [mixed], wide, 2 * width, lowrank, small["outlet_upper"], stream, gain, factor,
        ctx["picks"], cargo=cargo, widths=widths, routes=routes,
    )
    kept = dict(
        conv=conv, decay=decay, hidden=hidden, state_in=state_in, mixed=mixed, lowrank=lowrank,
        middle=middle, normed_two_full=normed_two_full,
    )
    return middle, normed_two_full, low_two, kept, parts


def hidden_part(normed_two_full, low_two, wide, small, ctx):
    pick = ctx["pick"]
    ranks = pick.shape[1]
    spread = wide.shape[1] // 3
    inner_two = [low_two[:, b * ranks : (b + 1) * ranks] for b in range(2)]
    branch_two = nn(normed_two_full, wide[:, : 2 * spread])
    up_gate = branch_two[:, :spread] + nn(inner_two[0], small["expand_upper"][0])
    up_value = branch_two[:, spread:] + nn(inner_two[1], small["expand_upper"][1])
    value, slope = gelu_pair(up_gate)
    product = (value * up_value).astype(BRAIN)
    factors = [(slope * up_value).astype(BRAIN), value.astype(BRAIN)]
    lowrank_two = masked(nt(product, small["shrink_lower"]), pick)
    return dict(
        inner_two=inner_two, factors=factors, product=product, lowrank_two=lowrank_two,
    )


def layer_backward(
    ident, d_stream, d_out, d_low_two, wide, small, upper_before, gains, kept, ctx, pending
):
    recur_wide, hidden_wide = wide
    pick, offset = ctx["pick"], ctx["offset"]
    own = d_stream.shape[0]
    rows = 2 * own
    width = recur_wide.shape[1] // 3
    spread = hidden_wide.shape[1] // 3

    d_product = nn(d_out, hidden_wide[:, 2 * spread :]) + nn(d_low_two, small["shrink_lower"])
    d_branch_two = [(part.astype(FLOAT) * d_product).astype(BRAIN) for part in kept["factors"]]
    d_inner_two = jnp.concatenate(
        [masked(nt(d_branch_two[b], small["expand_upper"][b]), pick) for b in range(2)], axis=1
    )
    d_middle, d_mid, d_low, shrink_upper, shrink_lower, expand_lower, expand_a, expand_b = turn(
        ident, d_branch_two, hidden_wide, 0, d_inner_two, small["expand_lower"], kept["middle"],
        gains[1:2], small["outlet_upper"], pick, d_stream,
        [kept["lowrank_two"], d_out, d_low_two, kept["product"], d_inner_two,
         kept["normed_two_full"], *kept["inner_two"]],
        [(0, 1), (2, 3), (4, 5), (6, 8), (7, 9)],
    )
    expand_upper = jnp.concatenate([expand_a, expand_b], axis=0)

    if pending is not None:
        d_mid, ctx["last"] = lax.optimization_barrier((d_mid, pending))
    d_mixed = nn(d_mid, recur_wide[:, 2 * width :]) + nn(d_low, small["outlet_lower"])
    d_branch = recur_backward(d_mixed, kept, offset, small)
    d_inner = jnp.concatenate(
        [masked(nt(d_branch[b], small["inlet_upper"][b]), pick) for b in range(2)], axis=1
    )
    if upper_before is None:
        outlet_upper = tn(kept["lowrank"], d_mid)
        outlet_lower = tn(d_low, kept["mixed"])
        inlet_lower = tn(d_inner, kept["normed_full"])
        inlet_a, inlet_b = (tn(kept["inner"][b], d_branch[b]) for b in range(2))
        result = tuple(
            nt(d_branch[0][part], recur_wide[:, :width])
            + nt(d_branch[1][part], recur_wide[:, width : 2 * width])
            + nn(d_inner[part], small["inlet_lower"])
            for part in (slice(0, own), slice(own, rows))
        )
    else:
        *result, outlet_upper, outlet_lower, inlet_lower, inlet_a, inlet_b = turn(
            ident + 1, d_branch, recur_wide, 0, d_inner, small["inlet_lower"], kept["stream"],
            gains[0:1], upper_before, pick, d_middle,
            [kept["lowrank"], d_mid, d_low, kept["mixed"], d_inner, kept["normed_full"],
             *kept["inner"]],
            [(0, 1), (2, 3), (4, 5), (6, 8), (7, 9)],
        )
    inlet_upper = jnp.concatenate([inlet_a, inlet_b], axis=0)
    shared = (inlet_lower, outlet_upper, expand_lower, shrink_upper)
    split = (inlet_upper, outlet_lower, expand_upper, shrink_lower)
    return d_middle, result, shared, split


def local(
    tokens, cotangent, adapter_ids, doc_lengths, norm_gain, inlet_weight, inlet_lower, inlet_upper,
    conv_weight, conv_bias, gate_weight, gate_bias, decay_param, outlet_weight, outlet_lower,
    outlet_upper, expand_weight, expand_lower, expand_upper, shrink_weight, shrink_lower,
    shrink_upper,
):
    row_at, col_at = lax.axis_index("row"), lax.axis_index("col")
    cols = lax.axis_size("col")
    shards = cols // 2
    rows = tokens.shape[0]
    own = rows // cols
    block = 2 * own
    docs = adapter_ids.shape[0]
    adapters, rank = inlet_lower.shape[3:]
    part_width, part_spread = inlet_weight.shape[3], expand_weight.shape[3]
    d_model = inlet_lower.shape[1]

    parity = (col_at % 2).astype(jnp.int32)
    ends = jnp.cumsum(doc_lengths)
    starts = ends - doc_lengths
    ordered = row_at * rows + (col_at // 2) * block + jnp.arange(block, dtype=jnp.int32)
    inside = (ordered[:, None] >= starts[None, :]) & (ordered[:, None] < ends[None, :])
    offset = (ordered - jnp.sum(jnp.where(inside, starts[None, :], 0), axis=1))[:, None]
    halves = (parity * own, own - parity * own)
    at_home = jnp.concatenate(
        [ordered[0] + begin + jnp.arange(own, dtype=jnp.int32) for begin in halves]
    )
    within = (at_home[:, None] >= starts[None, :]) & (at_home[:, None] < ends[None, :])
    pick = jnp.repeat(within.astype(FLOAT), rank, axis=1)
    picks = jnp.concatenate([pick, pick], axis=1)
    ctx = dict(pick=pick, picks=picks, offset=offset, pending={})


    def by_doc(factor, axis):
        return jnp.concatenate(
            [lax.dynamic_slice_in_dim(factor, adapter_ids[at], 1, axis) for at in range(docs)], axis
        )

    def lower_t(factor):
        return by_doc(jnp.moveaxis(factor, 1, -1), factor.ndim - 3)

    def upper_t(factor):
        return by_doc(factor, factor.ndim - 3)

    ranks = docs * rank
    lows = dict(
        inlet_lower=lower_t(inlet_lower).reshape(LAYERS, 2 * ranks, d_model),
        outlet_upper=upper_t(outlet_upper).reshape(LAYERS, ranks, d_model),
        expand_lower=lower_t(expand_lower).reshape(LAYERS, 2 * ranks, d_model),
        shrink_upper=upper_t(shrink_upper).reshape(LAYERS, ranks, d_model),
    )
    narrow_own = jnp.concatenate(
        [
            upper_t(inlet_upper).reshape(LAYERS, 2 * ranks, part_width),
            lower_t(outlet_lower).reshape(LAYERS, ranks, part_width),
        ],
        axis=1,
    )
    broad_own = jnp.concatenate(
        [
            upper_t(expand_upper).reshape(LAYERS, 2 * ranks, part_spread),
            lower_t(shrink_lower).reshape(LAYERS, ranks, part_spread),
        ],
        axis=1,
    )
    vectors_own = jnp.concatenate(
        [conv_weight, gate_bias, conv_bias[:, None], decay_param[:, None]], axis=1
    )

    def rows_of(value):
        return value.reshape(-1, value.shape[-1])

    def packed(pair, single):
        pack = jnp.concatenate([pair[:, 0], pair[:, 1], single], axis=1)
        short = -single.shape[1] % LANES
        if short:
            pack = jnp.pad(pack.reshape(pack.shape[0], PARTS, -1), ((0, 0), (0, 0), (0, short)))
            pack = pack.reshape(pack.shape[0], -1)
        return pack

    def gathered(packs, piece):
        whole = lax.all_gather(packs, "row", axis=0, tiled=True)
        if piece % LANES:
            whole = whole.reshape(whole.shape[0], PARTS * shards, -1)[:, :, :piece]
            whole = whole.reshape(whole.shape[0], -1)
        return whole

    def recur_small(layer, narrow, gates):
        return dict(
            inlet_lower=lows["inlet_lower"][layer],
            inlet_upper=narrow[: 2 * ranks].reshape(2, ranks, -1),
            outlet_lower=narrow[2 * ranks :],
            outlet_upper=lows["outlet_upper"][layer],
            conv_weight=vectors_all[layer, :CONV],
            gate_bias=vectors_all[layer, CONV : CONV + 2],
            conv_bias=vectors_all[layer, CONV + 2 : CONV + 3],
            soft=jax.nn.softplus(vectors_all[layer, CONV + 3 : CONV + 4]),
            gate_weight=gates,
        )

    def hidden_small(layer, broad):
        return dict(
            expand_lower=lows["expand_lower"][layer],
            expand_upper=broad[: 2 * ranks].reshape(2, ranks, -1),
            shrink_lower=broad[2 * ranks :],
            shrink_upper=lows["shrink_upper"][layer],
        )

    saved, wides, smalls = [], [], []
    recur_packs = [packed(inlet_weight[at], outlet_weight[at]) for at in range(LAYERS)]
    hidden_packs = [packed(expand_weight[at], shrink_weight[at]) for at in range(LAYERS)]
    def side_by_side(value):
        return jnp.concatenate([value[at] for at in range(shards)], axis=1)

    def heads_in_turn(value):
        return jnp.concatenate(
            [value[at].reshape((2, -1) + gate_weight.shape[3:]) for at in range(shards)], axis=1
        )

    stream, gains, vectors_all, recur_side = open_up(
        20, tokens, rows_of(norm_gain), rows_of(vectors_own), recur_packs[0]
    )
    gains = jnp.moveaxis(gains, 0, 1).reshape(LAYERS, 2, d_model)
    vectors_all = side_by_side(vectors_all).reshape(LAYERS, -1, shards * part_width)
    wide_one = gathered(recur_side, part_width)
    stream = stream.astype(FLOAT)
    _, normed = norm_forward(stream, gains[0][0])
    small = []
    for layer in range(LAYERS):
        small += [narrow_own[layer], rows_of(gate_weight[layer]), broad_own[layer]]
    normed_full, small, hidden_side = settle(21, normed, small, hidden_packs[0])
    bits = [
        (side_by_side(narrow), heads_in_turn(gates), side_by_side(broad))
        for narrow, gates, broad in zip(small[0::3], small[1::3], small[2::3])
    ]
    wide_two = gathered(hidden_side, part_spread)
    low = masked(nt(normed_full, lows["inlet_lower"][0]), picks)
    for layer in range(LAYERS):
        more_layers = layer + 1 < LAYERS
        kept = dict(stream=stream, normed_full=normed_full)
        narrow, gates, broad = bits[layer]
        small_one = recur_small(layer, narrow, gates)
        lead, gate, inner = recur_branch(normed_full, low, wide_one, small_one, ctx)
        ready, cargo, widths, routes = [], [], [], []
        if more_layers:
            packs = all_shards(after(recur_packs[layer + 1], normed_full))
            lead, packs[1:] = lax.optimization_barrier((lead, packs[1:]))
            cargo = [*packs, hidden_packs[layer + 1]]
            piece, spread_piece = (value.shape[1] // PARTS for value in cargo[-2:])
            widths = [PARTS * shards * piece, shards * spread_piece]
            routes = [
                (at, part * piece, piece, 0, (part * shards + at) * piece, 0)
                for part in range(PARTS)
                for at in range(shards)
            ] + routes_of(PARTS * spread_piece, [0], shards, 1)
        elif layer:
            ending = to_sequence(after(cotangent, lead))
            ready = [ending]
        middle, normed_two_full, low_two, more, sides = recur_part(
            3 + 2 * layer, stream, lead, gate, wide_one, small_one, gains[layer][1:2],
            lows["expand_lower"][layer], ctx, ready, cargo, widths, routes,
        )
        kept.update(inner=inner, gate=gate, **more)
        if more_layers:
            wide_next = gathered(sides[0], part_width)
            others = all_shards(after(hidden_packs[layer + 1][:, spread_piece:], middle))[1:]
        small_two = hidden_small(layer, broad)
        more = hidden_part(normed_two_full, low_two, wide_two, small_two, ctx)
        kept.update(more)
        wides.append((wide_one, wide_two))
        smalls.append({**small_one, **small_two})
        saved.append(kept)
        product, lowrank, upper = more["product"], more["lowrank_two"], small_two["shrink_upper"]
        spread = product.shape[1]
        if more_layers:
            product, others, kept["factors"] = lax.optimization_barrier(
                (product, others, more["factors"])
            )
            cargo = [hidden_packs[layer + 1], *others, sides[1]]
            routes = [
                (at, (part - (at > 0)) * spread_piece, spread_piece, 0,
                 (part * shards + at) * spread_piece, 0)
                for part in range(1, PARTS)
                for at in range(shards)
            ] + [(shards, 0, shards * spread_piece, 0, 0, 0)]
            stream, normed_full, low, hidden_side = turn(
                4 + 2 * layer, [product], wide_two, 2 * spread, lowrank, upper, middle,
                gains[layer + 1][0:1], lows["inlet_lower"][layer + 1], ctx["picks"], cargo=cargo, widths=[PARTS * shards * spread_piece],
                routes=routes,
            )
            wide_two_next = gathered(hidden_side, part_spread)
            wide_one, wide_two = wide_next, wide_two_next
        else:
            shrink = wide_two[:, 2 * spread :]
            parts = [
                nt(product[part], shrink) + nn(lowrank[part], upper)
                for part in (slice(0, own), slice(own, 2 * own))
            ]
            stream = middle + half_share(*parts)
            last_stream = stream
    ctx["pending"] = {LAYERS - 1: last_stream}
    d_out = jnp.concatenate(
        [ending, after(partner(after(ending, normed_two_full)), product)], axis=0
    )
    d_stream = ending.astype(FLOAT)
    d_low_two = masked(nt(d_out, smalls[-1]["shrink_upper"]), pick)
    shared_parts, split_parts = [], []
    for layer in reversed(range(LAYERS)):
        kept = saved[layer]
        d_middle, result, shared_more, split_more = layer_backward(
            3 + 2 * LAYERS + 2 * layer, d_stream, d_out, d_low_two, wides[layer], smalls[layer],
            lows["shrink_upper"][layer - 1] if layer else None, gains[layer], kept, ctx,
            ctx["pending"].get(layer),
        )
        shared_parts = [*shared_more, *shared_parts]
        split_parts = [*split_more, *split_parts]
        if layer:
            d_stream, d_out, d_low_two = result
    tokens_grad, states, shared_parts, split_parts = close(
        [*(kept["stream"] for kept in saved[1:]), ctx["last"]], result[0], result[1].astype(BRAIN), kept["stream"], d_middle, gains[0][:1], shared_parts,
        split_parts,
    )
    inlet_low, outlet_up, expand_low, shrink_up = (
        jnp.stack(shared_parts[at::4]) for at in range(4)
    )
    inlet_up, outlet_low, expand_up, shrink_low = (jnp.stack(split_parts[at::4]) for at in range(4))
    spread_out = (adapter_ids[None, :] == jnp.arange(adapters, dtype=jnp.int32)[:, None])

    def by_adapter(grad, count):
        grad = grad.reshape(LAYERS, count, docs, rank, -1)
        total = 0.0
        for doc in range(docs):
            total = total + jnp.where(
                spread_out[None, None, :, doc, None, None], grad[:, :, doc][:, :, None], 0.0
            )
        return total

    def lower_out(grad, count):
        grad = by_adapter(grad, count)
        if count == 1:
            grad = grad[:, 0]
        return jnp.moveaxis(grad, -1, 1)

    return (
        states,
        tokens_grad,
        lower_out(inlet_low, 2),
        by_adapter(inlet_up, 2),
        lower_out(outlet_low, 1),
        by_adapter(outlet_up, 1)[:, 0],
        lower_out(expand_low, 2),
        by_adapter(expand_up, 2),
        lower_out(shrink_low, 1),
        by_adapter(shrink_up, 1)[:, 0],
    )


def solution(mesh):
    return jax.shard_map(
        local,
        mesh=mesh,
        in_specs=(
            P("row", "col"),
            P("row", "col"),
            P(),
            P(),
            P(None, None, "col"),
            P(None, "row", None, "col"),
            P(),
            P(None, None, None, None, "col"),
            P(None, None, "col"),
            P(None, "col"),
            P(None, None, "col", None, None),
            P(None, None, "col"),
            P(None, "col"),
            P(None, "row", "col"),
            P(None, "col", None, None),
            P(),
            P(None, "row", None, "col"),
            P(),
            P(None, None, None, None, "col"),
            P(None, "row", "col"),
            P(None, "col", None, None),
            P(),
        ),
        out_specs=(
            P(None, "row", "col"),
            P("row", "col"),
            P(),
            P(None, None, None, None, "col"),
            P(None, "col", None, None),
            P(),
            P(),
            P(None, None, None, None, "col"),
            P(None, "col", None, None),
            P(),
        ),
        check_vma=False,
    )
```

```python
from functools import partial

import jax
import jax.numpy as jnp
from jax import lax
from jax.experimental import pallas as pl
from jax.experimental.pallas import tpu as pltpu
from jax.sharding import PartitionSpec as P

HS = 256
CONV = 4
LAYERS = 2
SEGS = 8

EPSILON = 1e-06
FLOAT = jnp.float32
BRAIN = jnp.bfloat16
VMEM_BYTES = 48 * 1024 * 1024
CURVE = 0.7978845608028654
CUBIC = 0.044715
LANES = 128
SLABS = HS // LANES
MESH = pl.DeviceIdType.MESH


def nn(left, right):
    return lax.dot_general(left, right, (((1,), (0,)), ((), ())), preferred_element_type=FLOAT)


def nt(left, right):
    return lax.dot_general(left, right, (((1,), (1,)), ((), ())), preferred_element_type=FLOAT)


def tn(left, right):
    return lax.dot_general(left, right, (((0,), (0,)), ((), ())), preferred_element_type=FLOAT)


def gelu_tanh(value):
    return 0.5 * value * (1.0 + jnp.tanh(CURVE * (value + CUBIC * value * value * value)))


def gelu_pair(value):
    square = value * value
    bend = jnp.tanh(CURVE * value * (1.0 + CUBIC * square))
    half = 0.5 * (1.0 + bend)
    slope = half + 0.5 * value * (1.0 - bend * bend) * CURVE * (1.0 + 3.0 * CUBIC * square)
    return value * half, slope


def one_less_square(twice, square):
    series = -twice * (
        1.0 + twice * (0.5 + twice * (1.0 / 6.0 + twice * (1.0 / 24.0 + twice * (1.0 / 120.0))))
    )
    return jnp.where(twice > -0.1, series, 1.0 - square)


def gate_values(conv, gate_w, gate_b, soft):
    rate = jax.nn.sigmoid(nn(conv, gate_w[0]) + gate_b[0:1])
    inward = jax.nn.sigmoid(nn(conv, gate_w[1]) + gate_b[1:2])
    log_decay = (-8.0 * soft) * rate
    raw = jnp.exp(log_decay)
    gap = one_less_square(2.0 * log_decay, raw * raw)
    return rate, inward, raw, gap


def chain(axis_row="row", axis_col="col"):
    blocks_in_row = lax.axis_size(axis_col) // 2
    blocks = lax.axis_size(axis_row) * blocks_in_row
    col = lax.axis_index(axis_col)
    side = col % 2
    here = lax.axis_index(axis_row) * blocks_in_row + col // 2

    def device(by):
        block = (here + by + blocks) % blocks
        return (block // blocks_in_row, (block % blocks_in_row) * 2 + side)

    return blocks, blocks_in_row, here, side, device


def greet(blocks, device):
    barrier = pltpu.get_barrier_semaphore()
    for by in range(1, blocks):
        pl.semaphore_signal(barrier, inc=1, device_id=device(by), device_id_type=MESH)
    pl.semaphore_wait(barrier, blocks - 1)


def share_totals(blocks, device, direction, totals, inbox, send_sems, recv_sems):
    copies = [
        pltpu.make_async_remote_copy(
            src_ref=totals,
            dst_ref=inbox.at[by - 1],
            send_sem=send_sems.at[by - 1],
            recv_sem=recv_sems.at[by - 1],
            device_id=device(direction * by),
            device_id_type=MESH,
        )
        for by in range(1, blocks)
    ]
    for copy in copies:
        copy.start()
    for copy in copies:
        copy.wait()


def folded(blocks, shards, ahead, direction, inbox):
    slabs = inbox.shape[1] // 2
    piece = slabs // shards
    state = jnp.zeros((slabs, LANES), FLOAT)
    for by in reversed(range(1, blocks)):
        turn = (direction * by) % shards * piece
        cum, add = (
            jnp.concatenate([part[turn:], part[:turn]], axis=0) if turn else part
            for part in (inbox[by - 1, 0:slabs], inbox[by - 1, slabs : 2 * slabs])
        )
        state = jnp.where(ahead >= by, cum * state + add, state)
    return state


def forward_kernel(
    lead, gate, offset, conv_w, conv_b, gate_w, gate_b, soft,
    conv_out, decay_out, hidden_out, mixed_out, carry_out,
    ext, drive, state_all, cum_all, seg, totals, halo, inbox,
    halo_sems, send_sems, recv_sems,
):
    rows, width = lead.shape
    heads = width // HS
    half = rows // 2
    span = rows // SEGS
    slabs = width // LANES
    blocks, shards, here, side, device = chain()
    start = pl.multiple_of(side * half, half)
    other = pl.multiple_of(half - side * half, half)
    greet(blocks, device)
    rim = pltpu.make_async_remote_copy(
        src_ref=lead.at[pl.ds(pl.multiple_of(other + half - 8, 8), 8)],
        dst_ref=halo,
        send_sem=halo_sems.at[0],
        recv_sem=halo_sems.at[1],
        device_id=device(1),
        device_id_type=MESH,
    )
    rim.start()
    rim.wait()

    def run_head(head, nothing):
        at = pl.ds(pl.multiple_of(head * HS, HS), HS)
        there = (head + heads // shards) % heads
        ext[0:8] = halo[:, pl.ds(pl.multiple_of(there * HS, HS), HS)]
        ext[8 : 8 + half] = lead[pl.ds(start, half), at]
        ext[8 + half : 8 + rows] = lead[pl.ds(other, half), at]
        place = offset[...]
        total = conv_b[:, at] + conv_w[0:1, at] * ext[8 : 8 + rows]
        for step in range(1, CONV):
            valid = (place >= step).astype(FLOAT)
            total = total + conv_w[step : step + 1, at] * ext[8 - step : 8 - step + rows] * valid
        conv = total.astype(BRAIN)
        conv_out[:, at] = conv
        rate, inward, raw, gap = gate_values(
            conv, (gate_w[0, head], gate_w[1, head]), gate_b[:, at], soft[:, at]
        )
        first = (place == 0).astype(FLOAT)
        keep = 1.0 - first
        decay = raw * keep
        pushed = (keep * jnp.sqrt(gap) + first) * inward * conv.astype(FLOAT)
        for slab in range(SLABS):
            decay_out[head * SLABS + slab] = decay[:, slab * LANES : (slab + 1) * LANES]
            drive[slab] = pushed[:, slab * LANES : (slab + 1) * LANES]

        def advance(step, carried):
            where = pl.ds(step, SEGS, stride=span)
            after = []
            for slab, (state, cum) in enumerate(carried):
                rates = decay_out[head * SLABS + slab, where, :]
                state = rates * state + drive[slab, where, :]
                cum = rates * cum
                state_all[head * SLABS + slab, where, :] = state
                cum_all[head * SLABS + slab, where, :] = cum
                after.append((state, cum))
            return tuple(after)

        fresh = (jnp.zeros((SEGS, LANES), FLOAT), jnp.ones((SEGS, LANES), FLOAT))
        ends = lax.fori_loop(0, span, advance, (fresh,) * SLABS, unroll=8)
        for slab, (state, cum) in enumerate(ends):
            run_state = jnp.zeros((1, LANES), FLOAT)
            run_cum = jnp.ones((1, LANES), FLOAT)
            at_slab = head * SLABS + slab
            for part in range(SEGS):
                seg[at_slab, part : part + 1] = run_state
                seg[at_slab, SEGS + part : SEGS + part + 1] = run_cum
                run_state = cum[part : part + 1] * run_state + state[part : part + 1]
                run_cum = cum[part : part + 1] * run_cum
            totals[pl.ds(at_slab, 1)] = run_cum
            totals[pl.ds(slabs + at_slab, 1)] = run_state
        return nothing

    lax.fori_loop(0, heads, run_head, 0)
    share_totals(blocks, device, 1, totals, inbox, send_sems, recv_sems)
    carry_out[...] = folded(blocks, shards, here, 1, inbox)

    def mix_slab(slab, nothing):
        at = pl.ds(pl.multiple_of(slab * LANES, LANES), LANES)
        entering = seg[slab, 0:SEGS] + seg[slab, SEGS : 2 * SEGS] * carry_out[pl.ds(slab, 1)]
        for part in range(SEGS):
            lines = slice(part * span, (part + 1) * span)
            hidden_out[slab, lines] = (
                state_all[slab, lines] + cum_all[slab, lines] * entering[part : part + 1]
            )
        for place, lines in ((start, slice(0, half)), (other, slice(half, rows))):
            mixed_out[pl.ds(place, half), at] = (
                hidden_out[slab, lines] * gelu_tanh(gate[pl.ds(place, half), at])
            ).astype(BRAIN)
        return nothing

    lax.fori_loop(0, slabs, mix_slab, 0)


def backward_kernel(
    grad, gate, hidden, decay, carry, conv, offset, conv_w, gate_w, gate_b, soft,
    lead_grad, gate_grad,
    ext, prior, grads, chain_decay, local_all, reach_all, seg, totals, arriving, heads_out,
    heads_in, tails, inbox, halo_sems, send_sems, recv_sems,
):
    rows, width = grad.shape
    heads = width // HS
    half = rows // 2
    span = rows // SEGS
    slabs = width // LANES
    blocks, shards, here, side, device = chain()
    start = pl.multiple_of(side * half, half)
    other = pl.multiple_of(half - side * half, half)
    greet(blocks, device)

    def run_slab(slab, nothing):
        at = pl.ds(pl.multiple_of(slab * LANES, LANES), LANES)
        for place, lines in ((start, slice(0, half)), (other, slice(half, rows))):
            value, slope = gelu_pair(gate[pl.ds(place, half), at])
            coming = grad[pl.ds(place, half), at]
            grads[lines] = coming * value
            gate_grad[pl.ds(place, half), at] = (
                coming * hidden[slab, lines] * slope
            ).astype(BRAIN)
        chain_decay[0:rows] = decay[slab]
        chain_decay[rows : rows + 8] = jnp.ones((8, LANES), FLOAT)

        def retreat(turn, carried):
            state, cum = carried
            step = span - 1 - turn
            where = pl.ds(step, SEGS, stride=span)
            rates = chain_decay[pl.ds(step + 1, SEGS, stride=span), :]
            state = rates * state + grads[where, :]
            cum = rates * cum
            local_all[slab, where, :] = state
            reach_all[slab, where, :] = cum
            return state, cum

        fresh = (jnp.zeros((SEGS, LANES), FLOAT), jnp.ones((SEGS, LANES), FLOAT))
        state, cum = lax.fori_loop(0, span, retreat, fresh, unroll=8)
        run_state = jnp.zeros((1, LANES), FLOAT)
        run_cum = jnp.ones((1, LANES), FLOAT)
        for part in reversed(range(SEGS)):
            seg[slab, part : part + 1] = run_state
            seg[slab, SEGS + part : SEGS + part + 1] = run_cum
            run_state = cum[part : part + 1] * run_state + state[part : part + 1]
            run_cum = cum[part : part + 1] * run_cum
        opening = chain_decay[0:1]
        totals[pl.ds(slab, 1)] = run_cum * opening
        totals[pl.ds(slabs + slab, 1)] = run_state * opening
        return nothing

    lax.fori_loop(0, slabs, run_slab, 0)
    share_totals(blocks, device, -1, totals, inbox, send_sems, recv_sems)
    arriving[...] = folded(blocks, shards, blocks - 1 - here, -1, inbox)

    def run_head(head, nothing):
        at = pl.ds(pl.multiple_of(head * HS, HS), HS)
        for slab in range(SLABS):
            slot = head * SLABS + slab
            lanes = slice(slab * LANES, (slab + 1) * LANES)
            entering = seg[slot, 0:SEGS] + seg[slot, SEGS : 2 * SEGS] * arriving[pl.ds(slot, 1)]
            for part in range(SEGS):
                lines = slice(part * span, (part + 1) * span)
                ext[lines, lanes] = (
                    local_all[slot, lines] + reach_all[slot, lines] * entering[part : part + 1]
                )
            prior[7:8, lanes] = carry[pl.ds(slot, 1)]
            prior[8 : 8 + rows, lanes] = hidden[slot]
        carried = ext[0:rows]
        before = prior[7 : 7 + rows]
        low = conv[:, at]
        value = low.astype(FLOAT)
        place = offset[...]
        first = (place == 0).astype(FLOAT)
        keep = 1.0 - first
        softness = soft[:, at]
        weights = (gate_w[0, head], gate_w[1, head])
        rate, inward, raw, gap = gate_values(low, weights, gate_b[:, at], softness)
        root = jnp.sqrt(gap)
        scale = keep * root + first
        pushed = carried * inward
        log_grad = keep * raw * (carried * before - pushed * value * (raw / root))
        rate_grad = ((-8.0 * softness) * log_grad * rate * (1.0 - rate)).astype(BRAIN)
        scaled = carried * scale
        input_grad = (scaled * value * inward * (1.0 - inward)).astype(BRAIN)
        conv_grad = scaled * inward + nt(rate_grad, weights[0]) + nt(input_grad, weights[1])
        ext[rows : rows + 8] = jnp.zeros((8, HS), FLOAT)
        total = conv_w[0:1, at] * conv_grad
        head_sum = jnp.zeros((8, HS), FLOAT)
        lines = lax.broadcasted_iota(jnp.int32, (8, 1), 0)
        for step in range(1, CONV):
            term = conv_w[step : step + 1, at] * conv_grad * (place >= step).astype(FLOAT)
            ext[0:rows] = term
            total = total + ext[step : step + rows]
            moved = pltpu.roll(term[0:8], 8 - step, 0)
            head_sum = head_sum + jnp.where(lines >= 8 - step, moved, 0.0)
        heads_out[:, at] = head_sum
        tails[:, at] = total[rows - 8 : rows]
        lead_grad[pl.ds(start, half), at] = total[0:half].astype(BRAIN)
        lead_grad[pl.ds(other, half), at] = total[half:rows].astype(BRAIN)
        return nothing

    lax.fori_loop(0, heads, run_head, 0)
    rim = pltpu.make_async_remote_copy(
        src_ref=heads_out,
        dst_ref=heads_in,
        send_sem=halo_sems.at[0],
        recv_sem=halo_sems.at[1],
        device_id=device(-1),
        device_id_type=MESH,
    )
    rim.start()
    rim.wait()
    followed = jnp.where(here < blocks - 1, 1.0, 0.0)
    for head in range(heads):
        at = slice(head * HS, (head + 1) * HS)
        there = (head - heads // shards) % heads
        whole = tails[:, at] + heads_in[:, there * HS : (there + 1) * HS] * followed
        kept = lead_grad[pl.ds(pl.multiple_of(other + half - 16, 16), 16), at]
        tails_pair = jnp.concatenate([kept[0:8], whole.astype(BRAIN)], axis=0)
        lead_grad[pl.ds(pl.multiple_of(other + half - 16, 16), 16), at] = tails_pair


def lasting(microseconds):
    return pl.CostEstimate(
        flops=int(microseconds * 1.1e9), bytes_accessed=int(microseconds * 3e6), transcendentals=0
    )


def block_call(kernel, ident, operands, outs, scratch, microseconds, anywhere=0):
    whole, open_place = pl.BlockSpec(memory_space=pltpu.VMEM), pl.BlockSpec(memory_space=pl.ANY)
    return pl.pallas_call(
        kernel,
        out_shape=[jax.ShapeDtypeStruct(*out) for out in outs],
        in_specs=[whole] * (len(operands) - anywhere) + [open_place] * anywhere,
        out_specs=[whole] * (len(outs) - anywhere) + [open_place] * anywhere,
        scratch_shapes=scratch,
        cost_estimate=lasting(microseconds),
        compiler_params=pltpu.CompilerParams(
            vmem_limit_bytes=VMEM_BYTES, collective_id=ident, has_side_effects=True
        ),
    )(*operands)


def message_scratch(width):
    others = lax.axis_size("row") * lax.axis_size("col") // 2 - 1
    slabs = width // LANES
    return [
        pltpu.VMEM((others, 2 * slabs, LANES), FLOAT),
        pltpu.SemaphoreType.DMA((2,)),
        pltpu.SemaphoreType.DMA((others,)),
        pltpu.SemaphoreType.DMA((others,)),
    ]


def recur_forward(lead, gate, offset, small):
    rows, width = lead.shape
    slabs = width // LANES
    stack = (slabs, rows, LANES)
    return block_call(
        forward_kernel,
        0,
        [lead, gate, offset, small["conv_weight"], small["conv_bias"], small["gate_weight"],
         small["gate_bias"], small["soft"]],
        [((rows, width), BRAIN), (stack, FLOAT), (stack, FLOAT), ((rows, width), BRAIN),
         ((slabs, LANES), FLOAT)],
        [
            pltpu.VMEM((rows + 8, HS), FLOAT),
            pltpu.VMEM((SLABS, rows, LANES), FLOAT),
            pltpu.VMEM(stack, FLOAT),
            pltpu.VMEM(stack, FLOAT),
            pltpu.VMEM((slabs, 2 * SEGS, LANES), FLOAT),
            pltpu.VMEM((2 * slabs, LANES), FLOAT),
            pltpu.VMEM((8, width), FLOAT),
        ]
        + message_scratch(width),
        27,
    )


def recur_backward(grad, kept, offset, small):
    rows, width = grad.shape
    slabs = width // LANES
    stack = (slabs, rows, LANES)
    return block_call(
        backward_kernel,
        1,
        [grad, kept["gate"], kept["hidden"], kept["decay"], kept["state_in"], kept["conv"], offset,
         small["conv_weight"], small["gate_weight"], small["gate_bias"], small["soft"]],
        [((rows, width), BRAIN), ((rows, width), BRAIN)],
        [
            pltpu.VMEM((rows + 8, HS), FLOAT),
            pltpu.VMEM((rows + 8, HS), FLOAT),
            pltpu.VMEM((rows, LANES), FLOAT),
            pltpu.VMEM((rows + 8, LANES), FLOAT),
            pltpu.VMEM(stack, FLOAT),
            pltpu.VMEM(stack, FLOAT),
            pltpu.VMEM((slabs, 2 * SEGS, LANES), FLOAT),
            pltpu.VMEM((2 * slabs, LANES), FLOAT),
            pltpu.VMEM((slabs, LANES), FLOAT),
            pltpu.VMEM((8, width), FLOAT),
            pltpu.VMEM((8, width), FLOAT),
            pltpu.VMEM((8, width), FLOAT),
        ]
        + message_scratch(width),
        30,
    )


def line_plan(pieces, unit):
    plan, line = [], 0
    for at, (rows, columns) in enumerate(pieces):
        for begin in range(0, columns, LANES):
            done = 0
            while done < rows:
                index, inner = divmod(line, unit)
                count = min(rows - done, unit - inner)
                plan.append(
                    (at, slice(done, done + count), slice(begin, begin + LANES), index,
                     slice(inner, inner + count))
                )
                done += count
                line += count
    return plan


def closing_sizes(shared, split, peers, cols, shards):
    shared_lines = sum(rows * columns for rows, columns in shared) // LANES
    split_lines = sum(rows * columns for rows, columns in split) // LANES // shards
    unit = -(-shared_lines // (peers * cols * 16)) * 16
    part = -(-split_lines // (peers * 16)) * 16
    return unit, part


def remote(source, target, sems, slot, device):
    return pltpu.make_async_remote_copy(
        src_ref=source,
        dst_ref=target,
        send_sem=sems.at[0, slot],
        recv_sem=sems.at[1, slot],
        device_id=device,
        device_id_type=MESH,
    )


def closing_kernel(count, layers, *refs):
    streams, refs = refs[:layers], refs[layers:]
    own_part, other_part, stream, d_middle, gain = refs[:5]
    shared, split = refs[5 : 5 + count], refs[5 + count : 5 + 2 * count]
    tokens_out, states_out, *refs = refs[5 + 2 * count :]
    shared_out, split_out = refs[:count], refs[count : 2 * count]
    (
        received, outgoing, homing, flat, beside_in, both, inbox, red, red_split, zbox, sbox, zfull,
        sfull, shared_all, split_all, pair_sems, beside_sems, row_sems, col_sems, turn_sems,
        spread_sems, shared_sems, split_sems, token_sems, leaving, state_sems,
    ) = refs[2 * count :]
    peers, cols = lax.axis_size("row"), lax.axis_size("col")
    shards = cols // 2
    row, col = lax.axis_index("row"), lax.axis_index("col")
    own, d_model = stream.shape
    piece = d_model // cols
    unit, part = zbox.shape[1], sbox.shape[1]
    shared_lines = cols * unit

    side, place, places = row % 2, row // 2, peers // 2
    beside = (row + 1 - 2 * side, col)

    def along(by):
        return (((place + by) % places) * 2 + side, col)

    barrier = pltpu.get_barrier_semaphore()
    greeted = [beside]
    greeted += [along(by) for by in range(1, places)]
    greeted += [(row, (col + by) % cols) for by in range(1, cols)]
    for to in greeted:
        pl.semaphore_signal(barrier, inc=1, device_id=to, device_id_type=MESH)

    sizes = [value.shape for value in shared]
    shared_plan = line_plan(sizes, unit)
    thin = [(value.shape[0], value.shape[1] // shards) for value in split]
    split_plan = line_plan(thin, part)
    flat[...] = jnp.zeros(flat.shape, BRAIN)
    for at, rows, lanes, index, lines in shared_plan:
        begin, owner = index % cols * unit, index // cols
        flat[owner % 2, owner // 2, begin + lines.start : begin + lines.stop] = shared[at][
            rows, lanes
        ].astype(BRAIN)
    for turn in range(shards):
        for at, rows, lanes, index, lines in split_plan:
            begin = shared_lines + turn * part
            skip = turn * thin[at][1]
            flat[index % 2, index // 2, begin + lines.start : begin + lines.stop] = split[at][
                rows, skip + lanes.start : skip + lanes.stop
            ].astype(BRAIN)
    pl.semaphore_wait(barrier, len(greeted))

    paired = remote(flat.at[1 - side], beside_in, beside_sems, 0, beside)
    paired.start()
    mine = pl.ds(pl.multiple_of(col * own, own), own)
    for layer in range(layers):
        for at in range(cols):
            leaving[layer, at] = streams[layer][:, at * piece : (at + 1) * piece].astype(BRAIN)
    states = []
    for by in range(1, cols):
        to = (col + by) % cols
        for layer in range(layers):
            slot = layer * (cols - 1) + by - 1
            there = states_out.at[layer, mine]
            copy = remote(leaving.at[layer, to], there, state_sems, slot, (row, to))
            states.append(copy)
    for layer in range(layers):
        states_out[layer, mine] = leaving[layer, col]
    pair = remote(other_part, received, pair_sems, 0, (row, col + 1 - 2 * (col % 2)))
    pair.start()
    for copy in states[0::layers]:
        copy.start()
    paired.wait()

    def add_pair(at, nothing):
        both[at] = (flat[side, at].astype(FLOAT) + beside_in[at].astype(FLOAT)).astype(BRAIN)
        return nothing

    lax.fori_loop(0, places, add_pair, 0)
    scattered = []
    for by in range(1, places):
        to = (place + by) % places
        copy = remote(both.at[to], inbox.at[by - 1], row_sems, by - 1, along(by))
        copy.start()
        scattered.append(copy)
    pair.wait()

    def norm_rows(at, nothing):
        lines = pl.ds(pl.multiple_of(at * 16, 16), 16)
        value = stream[lines]
        scale = lax.rsqrt(jnp.mean(value * value, axis=1, keepdims=True) + EPSILON)
        gained = (own_part[lines] + received[lines].astype(FLOAT)) * gain[...]
        total = jnp.mean(gained * value, axis=1, keepdims=True)
        result = d_middle[lines] + scale * gained - value * (scale * scale * scale * total)
        for to in range(cols):
            outgoing[to, lines] = result[:, to * piece : (to + 1) * piece].astype(BRAIN)
        return nothing

    lax.fori_loop(0, own // 16, norm_rows, 0)
    for copy in scattered:
        copy.wait()
    total = both[place].astype(FLOAT)
    for by in range(1, places):
        total = total + inbox[by - 1].astype(FLOAT)
    for at in range(cols):
        red[at] = total[at * unit : (at + 1) * unit].astype(BRAIN)
    for turn in range(shards):
        begin = shared_lines + turn * part
        red_split[turn] = total[begin : begin + part].astype(BRAIN)

    copies = []
    for by in range(1, cols):
        to = (col + by) % cols
        copies.append(remote(red.at[to], zbox.at[by - 1], col_sems, by - 1, (row, to)))
    for turn in range(1, shards):
        to = (col + 2 * turn) % cols
        copies.append(remote(red_split.at[turn], sbox.at[turn - 1], turn_sems, turn - 1, (row, to)))
    for copy in copies:
        copy.start()
    for copy in copies:
        copy.wait()
    total = red[col].astype(FLOAT)
    for by in range(1, cols):
        total = total + zbox[by - 1].astype(FLOAT)
    zfull[col] = total.astype(BRAIN)
    total = red_split[0].astype(FLOAT)
    for turn in range(1, shards):
        total = total + sbox[turn - 1].astype(FLOAT)
    sfull[...] = total.astype(BRAIN)

    spread = []
    for by in range(1, cols):
        to = (col + by) % cols
        copy = remote(zfull.at[col], zfull.at[col], spread_sems, by - 1, (row, to))
        copy.start()
        spread.append(copy)
    last = []
    for by in range(1, places):
        copy = remote(sfull, split_all.at[side, place], split_sems, by - 1, along(by))
        copy.start()
        last.append(copy)
    split_all[side, place] = sfull[...]
    for copy in spread:
        copy.wait()
    for by in range(1, places):
        copy = remote(zfull, shared_all.at[side, place], shared_sems, by - 1, along(by))
        copy.start()
        last.append(copy)
    shared_all[side, place] = zfull[...]
    returned = []
    for by in range(1, cols):
        to = (col + by) % cols
        copy = remote(outgoing.at[to], homing.at[col], token_sems, by - 1, (row, to))
        copy.start()
        returned.append(copy)
    for layer in range(1, layers):
        for copy in states[layer::layers]:
            copy.start()
    homing[col] = outgoing[col]
    for copy in last:
        copy.wait()
    lanes_over = [
        remote(split_all.at[side], split_all.at[side], beside_sems, 1, beside),
        remote(shared_all.at[side], shared_all.at[side], beside_sems, 2, beside),
    ]
    for copy in lanes_over:
        copy.start()
    for copy in lanes_over:
        copy.wait()
    for at, rows, lanes, index, lines in shared_plan:
        owner = index // cols
        shared_out[at][rows, lanes] = shared_all[
            owner % 2, owner // 2, index % cols, lines
        ].astype(FLOAT)
    for at, rows, lanes, index, lines in split_plan:
        split_out[at][rows, lanes] = split_all[index % 2, index // 2, lines].astype(FLOAT)
    for copy in returned + states:
        copy.wait()
    for at in range(cols):
        tokens_out[at * own : (at + 1) * own] = homing[at].astype(FLOAT)


def close(streams, own_part, other_part, stream, d_middle, gain, shared, split):
    peers, cols = lax.axis_size("row"), lax.axis_size("col")
    shards = cols // 2
    own, d_model = stream.shape
    pieces = [value.shape[1] // shards for value in split]

    def widened(value):
        cut = value.reshape(value.shape[0], shards, -1)
        short = -cut.shape[2] % LANES
        return jnp.pad(cut, ((0, 0), (0, 0), (0, short))).reshape(value.shape[0], -1)

    split = [widened(value) if piece % LANES else value for value, piece in zip(split, pieces)]
    shared_sizes = [value.shape for value in shared]
    split_sizes = [value.shape for value in split]
    places = peers // 2
    unit, part = closing_sizes(shared_sizes, split_sizes, peers, cols, shards)
    lines = cols * unit + shards * part
    sems = [
        pltpu.SemaphoreType.DMA((2, count))
        for count in (1, 3, places - 1, cols - 1, max(shards - 1, 1), cols - 1, places - 1,
                      places - 1, cols - 1)
    ]
    result = block_call(
        partial(closing_kernel, len(shared), len(streams)),
        2,
        [*streams, own_part, other_part, stream, d_middle, gain, *shared, *split],
        [((own * cols, d_model // cols), FLOAT)]
        + [((len(streams), own * cols, d_model // cols), BRAIN)]
        + [(size, FLOAT) for size in shared_sizes]
        + [((rows, columns // shards), FLOAT) for rows, columns in split_sizes],
        [
            pltpu.VMEM((own, d_model), BRAIN),
            pltpu.VMEM((cols, own, d_model // cols), BRAIN),
            pltpu.VMEM((cols, own, d_model // cols), BRAIN),
            pltpu.VMEM((2, places, lines, LANES), BRAIN),
            pltpu.VMEM((places, lines, LANES), BRAIN),
            pltpu.VMEM((places, lines, LANES), BRAIN),
            pltpu.VMEM((places - 1, lines, LANES), BRAIN),
            pltpu.VMEM((cols, unit, LANES), BRAIN),
            pltpu.VMEM((shards, part, LANES), BRAIN),
            pltpu.VMEM((cols - 1, unit, LANES), BRAIN),
            pltpu.VMEM((max(shards - 1, 1), part, LANES), BRAIN),
            pltpu.VMEM((cols, unit, LANES), BRAIN),
            pltpu.VMEM((part, LANES), BRAIN),
            pltpu.VMEM((2, places, cols, unit, LANES), BRAIN),
            pltpu.VMEM((2, places, part, LANES), BRAIN),
        ]
        + sems
        + [
            pltpu.VMEM((len(streams), cols, own, d_model // cols), BRAIN),
            pltpu.SemaphoreType.DMA((2, len(streams) * (cols - 1))),
        ],
        80,
    )
    count = len(shared)
    split = [value[:, :piece] for value, piece in zip(result[2 + count :], pieces)]
    return result[0], result[1], result[2 : 2 + count], split


PARTS = 3


def routes_of(pack_width, parts, source, target, begin=0):
    shards = lax.axis_size("col") // 2
    piece = pack_width // PARTS
    return [
        (source, part * piece, piece, target, ((part - begin) * shards + shard) * piece, shard)
        for part in parts
        for shard in range(shards)
    ]


def shipped(routes, sources, targets, sems):
    cols = lax.axis_size("col")
    row, col = lax.axis_index("row"), lax.axis_index("col")
    copies = []
    for slot, (source, begin, width, target, place, shard) in enumerate(routes):
        held = sources[source].at[:, pl.ds(begin, width)]
        there = targets[target].at[:, pl.ds(place, width)]
        if shard:
            to = (row, (col + cols - 2 * shard) % cols)
            copies.append(remote(held, there, sems, slot, to))
        else:
            copies.append(pltpu.make_async_copy(held, there, sems.at[0, slot]))
    return copies


def opening_kernel(
    routes, tokens, gains, vectors, pack,
    tokens_out, gains_out, vectors_out, packs_out,
    token_got, token_sems, gain_sems, vector_sems, pack_sems,
):
    cols = lax.axis_size("col")
    shards = cols // 2
    row, col = lax.axis_index("row"), lax.axis_index("col")
    own, piece = tokens_out.shape[0], tokens.shape[1]
    barrier = pltpu.get_barrier_semaphore()
    for by in range(1, cols):
        pl.semaphore_signal(barrier, inc=1, device_id=(row, (col + by) % cols), device_id_type=MESH)
    pl.semaphore_wait(barrier, cols - 1)
    copies = shipped(routes, [pack], [packs_out], pack_sems)
    for turn in range(1, shards):
        to = (row, (col + cols - 2 * turn) % cols)
        copies.append(remote(vectors, vectors_out.at[turn], vector_sems, turn - 1, to))
    for by in range(1, cols):
        to = (col + by) % cols
        there = pl.ds(pl.multiple_of(to * own, own), own)
        copies.append(remote(tokens.at[there], token_got.at[col], token_sems, by - 1, (row, to)))
        copies.append(remote(gains, gains_out.at[col], gain_sems, by - 1, (row, to)))
    for copy in copies:
        copy.start()
    token_got[col] = tokens[pl.ds(pl.multiple_of(col * own, own), own)]
    gains_out[col] = gains[...]
    vectors_out[0] = vectors[...]
    for copy in copies:
        copy.wait()
    for at in range(cols):
        tokens_out[:, at * piece : (at + 1) * piece] = token_got[at]


def open_up(ident, tokens, gains, vectors, pack):
    cols = lax.axis_size("col")
    shards = cols // 2
    rows, piece = tokens.shape
    own = rows // cols
    routes = routes_of(pack.shape[1], range(PARTS), 0, 0)
    outs = [
        ((own, piece * cols), BRAIN),
        ((cols,) + gains.shape, FLOAT),
        ((shards,) + vectors.shape, FLOAT),
        ((pack.shape[0], pack.shape[1] * shards), BRAIN),
    ]
    sizes = (cols - 1, cols - 1, max(shards - 1, 1), len(routes))
    scratch = [pltpu.VMEM((cols, own, piece), BRAIN)]
    scratch += [pltpu.SemaphoreType.DMA((2, size)) for size in sizes]
    return block_call(
        partial(opening_kernel, routes), ident, [tokens, gains, vectors, pack], outs, scratch, 30,
        anywhere=1,
    )


def settling_kernel(count, routes, *refs):
    normed, small, pack, refs = refs[0], refs[1 : 1 + count], refs[1 + count], refs[2 + count :]
    full_out, small_out, packs_out, refs = refs[0], refs[1 : 1 + count], refs[1 + count], refs[2 + count :]
    flat, got, others, pair_sems, across_sems, spread_sems, pack_sems = refs
    peers, cols = lax.axis_size("row"), lax.axis_size("col")
    shards = cols // 2
    row, col = lax.axis_index("row"), lax.axis_index("col")
    own = normed.shape[0]
    plan = line_plan([value.shape for value in small], flat.shape[1])
    peer = (row, col + 1 - 2 * (col % 2))
    signals = [peer] + [(row, (col + 2 * turn) % cols) for turn in range(1, shards)]
    signals += [((row + by) % peers, col) for by in range(1, peers)]
    barrier = pltpu.get_barrier_semaphore()
    for to in signals:
        pl.semaphore_signal(barrier, inc=1, device_id=to, device_id_type=MESH)
    flat[...] = jnp.zeros(flat.shape, BRAIN)
    for at, rows, lanes, index, lines in plan:
        flat[index, lines] = small[at][rows, lanes]
    pl.semaphore_wait(barrier, len(signals))

    across = []
    for turn in range(1, shards):
        to = (row, (col + cols - 2 * turn) % cols)
        across.append(remote(flat.at[row], got.at[turn - 1], across_sems, turn - 1, to))
    pair = remote(normed, full_out.at[pl.ds(own, own)], pair_sems, 0, peer)
    copies = [pair] + shipped(routes, [pack], [packs_out], pack_sems)
    for copy in across + copies:
        copy.start()
    full_out[0:own] = normed[...]
    for at in range(count):
        small_out[at][0] = small[at][...]
    spread = []
    for turn in range(1, shards):
        across[turn - 1].wait()
        for by in range(1, peers):
            to = ((row + by) % peers, col)
            slot = (turn - 1) * (peers - 1) + by - 1
            copy = remote(got.at[turn - 1], others.at[turn - 1, row], spread_sems, slot, to)
            copy.start()
            spread.append(copy)
        others[turn - 1, row] = got[turn - 1]
    for copy in spread:
        copy.wait()
    for turn in range(1, shards):
        for at, rows, lanes, index, lines in plan:
            small_out[at][turn, rows, lanes] = others[turn - 1, index, lines]
    for copy in copies:
        copy.wait()


def settle(ident, normed, small, pack):
    peers, shards = lax.axis_size("row"), lax.axis_size("col") // 2
    rest = max(shards - 1, 1)
    kept = [value.shape[1] for value in small]
    small = [
        jnp.pad(value, ((0, 0), (0, -value.shape[1] % LANES))) if value.shape[1] % LANES else value
        for value in small
    ]
    lines = sum(value.shape[0] * value.shape[1] for value in small) // LANES
    unit = -(-lines // (peers * 16)) * 16
    own, d_model = normed.shape
    routes = routes_of(pack.shape[1], range(PARTS), 0, 0)
    outs = [((2 * own, d_model), BRAIN)]
    outs += [((shards,) + value.shape, BRAIN) for value in small]
    outs += [((pack.shape[0], pack.shape[1] * shards), BRAIN)]
    scratch = [
        pltpu.VMEM((peers, unit, LANES), BRAIN),
        pltpu.VMEM((rest, unit, LANES), BRAIN),
        pltpu.VMEM((rest, peers, unit, LANES), BRAIN),
    ]
    sizes = (1, rest, rest * (peers - 1), len(routes))
    scratch += [pltpu.SemaphoreType.DMA((2, size)) for size in sizes]
    full, *values, packs = block_call(
        partial(settling_kernel, len(small), routes), ident, [normed, *small, pack], outs, scratch,
        40, anywhere=1,
    )
    return full, [value[:, :, :size] for value, size in zip(values, kept)], packs


TILE = 256
LINES = 64


def turn_kernel(backward, lefts, offset, plan, sources, counts, routes, *refs):
    xs, refs = refs[:lefts], refs[lefts:]
    (wide, x2, w2, stream, gain, d_stream, factor, mask), refs = refs[:8], refs[8:]
    extra, refs = refs[:sources], refs[sources:]
    cargo, refs = refs[: counts[0]], refs[counts[0] :]
    (new_out, full_out, low_out), refs = refs[:3], refs[3:]
    grad_outs, refs = refs[: len(plan)], refs[len(plan) :]
    cargo_outs, refs = refs[: counts[1]], refs[counts[1] :]
    weights, sending, received, mine, weight_sems, share_sems, spread_sems, cargo_sems = refs
    cols = lax.axis_size("col")
    shards = cols // 2
    own = stream.shape[0]
    depths = [x.shape[1] for x in xs]
    depth = sum(depths)
    tiles = sending.shape[0]
    row, col = lax.axis_index("row"), lax.axis_index("col")
    peer = (row, col + 1 - 2 * (col % 2))

    barrier = pltpu.get_barrier_semaphore()
    greeted = [peer]
    if any(route[-1] for route in routes):
        greeted += [(row, (col + 2 * other) % cols) for other in range(1, shards)]
    for to in greeted:
        pl.semaphore_signal(barrier, inc=1, device_id=to, device_id_type=MESH)

    def weight_copy(tile):
        lines = pl.ds(pl.multiple_of(tile * TILE, TILE), TILE)
        return pltpu.make_async_copy(
            wide.at[lines, pl.ds(offset, depth)], weights.at[tile], weight_sems.at[tile]
        )

    def share_copy(tile):
        return remote(sending.at[tile], received.at[tile], share_sems, tile, peer)

    def spread_copy(at):
        lines = pl.multiple_of(at * LINES, LINES)
        return pltpu.make_async_remote_copy(
            src_ref=full_out.at[pl.ds(lines, LINES)],
            dst_ref=full_out.at[pl.ds(pl.multiple_of(own + lines, LINES), LINES)],
            send_sem=spread_sems.at[0, at],
            recv_sem=spread_sems.at[1, at],
            device_id=peer,
            device_id_type=MESH,
        )

    def begin(tile, nothing):
        weight_copy(tile).start()
        return nothing

    lax.fori_loop(0, tiles, begin, 0)
    pl.semaphore_wait(barrier, len(greeted))
    carried = shipped(routes, cargo, cargo_outs, cargo_sems)
    for copy in carried:
        copy.start()

    def project(tile, nothing):
        weight_copy(tile).wait()
        at = pl.ds(pl.multiple_of(tile * TILE, TILE), TILE)
        total = nn(x2[...], w2[:, at])
        begin = 0
        for x, size in zip(xs, depths):
            total = total + nt(x[...], weights[tile, :, begin : begin + size])
            begin += size
        sending[tile] = total[own:].astype(BRAIN)
        mine[tile] = total[:own]
        share_copy(tile).start()
        return nothing

    lax.fori_loop(0, tiles, project, 0)

    def gradients(part):
        for (left, right), out in part:
            out[...] = tn(extra[left][...], (*extra, *xs)[right][...])

    pairs = list(zip(plan, grad_outs))
    gradients(pairs[: len(pairs) // 2])

    def arrive(tile, nothing):
        share_copy(tile).wait()
        return nothing

    lax.fori_loop(0, tiles, arrive, 0)

    def finish(at, nothing):
        lines = pl.ds(pl.multiple_of(at * LINES, LINES), LINES)
        total = jnp.concatenate(
            [mine[tile, lines] + received[tile, lines].astype(FLOAT) for tile in range(tiles)],
            axis=1,
        )
        value = stream[lines]
        if backward:
            scale = lax.rsqrt(jnp.mean(value * value, axis=1, keepdims=True) + EPSILON)
            gained = total * gain[...]
            shift = jnp.mean(gained * value, axis=1, keepdims=True)
            result = d_stream[lines] + scale * gained - value * (scale * scale * scale * shift)
            new_out[lines] = result
            full_out[lines] = result.astype(BRAIN)
        else:
            result = value + total
            scale = lax.rsqrt(jnp.mean(result * result, axis=1, keepdims=True) + EPSILON)
            new_out[lines] = result
            full_out[lines] = (result * scale * gain[...]).astype(BRAIN)
        spread_copy(at).start()
        return nothing

    lax.fori_loop(0, own // LINES, finish, 0)
    gradients(pairs[len(pairs) // 2 :])

    def lower(lines):
        low_out[lines] = (nt(full_out[lines], factor[...]) * mask[lines]).astype(BRAIN)

    lower(slice(0, own))

    def leave(at, nothing):
        spread_copy(at).wait()
        return nothing

    lax.fori_loop(0, own // LINES, leave, 0)
    lower(slice(own, 2 * own))
    for copy in carried:
        copy.wait()


def turn(
    ident, xs, wide, offset, x2, w2, stream, gain, factor, mask, d_stream=None, extra=(), plan=(),
    cargo=(), widths=(), routes=(),
):
    own, d_model = stream.shape
    depth = sum(x.shape[1] for x in xs)
    tiles = d_model // TILE
    whole = pl.BlockSpec(memory_space=pltpu.VMEM)
    backward = d_stream is not None
    operands = [*xs, wide, x2, w2, stream, gain, d_stream if backward else gain, factor, mask]
    operands += extra
    specs = [whole] * len(operands)
    anywhere = pl.BlockSpec(memory_space=pl.ANY)
    specs[len(xs)] = anywhere
    operands += cargo
    specs += [anywhere] * len(cargo)
    plan = tuple(plan)
    sizes = []
    for left, right in plan:
        sizes.append((extra[left].shape[1], [*extra, *xs][right].shape[1]))
    return pl.pallas_call(
        partial(turn_kernel, backward, len(xs), offset, plan, len(extra), (len(cargo), len(widths)), tuple(routes)),
        out_shape=[
            jax.ShapeDtypeStruct((own, d_model), FLOAT),
            jax.ShapeDtypeStruct((2 * own, d_model), BRAIN),
            jax.ShapeDtypeStruct((2 * own, factor.shape[0]), BRAIN),
        ]
        + [jax.ShapeDtypeStruct(size, FLOAT) for size in sizes]
        + [jax.ShapeDtypeStruct((cargo[0].shape[0], size), cargo[0].dtype) for size in widths],
        in_specs=specs,
        out_specs=[whole] * (3 + len(plan)) + [anywhere] * len(widths),
        scratch_shapes=[
            pltpu.VMEM((tiles, TILE, depth), BRAIN),
            pltpu.VMEM((tiles, own, TILE), BRAIN),
            pltpu.VMEM((tiles, own, TILE), BRAIN),
            pltpu.VMEM((tiles, own, TILE), FLOAT),
            pltpu.SemaphoreType.DMA((tiles,)),
            pltpu.SemaphoreType.DMA((2, tiles)),
            pltpu.SemaphoreType.DMA((2, own // LINES)),
            pltpu.SemaphoreType.DMA((2, max(len(routes), 1))),
        ],
        cost_estimate=lasting(40),
        compiler_params=pltpu.CompilerParams(
            vmem_limit_bytes=VMEM_BYTES, collective_id=ident, has_side_effects=True
        ),
    )(*operands)


def partner(value):
    peers = lax.axis_size("col")
    return lax.ppermute(value, "col", [(at, at ^ 1) for at in range(peers)])


def from_shard(value, turn):
    peers = lax.axis_size("col")
    return lax.ppermute(value, "col", [((at + 2 * turn) % peers, at) for at in range(peers)])


def to_shard(value, turn):
    peers = lax.axis_size("col")
    return lax.ppermute(value, "col", [(at, (at + 2 * turn) % peers) for at in range(peers)])


def all_shards(value):
    return [value] + [from_shard(value, turn) for turn in range(1, lax.axis_size("col") // 2)]


def after(value, anchor):
    return lax.optimization_barrier((value, anchor))[0] if jax.tree.leaves(anchor) else value


def to_sequence(value):
    return lax.all_to_all(value, "col", split_axis=0, concat_axis=1, tiled=True)


def half_share(own, other):
    return own + partner(other.astype(BRAIN)).astype(FLOAT)


def norm_forward(stream, gain):
    scale = lax.rsqrt(jnp.mean(stream * stream, axis=1, keepdims=True) + EPSILON)
    return scale, (stream * scale * gain[None, :]).astype(BRAIN)


def masked(value, pick):
    return (value * pick).astype(BRAIN)


def recur_branch(normed_full, low, wide, small, ctx):
    ranks = ctx["pick"].shape[1]
    width = wide.shape[1] // 3
    inner = [low[:, b * ranks : (b + 1) * ranks] for b in range(2)]
    branch = nn(normed_full, wide[:, : 2 * width])
    lead = branch[:, :width] + nn(inner[0], small["inlet_upper"][0])
    gate = branch[:, width:] + nn(inner[1], small["inlet_upper"][1])
    return lead, gate, inner


def recur_part(
    ident, stream, lead, gate, wide, small, gain, factor, ctx, ready, cargo, widths, routes
):
    pick, offset = ctx["pick"], ctx["offset"]
    width = lead.shape[1]
    conv, decay, hidden, mixed, state_in = recur_forward(lead, gate, offset, small)
    mixed = after(mixed, ready)
    lowrank = masked(nt(mixed, small["outlet_lower"]), pick)
    middle, normed_two_full, low_two, *parts = turn(
        ident, [mixed], wide, 2 * width, lowrank, small["outlet_upper"], stream, gain, factor,
        ctx["picks"], cargo=cargo, widths=widths, routes=routes,
    )
    kept = dict(
        conv=conv, decay=decay, hidden=hidden, state_in=state_in, mixed=mixed, lowrank=lowrank,
        middle=middle, normed_two_full=normed_two_full,
    )
    return middle, normed_two_full, low_two, kept, parts


def hidden_part(normed_two_full, low_two, wide, small, ctx):
    pick = ctx["pick"]
    ranks = pick.shape[1]
    spread = wide.shape[1] // 3
    inner_two = [low_two[:, b * ranks : (b + 1) * ranks] for b in range(2)]
    branch_two = nn(normed_two_full, wide[:, : 2 * spread])
    up_gate = branch_two[:, :spread] + nn(inner_two[0], small["expand_upper"][0])
    up_value = branch_two[:, spread:] + nn(inner_two[1], small["expand_upper"][1])
    value, slope = gelu_pair(up_gate)
    product = (value * up_value).astype(BRAIN)
    factors = [(slope * up_value).astype(BRAIN), value.astype(BRAIN)]
    lowrank_two = masked(nt(product, small["shrink_lower"]), pick)
    return dict(
        inner_two=inner_two, factors=factors, product=product, lowrank_two=lowrank_two,
    )


def layer_backward(
    ident, d_stream, d_out, d_low_two, wide, small, upper_before, gains, kept, ctx, pending
):
    recur_wide, hidden_wide = wide
    pick, offset = ctx["pick"], ctx["offset"]
    own = d_stream.shape[0]
    rows = 2 * own
    width = recur_wide.shape[1] // 3
    spread = hidden_wide.shape[1] // 3

    d_product = nn(d_out, hidden_wide[:, 2 * spread :]) + nn(d_low_two, small["shrink_lower"])
    d_branch_two = [(part.astype(FLOAT) * d_product).astype(BRAIN) for part in kept["factors"]]
    d_inner_two = jnp.concatenate(
        [masked(nt(d_branch_two[b], small["expand_upper"][b]), pick) for b in range(2)], axis=1
    )
    d_middle, d_mid, d_low, shrink_upper, shrink_lower, expand_lower, expand_a, expand_b = turn(
        ident, d_branch_two, hidden_wide, 0, d_inner_two, small["expand_lower"], kept["middle"],
        gains[1:2], small["outlet_upper"], pick, d_stream,
        [kept["lowrank_two"], d_out, d_low_two, kept["product"], d_inner_two,
         kept["normed_two_full"], *kept["inner_two"]],
        [(0, 1), (2, 3), (4, 5), (6, 8), (7, 9)],
    )
    expand_upper = jnp.concatenate([expand_a, expand_b], axis=0)

    if pending is not None:
        d_mid, ctx["last"] = lax.optimization_barrier((d_mid, pending))
    d_mixed = nn(d_mid, recur_wide[:, 2 * width :]) + nn(d_low, small["outlet_lower"])
    d_branch = recur_backward(d_mixed, kept, offset, small)
    d_inner = jnp.concatenate(
        [masked(nt(d_branch[b], small["inlet_upper"][b]), pick) for b in range(2)], axis=1
    )
    if upper_before is None:
        outlet_upper = tn(kept["lowrank"], d_mid)
        outlet_lower = tn(d_low, kept["mixed"])
        inlet_lower = tn(d_inner, kept["normed_full"])
        inlet_a, inlet_b = (tn(kept["inner"][b], d_branch[b]) for b in range(2))
        result = tuple(
            nt(d_branch[0][part], recur_wide[:, :width])
            + nt(d_branch[1][part], recur_wide[:, width : 2 * width])
            + nn(d_inner[part], small["inlet_lower"])
            for part in (slice(0, own), slice(own, rows))
        )
    else:
        *result, outlet_upper, outlet_lower, inlet_lower, inlet_a, inlet_b = turn(
            ident + 1, d_branch, recur_wide, 0, d_inner, small["inlet_lower"], kept["stream"],
            gains[0:1], upper_before, pick, d_middle,
            [kept["lowrank"], d_mid, d_low, kept["mixed"], d_inner, kept["normed_full"],
             *kept["inner"]],
            [(0, 1), (2, 3), (4, 5), (6, 8), (7, 9)],
        )
    inlet_upper = jnp.concatenate([inlet_a, inlet_b], axis=0)
    shared = (inlet_lower, outlet_upper, expand_lower, shrink_upper)
    split = (inlet_upper, outlet_lower, expand_upper, shrink_lower)
    return d_middle, result, shared, split


def local(
    tokens, cotangent, adapter_ids, doc_lengths, norm_gain, inlet_weight, inlet_lower, inlet_upper,
    conv_weight, conv_bias, gate_weight, gate_bias, decay_param, outlet_weight, outlet_lower,
    outlet_upper, expand_weight, expand_lower, expand_upper, shrink_weight, shrink_lower,
    shrink_upper,
):
    row_at, col_at = lax.axis_index("row"), lax.axis_index("col")
    cols = lax.axis_size("col")
    shards = cols // 2
    rows = tokens.shape[0]
    own = rows // cols
    block = 2 * own
    docs = adapter_ids.shape[0]
    adapters, rank = inlet_lower.shape[3:]
    part_width, part_spread = inlet_weight.shape[3], expand_weight.shape[3]
    d_model = inlet_lower.shape[1]

    parity = (col_at % 2).astype(jnp.int32)
    ends = jnp.cumsum(doc_lengths)
    starts = ends - doc_lengths
    ordered = row_at * rows + (col_at // 2) * block + jnp.arange(block, dtype=jnp.int32)
    inside = (ordered[:, None] >= starts[None, :]) & (ordered[:, None] < ends[None, :])
    offset = (ordered - jnp.sum(jnp.where(inside, starts[None, :], 0), axis=1))[:, None]
    halves = (parity * own, own - parity * own)
    at_home = jnp.concatenate(
        [ordered[0] + begin + jnp.arange(own, dtype=jnp.int32) for begin in halves]
    )
    within = (at_home[:, None] >= starts[None, :]) & (at_home[:, None] < ends[None, :])
    pick = jnp.repeat(within.astype(FLOAT), rank, axis=1)
    picks = jnp.concatenate([pick, pick], axis=1)
    ctx = dict(pick=pick, picks=picks, offset=offset, pending={})


    def by_doc(factor, axis):
        return jnp.concatenate(
            [lax.dynamic_slice_in_dim(factor, adapter_ids[at], 1, axis) for at in range(docs)], axis
        )

    def lower_t(factor):
        return by_doc(jnp.moveaxis(factor, 1, -1), factor.ndim - 3)

    def upper_t(factor):
        return by_doc(factor, factor.ndim - 3)

    ranks = docs * rank
    lows = dict(
        inlet_lower=lower_t(inlet_lower).reshape(LAYERS, 2 * ranks, d_model),
        outlet_upper=upper_t(outlet_upper).reshape(LAYERS, ranks, d_model),
        expand_lower=lower_t(expand_lower).reshape(LAYERS, 2 * ranks, d_model),
        shrink_upper=upper_t(shrink_upper).reshape(LAYERS, ranks, d_model),
    )
    narrow_own = jnp.concatenate(
        [
            upper_t(inlet_upper).reshape(LAYERS, 2 * ranks, part_width),
            lower_t(outlet_lower).reshape(LAYERS, ranks, part_width),
        ],
        axis=1,
    )
    broad_own = jnp.concatenate(
        [
            upper_t(expand_upper).reshape(LAYERS, 2 * ranks, part_spread),
            lower_t(shrink_lower).reshape(LAYERS, ranks, part_spread),
        ],
        axis=1,
    )
    vectors_own = jnp.concatenate(
        [conv_weight, gate_bias, conv_bias[:, None], decay_param[:, None]], axis=1
    )

    def rows_of(value):
        return value.reshape(-1, value.shape[-1])

    def packed(pair, single):
        pack = jnp.concatenate([pair[:, 0], pair[:, 1], single], axis=1)
        short = -single.shape[1] % LANES
        if short:
            pack = jnp.pad(pack.reshape(pack.shape[0], PARTS, -1), ((0, 0), (0, 0), (0, short)))
            pack = pack.reshape(pack.shape[0], -1)
        return pack

    def gathered(packs, piece):
        whole = lax.all_gather(packs, "row", axis=0, tiled=True)
        if piece % LANES:
            whole = whole.reshape(whole.shape[0], PARTS * shards, -1)[:, :, :piece]
            whole = whole.reshape(whole.shape[0], -1)
        return whole

    def recur_small(layer, narrow, gates):
        return dict(
            inlet_lower=lows["inlet_lower"][layer],
            inlet_upper=narrow[: 2 * ranks].reshape(2, ranks, -1),
            outlet_lower=narrow[2 * ranks :],
            outlet_upper=lows["outlet_upper"][layer],
            conv_weight=vectors_all[layer, :CONV],
            gate_bias=vectors_all[layer, CONV : CONV + 2],
            conv_bias=vectors_all[layer, CONV + 2 : CONV + 3],
            soft=jax.nn.softplus(vectors_all[layer, CONV + 3 : CONV + 4]),
            gate_weight=gates,
        )

    def hidden_small(layer, broad):
        return dict(
            expand_lower=lows["expand_lower"][layer],
            expand_upper=broad[: 2 * ranks].reshape(2, ranks, -1),
            shrink_lower=broad[2 * ranks :],
            shrink_upper=lows["shrink_upper"][layer],
        )

    saved, wides, smalls = [], [], []
    recur_packs = [packed(inlet_weight[at], outlet_weight[at]) for at in range(LAYERS)]
    hidden_packs = [packed(expand_weight[at], shrink_weight[at]) for at in range(LAYERS)]
    def side_by_side(value):
        return jnp.concatenate([value[at] for at in range(shards)], axis=1)

    def heads_in_turn(value):
        return jnp.concatenate(
            [value[at].reshape((2, -1) + gate_weight.shape[3:]) for at in range(shards)], axis=1
        )

    stream, gains, vectors_all, recur_side = open_up(
        20, tokens, rows_of(norm_gain), rows_of(vectors_own), recur_packs[0]
    )
    gains = jnp.moveaxis(gains, 0, 1).reshape(LAYERS, 2, d_model)
    vectors_all = side_by_side(vectors_all).reshape(LAYERS, -1, shards * part_width)
    wide_one = gathered(recur_side, part_width)
    stream = stream.astype(FLOAT)
    _, normed = norm_forward(stream, gains[0][0])
    small = []
    for layer in range(LAYERS):
        small += [narrow_own[layer], rows_of(gate_weight[layer]), broad_own[layer]]
    normed_full, small, hidden_side = settle(21, normed, small, hidden_packs[0])
    bits = [
        (side_by_side(narrow), heads_in_turn(gates), side_by_side(broad))
        for narrow, gates, broad in zip(small[0::3], small[1::3], small[2::3])
    ]
    wide_two = gathered(hidden_side, part_spread)
    low = masked(nt(normed_full, lows["inlet_lower"][0]), picks)
    for layer in range(LAYERS):
        more_layers = layer + 1 < LAYERS
        kept = dict(stream=stream, normed_full=normed_full)
        narrow, gates, broad = bits[layer]
        small_one = recur_small(layer, narrow, gates)
        lead, gate, inner = recur_branch(normed_full, low, wide_one, small_one, ctx)
        ready, cargo, widths, routes = [], [], [], []
        if more_layers:
            packs = all_shards(after(recur_packs[layer + 1], normed_full))
            lead, packs[1:] = lax.optimization_barrier((lead, packs[1:]))
            cargo = [*packs, hidden_packs[layer + 1]]
            piece, spread_piece = (value.shape[1] // PARTS for value in cargo[-2:])
            widths = [PARTS * shards * piece, shards * spread_piece]
            routes = [
                (at, part * piece, piece, 0, (part * shards + at) * piece, 0)
                for part in range(PARTS)
                for at in range(shards)
            ] + routes_of(PARTS * spread_piece, [0], shards, 1)
        elif layer:
            ending = to_sequence(after(cotangent, lead))
            ready = [ending]
        middle, normed_two_full, low_two, more, sides = recur_part(
            3 + 2 * layer, stream, lead, gate, wide_one, small_one, gains[layer][1:2],
            lows["expand_lower"][layer], ctx, ready, cargo, widths, routes,
        )
        kept.update(inner=inner, gate=gate, **more)
        if more_layers:
            wide_next = gathered(sides[0], part_width)
            others = all_shards(after(hidden_packs[layer + 1][:, spread_piece:], middle))[1:]
        small_two = hidden_small(layer, broad)
        more = hidden_part(normed_two_full, low_two, wide_two, small_two, ctx)
        kept.update(more)
        wides.append((wide_one, wide_two))
        smalls.append({**small_one, **small_two})
        saved.append(kept)
        product, lowrank, upper = more["product"], more["lowrank_two"], small_two["shrink_upper"]
        spread = product.shape[1]
        if more_layers:
            product, others, kept["factors"] = lax.optimization_barrier(
                (product, others, more["factors"])
            )
            cargo = [hidden_packs[layer + 1], *others, sides[1]]
            routes = [
                (at, (part - (at > 0)) * spread_piece, spread_piece, 0,
                 (part * shards + at) * spread_piece, 0)
                for part in range(1, PARTS)
                for at in range(shards)
            ] + [(shards, 0, shards * spread_piece, 0, 0, 0)]
            stream, normed_full, low, hidden_side = turn(
                4 + 2 * layer, [product], wide_two, 2 * spread, lowrank, upper, middle,
                gains[layer + 1][0:1], lows["inlet_lower"][layer + 1], ctx["picks"], cargo=cargo, widths=[PARTS * shards * spread_piece],
                routes=routes,
            )
            wide_two_next = gathered(hidden_side, part_spread)
            wide_one, wide_two = wide_next, wide_two_next
        else:
            shrink = wide_two[:, 2 * spread :]
            parts = [
                nt(product[part], shrink) + nn(lowrank[part], upper)
                for part in (slice(0, own), slice(own, 2 * own))
            ]
            stream = middle + half_share(*parts)
            last_stream = stream
    ctx["pending"] = {LAYERS - 1: last_stream}
    d_out = jnp.concatenate(
        [ending, after(partner(after(ending, normed_two_full)), product)], axis=0
    )
    d_stream = ending.astype(FLOAT)
    d_low_two = masked(nt(d_out, smalls[-1]["shrink_upper"]), pick)
    shared_parts, split_parts = [], []
    for layer in reversed(range(LAYERS)):
        kept = saved[layer]
        d_middle, result, shared_more, split_more = layer_backward(
            3 + 2 * LAYERS + 2 * layer, d_stream, d_out, d_low_two, wides[layer], smalls[layer],
            lows["shrink_upper"][layer - 1] if layer else None, gains[layer], kept, ctx,
            ctx["pending"].get(layer),
        )
        shared_parts = [*shared_more, *shared_parts]
        split_parts = [*split_more, *split_parts]
        if layer:
            d_stream, d_out, d_low_two = result
    tokens_grad, states, shared_parts, split_parts = close(
        [*(kept["stream"] for kept in saved[1:]), ctx["last"]], result[0], result[1].astype(BRAIN), kept["stream"], d_middle, gains[0][:1], shared_parts,
        split_parts,
    )
    inlet_low, outlet_up, expand_low, shrink_up = (
        jnp.stack(shared_parts[at::4]) for at in range(4)
    )
    inlet_up, outlet_low, expand_up, shrink_low = (jnp.stack(split_parts[at::4]) for at in range(4))
    spread_out = (adapter_ids[None, :] == jnp.arange(adapters, dtype=jnp.int32)[:, None])

    def by_adapter(grad, count):
        grad = grad.reshape(LAYERS, count, docs, rank, -1)
        total = 0.0
        for doc in range(docs):
            total = total + jnp.where(
                spread_out[None, None, :, doc, None, None], grad[:, :, doc][:, :, None], 0.0
            )
        return total

    def lower_out(grad, count):
        grad = by_adapter(grad, count)
        if count == 1:
            grad = grad[:, 0]
        return jnp.moveaxis(grad, -1, 1)

    return (
        states,
        tokens_grad,
        lower_out(inlet_low, 2),
        by_adapter(inlet_up, 2),
        lower_out(outlet_low, 1),
        by_adapter(outlet_up, 1)[:, 0],
        lower_out(expand_low, 2),
        by_adapter(expand_up, 2),
        lower_out(shrink_low, 1),
        by_adapter(shrink_up, 1)[:, 0],
    )


def solution(mesh):
    return jax.shard_map(
        local,
        mesh=mesh,
        in_specs=(
            P("row", "col"),
            P("row", "col"),
            P(),
            P(),
            P(None, None, "col"),
            P(None, "row", None, "col"),
            P(),
            P(None, None, None, None, "col"),
            P(None, None, "col"),
            P(None, "col"),
            P(None, None, "col", None, None),
            P(None, None, "col"),
            P(None, "col"),
            P(None, "row", "col"),
            P(None, "col", None, None),
            P(),
            P(None, "row", None, "col"),
            P(),
            P(None, None, None, None, "col"),
            P(None, "row", "col"),
            P(None, "col", None, None),
            P(),
        ),
        out_specs=(
            P(None, "row", "col"),
            P("row", "col"),
            P(),
            P(None, None, None, None, "col"),
            P(None, "col", None, None),
            P(),
            P(),
            P(None, None, None, None, "col"),
            P(None, "col", None, None),
            P(),
        ),
        check_vma=False,
    )
```
